32 devices in a mesh: cohort: 2 (over y), people: 4 (over z), markers: 4 (over x, core).
Axes of the slice: x: 2, y: 2, z: 4, core: 2. Of those that a mesh axis runs over, the one named last changes fastest.
Arguments:
- genotype: int32 [12288, 2048], P(('cohort', 'people'), 'markers'), parts along dimension 0, may hold values from 0 to 170, as said below
- allele_freq: float32 [16384], P(('cohort', 'markers')), parts along dimension 0, may hold values from 0.05 to 0.5
- person_weight: float32 [12288], P(('cohort', 'people')), parts along dimension 0, may hold values from 0.5 to 18, as said below
- basis: bfloat16 [64, 8192], P('cohort', 'markers'), parts along dimension 0, may hold values from -0.0625 to 0.0625
- residuals: bfloat16 [128, 6144], P('cohort', 'people'), parts along dimension 0, may hold values from -6 to 6
- block_markers: int32 [2048], P('markers'), may hold values from 0 to 8191, as said below
Outputs:
- components: float32 [64, 6144], P('cohort', 'people'), parts along dimension 0
- coefficients: float32 [64, 64], P('cohort'), parts along dimension 0
- basis_next: float32 [4, 64, 2048], P('markers', 'cohort', 'people'), parts along dimension 1
- scores: float32 [4, 128, 512], P('markers', 'cohort', 'people'), parts along dimension 1
The draws below stay inside these ranges and needn't reach their ends.
There are 2 independent parts, one for each index of `cohort`. The reference program is written for one: setup_inputs(seed, part) draws one part's arguments, and reference() takes and returns one part's arrays. A program takes and returns all parts, laid end to end along the dimension named above; an argument that names none is the same for every part. Nothing has to cross between parts.
Inputs may be any that keep to these rules, and one draw needn't show every extreme that they name: `genotype`: each word packs the dosages (0, 1 or 2) of four consecutive markers of one person, marker 4 w + j in bits 2 j and 2 j + 1. `block_markers`: the j-th run of 512 entries holds distinct increasing markers among j * 2048 to (j + 1) * 2048 - 1, always including both of these ends. `person_weight`: positive weights.
All inputs are finite; a program needn't handle non-finite values.
Results may differ from the reference program's by a relative error of at most 0.0054.
Values sent between devices are 32-bit elements; how exact they have to be, the bound alone decides.
No kernel may reach another device: no remote copies, remote signals or barrier semaphores. Data moves between devices by JAX's collectives and lax.ppermute only.
A program may use at most 128 MiB of HBM per device.

```python
import math
import jax
import jax.numpy as jnp
from jax import lax

K = 32
R = 64
P_DEV = 1536
M_DEV = 2048
MB_DEV = 512
PEOPLE = 6144
MARKERS = 8192
BLOCK = 2048
N_PEOPLE = 4
N_MARKERS = 4


def draw_genotype(key, part):
    number = jax.random.randint(key, (PEOPLE, MARKERS // 4), 0, 81)
    first = number % 3
    second = number // 3 % 3
    third = number // 9 % 3
    fourth = number // 27
    return (first + 4 * second + 16 * third + 64 * fourth).astype(jnp.int32)


def draw_person_weight(key, part):
    ramp = jnp.arange(PEOPLE, dtype=jnp.float32) / float(PEOPLE - 1)
    rough = jnp.exp(jax.random.uniform(key, (PEOPLE,), jnp.float32, -0.69, 0.69))
    values = jnp.exp(ramp * jnp.log(3.0)) * rough
    return values.astype(jnp.float32)


def draw_block_markers(key, part):
    shard_count = MARKERS // M_DEV
    keys = jax.random.split(key, shard_count)

    def one_shard(shard_key):
        inner = jax.random.permutation(shard_key, M_DEV - 2) + 1
        picked = jnp.sort(inner[:MB_DEV - 2])
        ends_low = jnp.zeros((1,), jnp.int32)
        ends_high = jnp.full((1,), M_DEV - 1, jnp.int32)
        return jnp.concatenate([ends_low, picked.astype(jnp.int32), ends_high])
    local = jax.vmap(one_shard)(keys)
    offsets = (jnp.arange(shard_count, dtype=jnp.int32) * M_DEV)[:, None]
    return (local + offsets).reshape(shard_count * MB_DEV).astype(jnp.int32)


def levels(rng, shape, cuts, smallest, largest):
    def one(axis_at, parts):
        draws = jax.random.uniform(jax.random.fold_in(jax.random.fold_in(rng, 6), axis_at), (parts,), jnp.float32, smallest / len(cuts), largest / len(cuts))
        return jnp.repeat(jnp.exp(draws), shape[axis_at] // parts).reshape((-1,) + (1,) * (len(shape) - axis_at - 1))

    gain = one(*cuts[0])
    for cut in cuts[1:]:
        gain = gain * one(*cut)
    return gain


def noise(key, dims, deviation, most, pieces=(), kind=jnp.bfloat16):
    drawn = deviation * jax.random.normal(key, dims, jnp.float32)
    if pieces:
        drawn = drawn * levels(key, dims, pieces, -0.22, 0.18)
    return jnp.clip(drawn, -most, most).astype(kind)


def setup_inputs(seed: int = 0, part: int = 0) -> dict:
    streams_of = jax.random.split(jax.random.key(seed), 7)
    part_keys = jax.random.split(jax.random.fold_in(streams_of[6], part), 7)
    genotype = draw_genotype(jax.random.fold_in(jax.random.fold_in(streams_of[6], part), 71), part)
    allele_freq = jnp.clip(0.05 + 0.45 * jax.random.uniform(part_keys[1], (MARKERS,), jnp.float32) ** levels(part_keys[1], (MARKERS,), ((0, 4),), -0.2, 0.2), 0.05, 0.5)
    person_weight = draw_person_weight(jax.random.fold_in(jax.random.fold_in(streams_of[6], part), 71), part)
    basis = noise(part_keys[3], (K, MARKERS), MARKERS ** -0.5, 0.0625, ((1, 4),))
    residuals = noise(part_keys[4], (R, PEOPLE), 1.0, 6.0, ((1, 4),))
    block_markers = draw_block_markers(jax.random.fold_in(streams_of[6], 71), part)
    return {"genotype": genotype, "allele_freq": allele_freq, "person_weight": person_weight, "basis": basis, "residuals": residuals, "block_markers": block_markers}


def decode(packed, freq, weight):
    shifts = 2 * jnp.arange(4, dtype=jnp.int32)
    dosage = jnp.bitwise_and(jnp.right_shift(packed[:, :, None], shifts[None, None, :]), 3)
    dosage = dosage.reshape(packed.shape[0], packed.shape[1] * 4).astype(jnp.float32)
    standard = (dosage - 2.0 * freq[None, :]) / jnp.sqrt(2.0 * freq * (1.0 - freq))[None, :]
    return (weight[:, None] * standard).astype(jnp.bfloat16)

def reference(genotype, allele_freq, person_weight, basis, residuals, block_markers):
    packed_blocks = genotype.reshape(N_PEOPLE, P_DEV, MARKERS // 4)
    weight_blocks = person_weight.reshape(N_PEOPLE, P_DEV)

    def sketch_block(inputs):
        weighted = decode(inputs[0], allele_freq, inputs[1])
        return jnp.dot(basis.astype(jnp.float32), weighted.T.astype(jnp.float32), preferred_element_type=jnp.float32)
    sketch_parts = lax.map(sketch_block, (packed_blocks, weight_blocks))
    sketch = jnp.transpose(sketch_parts, (1, 0, 2)).reshape(K, PEOPLE)
    gram_matrix = jnp.dot(sketch, sketch.T, precision=lax.Precision.HIGHEST)
    factor_low = jnp.linalg.cholesky(gram_matrix)
    ortho = jax.scipy.linalg.solve_triangular(factor_low, sketch, lower=True)
    resid_float = residuals.astype(jnp.float32)
    coefficients = jnp.dot(ortho, resid_float.T, precision=lax.Precision.HIGHEST)
    projected = (resid_float - jnp.dot(coefficients.T, ortho, precision=lax.Precision.HIGHEST)).astype(jnp.bfloat16)
    ortho_half = ortho.astype(jnp.bfloat16)
    ortho_blocks = jnp.transpose(ortho_half.reshape(K, N_PEOPLE, P_DEV), (1, 0, 2))
    proj_blocks = jnp.transpose(projected.reshape(R, N_PEOPLE, P_DEV), (1, 0, 2))

    def accumulate(carry, inputs):
        basis_acc, score_acc = carry
        weighted = decode(inputs[0], allele_freq, inputs[1])
        basis_acc = basis_acc + jnp.dot(inputs[2].astype(jnp.float32), weighted.astype(jnp.float32), preferred_element_type=jnp.float32)
        chosen = jnp.take(weighted, block_markers, axis=1)
        score_acc = score_acc + jnp.dot(inputs[3].astype(jnp.float32), chosen.astype(jnp.float32), preferred_element_type=jnp.float32)
        return ((basis_acc, score_acc), 0)
    start = (jnp.zeros((K, MARKERS), jnp.float32), jnp.zeros((R, BLOCK), jnp.float32))
    (basis_acc, score_acc), unused = lax.scan(accumulate, start, (packed_blocks, weight_blocks, ortho_blocks, proj_blocks))
    basis_next = jnp.transpose(basis_acc.reshape(K, N_MARKERS, M_DEV), (1, 0, 2))
    scores = jnp.transpose((score_acc / math.sqrt(PEOPLE)).reshape(R, N_MARKERS, MB_DEV), (1, 0, 2))
    components = math.sqrt(PEOPLE) * ortho
    return (components, coefficients, basis_next, scores)
```

```python
import functools
import math

import jax
import jax.numpy as jnp
from jax import lax
from jax.experimental import pallas as pl
from jax.experimental.pallas import tpu as pltpu
from jax.sharding import PartitionSpec as P

LANES = 128
PER_WORD = 4
GROUP = LANES * PER_WORD
VMEM_LIMIT = 40 * 1024 * 1024
HIGHEST = lax.Precision.HIGHEST


def from_partner(block, axis, apart):
    count = lax.axis_size(axis)
    route = [(low, low ^ apart) for low in range(count)]
    return lax.ppermute(block, axis, route)


def split2(value):
    high = value.astype(jnp.bfloat16)
    low = (value - high.astype(jnp.float32)).astype(jnp.bfloat16)
    return high, low


def split3(value):
    high, rest = value.astype(jnp.bfloat16), None
    rest = value - high.astype(jnp.float32)
    middle, low = split2(rest)
    return high, middle, low


def digits(words):
    out = []
    for j in range(PER_WORD):
        one = words if j == 0 else jnp.right_shift(words, 2 * j)
        one = one if j == PER_WORD - 1 else jnp.bitwise_and(one, 3)
        out.append(one.astype(jnp.float32).astype(jnp.bfloat16))
    return out


def natural_of_column(shape):
    column = lax.broadcasted_iota(jnp.int32, shape, len(shape) - 1)
    return PER_WORD * jnp.bitwise_and(column, LANES - 1) + jnp.right_shift(column, 7)


def to_digit_order():
    row = lax.broadcasted_iota(jnp.int32, (GROUP, GROUP), 0)
    column = natural_of_column((1, GROUP))
    return jnp.where(row == column, 1.0, 0.0).astype(jnp.bfloat16)


def to_natural_order():
    row = lax.broadcasted_iota(jnp.int32, (GROUP, GROUP), 0)
    natural = PER_WORD * jnp.bitwise_and(row, LANES - 1) + jnp.right_shift(row, 7)
    column = lax.broadcasted_iota(jnp.int32, (GROUP, GROUP), 1)
    return jnp.where(natural == column, 1.0, 0.0).astype(jnp.bfloat16)


def dot32(a, b):
    return jnp.dot(a, b, preferred_element_type=jnp.float32)


def sketch_kernel(chunk, words_ref, freq_ref, weight_ref, basis_ref, out_ref, order_ref, held, held_sem):
    people = held.shape[0]
    steps = people // chunk
    copies = []
    for step in range(steps):
        rows = pl.ds(step * chunk, chunk)
        copy = pltpu.make_async_copy(words_ref.at[rows, :], held.at[rows, :], held_sem.at[step])
        copy.start()
        copies.append(copy)
    k = basis_ref.shape[0]
    markers = basis_ref.shape[1]
    words = markers // PER_WORD
    freq = freq_ref[...]
    scaled = basis_ref[...].astype(jnp.float32) * lax.rsqrt(2.0 * freq * (1.0 - freq))
    offset = jnp.sum(scaled * (2.0 * freq), axis=1, keepdims=True)
    high, low = split2(scaled)
    f_parts = split3(jnp.broadcast_to(freq, (8, markers)))
    stacked = jnp.concatenate((high, low) + f_parts, axis=0)
    order = to_digit_order()
    pieces = [[None] * (markers // GROUP) for _ in range(PER_WORD)]
    for group in range(markers // GROUP):
        moved = dot32(stacked[:, group * GROUP:(group + 1) * GROUP], order)
        for j in range(PER_WORD):
            pieces[j][group] = moved[:2 * k, j * LANES:(j + 1) * LANES].astype(jnp.bfloat16)
        freq_moved = moved[2 * k:2 * k + 8] + moved[2 * k + 8:2 * k + 16] + moved[2 * k + 16:2 * k + 24]
        order_ref[:, group * GROUP:(group + 1) * GROUP] = freq_moved
    arranged = [jnp.concatenate(pieces[j], axis=1) for j in range(PER_WORD)]
    for step in range(steps):
        copies[step].wait()
        rows = pl.ds(step * chunk, chunk)
        planes = digits(held[rows, :])
        total = None
        for j in range(PER_WORD):
            term = lax.dot_general(
                arranged[j], planes[j], (((1,), (1,)), ((), ())), preferred_element_type=jnp.float32
            )
            total = term if total is None else total + term
        out_ref[:, rows] = (total[:k] + total[k:] - offset) * weight_ref[:, rows]


def sketch_partial(genotype, freq, weight, basis, chunk):
    people, words = genotype.shape
    k, markers = basis.shape
    vmem = pl.BlockSpec(memory_space=pltpu.VMEM)
    return pl.pallas_call(
        functools.partial(sketch_kernel, chunk),
        out_shape=(
            jax.ShapeDtypeStruct((k, people), jnp.float32),
            jax.ShapeDtypeStruct((8, markers), jnp.float32),
        ),
        in_specs=[pl.BlockSpec(memory_space=pl.ANY), vmem, vmem, vmem],
        out_specs=(vmem, vmem),
        scratch_shapes=[
            pltpu.VMEM((people, words), jnp.int32),
            pltpu.SemaphoreType.DMA((people // chunk,)),
        ],
        compiler_params=pltpu.CompilerParams(vmem_limit_bytes=VMEM_LIMIT),
        name="sketch",
    )(genotype, freq, weight, basis)


def product_kernel(
    first_ref, second_ref, residual_ref, weight_ref, freq_ref, chosen_ref, words_ref,
    sketch_ref, basis_ref, score_ref, gram_ref, held, held_sem
):
    people, words = held.shape
    groups = words // LANES
    copies = []
    for group in range(groups):
        columns = pl.ds(group * LANES, LANES)
        copy = pltpu.make_async_copy(words_ref.at[:, columns], held.at[:, columns], held_sem.at[group])
        copy.start()
        copies.append(copy)
    sketch = first_ref[...] + second_ref[...]
    sketch_ref[...] = sketch
    k = sketch.shape[0]
    rows = jnp.concatenate([sketch, residual_ref[...].astype(jnp.float32)], axis=0)
    n_rows = rows.shape[0]
    gram_ref[:, :n_rows] = lax.dot_general(
        sketch, rows, (((1,), (1,)), ((), ())), precision=HIGHEST, preferred_element_type=jnp.float32
    )
    gram_ref[:, n_rows:] = jnp.zeros((k, gram_ref.shape[1] - n_rows), jnp.float32)
    rows = rows * weight_ref[...]
    row_sum = jnp.sum(rows, axis=1, keepdims=True)
    high, low = split2(rows)
    both = jnp.concatenate([high, low], axis=0)
    chosen = chosen_ref[...]
    score = None
    for group in range(groups):
        span = pl.ds(group * GROUP, GROUP)
        copies[group].wait()
        planes = jnp.concatenate(digits(held[:, group * LANES:(group + 1) * LANES]), axis=1)
        raw = dot32(both, planes)
        freq = freq_ref[0:1, span]
        value = (raw[:n_rows] + raw[n_rows:] - row_sum * (2.0 * freq)) * lax.rsqrt(2.0 * freq * (1.0 - freq))
        basis_ref[:, span] = value[:k]
        row = lax.broadcasted_iota(jnp.int32, (GROUP, 1), 0)
        natural = PER_WORD * jnp.bitwise_and(row, LANES - 1) + jnp.right_shift(row, 7) + group * GROUP
        pick = jnp.where(natural == chosen, 1.0, 0.0).astype(jnp.bfloat16)
        v_high, v_low = split2(value)
        term = dot32(v_high, pick) + dot32(v_low, pick)
        score = term if score is None else score + term
    score_ref[...] = score


def products(first, second, residuals, weight, freq, chosen, genotype):
    k, people = first.shape
    r = residuals.shape[0]
    words = genotype.shape[1]
    vmem = pl.BlockSpec(memory_space=pltpu.VMEM)
    return pl.pallas_call(
        product_kernel,
        out_shape=(
            jax.ShapeDtypeStruct((k, people), jnp.float32),
            jax.ShapeDtypeStruct((k, words * PER_WORD), jnp.float32),
            jax.ShapeDtypeStruct((k + r, chosen.shape[1]), jnp.float32),
            jax.ShapeDtypeStruct((k, LANES), jnp.float32),
        ),
        in_specs=[vmem] * 6 + [pl.BlockSpec(memory_space=pl.ANY)],
        out_specs=(vmem,) * 4,
        scratch_shapes=[
            pltpu.VMEM((people, words), jnp.int32),
            pltpu.SemaphoreType.DMA((words // LANES,)),
        ],
        compiler_params=pltpu.CompilerParams(vmem_limit_bytes=VMEM_LIMIT),
        name="products",
    )(first, second, residuals, weight, freq, chosen, genotype)


def eliminate(system, k):
    row_at = lax.broadcasted_iota(jnp.int32, (k, 1), 0)
    for j in range(k):
        pivot = system[j:j + 1, j:j + 1]
        scaled = system[j:j + 1, :] * lax.rsqrt(pivot)
        factor = system[:, j:j + 1] * lax.rsqrt(pivot)
        updated = system - factor * scaled
        system = jnp.where(row_at == j, scaled, jnp.where(row_at > j, updated, system))
    return system


def finish_kernel(
    root_people, k, r, digit_order, sketch_ref, gram_ref, *refs
):
    count = (len(refs) - 4) // 2
    basis_refs, score_refs = refs[:count], refs[count:2 * count]
    components_ref, coefficients_ref, next_ref, out_ref = refs[2 * count:]
    row_at = lax.broadcasted_iota(jnp.int32, (k, k), 0)
    column_at = lax.broadcasted_iota(jnp.int32, (k, k), 1)
    identity = jnp.where(row_at == column_at, 1.0, 0.0)
    grams = [gram_ref[i] for i in range(gram_ref.shape[0])]
    while len(grams) > 1:
        grams = [a + b for a, b in zip(grams[::2], grams[1::2])]
    system = jnp.concatenate([grams[0][:, :k + r], identity], axis=1)
    system = eliminate(system, k)
    coefficients = system[:, k:k + r]
    inverse = system[:, k + r:]
    coefficients_ref[...] = coefficients
    highest = functools.partial(jnp.dot, precision=HIGHEST, preferred_element_type=jnp.float32)
    components_ref[...] = root_people * highest(inverse, sketch_ref[...])
    basis_total, score_total = basis_refs[0][...], score_refs[0][...]
    for ref in basis_refs[1:]:
        basis_total = basis_total + ref[...]
    for ref in score_refs[1:]:
        score_total = score_total + ref[...]
    basis = highest(inverse, basis_total)
    if digit_order:
        order = to_natural_order()
        parts = split3(basis)
        basis = dot32(parts[0], order) + dot32(parts[1], order) + dot32(parts[2], order)
    next_ref[...] = basis
    removed = lax.dot_general(
        coefficients, highest(inverse, score_total[:k]), (((0,), (0,)), ((), ())),
        precision=HIGHEST, preferred_element_type=jnp.float32,
    )
    out_ref[...] = (score_total[k:] - removed) * (1.0 / root_people)


def finish(root_people, r, digit_order, sketch, grams, basis_parts, score_parts):
    k = sketch.shape[0]
    vmem = pl.BlockSpec(memory_space=pltpu.VMEM)
    return pl.pallas_call(
        functools.partial(finish_kernel, root_people, k, r, digit_order),
        out_shape=(
            jax.ShapeDtypeStruct(sketch.shape, jnp.float32),
            jax.ShapeDtypeStruct((k, r), jnp.float32),
            jax.ShapeDtypeStruct(basis_parts[0].shape, jnp.float32),
            jax.ShapeDtypeStruct((r, score_parts[0].shape[1]), jnp.float32),
        ),
        in_specs=[vmem] * (2 + len(basis_parts) + len(score_parts)),
        out_specs=(vmem,) * 4,
        compiler_params=pltpu.CompilerParams(vmem_limit_bytes=VMEM_LIMIT),
        name="finish",
    )(sketch, grams, *basis_parts, *score_parts)


def shards(genotype, allele_freq, person_weight, basis, residuals, block_markers):
    people, words = genotype.shape
    markers = words * PER_WORD
    k, r = basis.shape[0], residuals.shape[0]
    marker_count = lax.axis_size("markers")
    people_count = lax.axis_size("people")
    people_index = lax.axis_index("people")
    weight = person_weight[None, :]
    chosen = (block_markers - lax.axis_index("markers") * markers)[None, :]
    sketch, freq = sketch_partial(genotype, allele_freq[None, :], weight, basis, people // 4)
    apart = 1
    while apart * 2 < marker_count:
        sketch = sketch + from_partner(sketch, "markers", apart)
        apart *= 2
    other = from_partner(sketch, "markers", apart)
    sketch, basis_part, score_part, gram = products(
        sketch, other, residuals, weight, freq, chosen, genotype
    )
    basis_width = markers // people_count
    score_width = score_part.shape[1] // people_count
    if people_count == 4 and basis_width == GROUP:
        grams, basis_parts, score_parts = [gram], [], []
        for apart in range(4):
            target = jnp.bitwise_xor(people_index, apart)
            one_basis = lax.dynamic_slice_in_dim(basis_part, target * basis_width, basis_width, 1)
            one_score = lax.dynamic_slice_in_dim(score_part, target * score_width, score_width, 1)
            if apart == 0:
                basis_parts.append(one_basis)
                score_parts.append(one_score)
                continue
            sent = jnp.concatenate([one_basis] + [one_score[i * k:(i + 1) * k] for i in range((k + r) // k)] + [gram], axis=1)
            got = from_partner(sent, "people", apart)
            basis_parts.append(got[:, :basis_width])
            score_parts.append(jnp.concatenate([got[:, basis_width + i * score_width:basis_width + (i + 1) * score_width] for i in range((k + r) // k)], axis=0))
            grams.append(got[:, -LANES:])
        grams = jnp.stack(grams)
    else:
        basis_part = basis_part.reshape(k, markers // GROUP, PER_WORD, LANES)
        basis_part = jnp.swapaxes(basis_part, 2, 3).reshape(k, markers)
        basis_total, score_total, grams = lax.psum((basis_part, score_part, gram), "people")
        basis_parts = [lax.dynamic_slice_in_dim(basis_total, people_index * basis_width, basis_width, 1)]
        score_parts = [lax.dynamic_slice_in_dim(score_total, people_index * score_width, score_width, 1)]
        grams = grams[None]
    components, coefficients, basis_own, score_own = finish(
        math.sqrt(people * people_count), r, len(basis_parts) > 1, sketch, grams, basis_parts, score_parts
    )
    return components, coefficients, basis_own[None], score_own[None]


def solution(mesh):
    placed = (
        P(("cohort", "people"), "markers"),
        P(("cohort", "markers")),
        P(("cohort", "people")),
        P("cohort", "markers"),
        P("cohort", "people"),
        P("markers"),
    )
    return jax.shard_map(
        shards,
        mesh=mesh,
        in_specs=placed,
        out_specs=(
            P("cohort", "people"),
            P("cohort", None),
            P("markers", "cohort", "people"),
            P("markers", "cohort", "people"),
        ),
        check_vma=False,
    )
```

```python
import functools
import math

import jax
import jax.numpy as jnp
from jax import lax
from jax.experimental import pallas as pl
from jax.experimental.pallas import tpu as pltpu
from jax.sharding import PartitionSpec as P

LANES = 128
PER_WORD = 4
GROUP = LANES * PER_WORD
VMEM_LIMIT = 40 * 1024 * 1024
HIGHEST = lax.Precision.HIGHEST
IN_HBM = pl.BlockSpec(memory_space=pltpu.HBM)
IN_VMEM = pl.BlockSpec(memory_space=pltpu.VMEM)


def from_partner(block, axis, apart):
    count = lax.axis_size(axis)
    route = [(low, low ^ apart) for low in range(count)]
    return lax.ppermute(block, axis, route)


def split2(value):
    high = value.astype(jnp.bfloat16)
    low = (value - high.astype(jnp.float32)).astype(jnp.bfloat16)
    return high, low


def split3(value):
    high, rest = value.astype(jnp.bfloat16), None
    rest = value - high.astype(jnp.float32)
    middle, low = split2(rest)
    return high, middle, low


def digits(words):
    out = []
    for j in range(PER_WORD):
        one = words if j == 0 else jnp.right_shift(words, 2 * j)
        one = one if j == PER_WORD - 1 else jnp.bitwise_and(one, 3)
        out.append(one.astype(jnp.float32).astype(jnp.bfloat16))
    return out


def natural_of_column(shape):
    column = lax.broadcasted_iota(jnp.int32, shape, len(shape) - 1)
    return PER_WORD * jnp.bitwise_and(column, LANES - 1) + jnp.right_shift(column, 7)


def to_digit_order():
    row = lax.broadcasted_iota(jnp.int32, (GROUP, GROUP), 0)
    column = natural_of_column((1, GROUP))
    return jnp.where(row == column, 1.0, 0.0).astype(jnp.bfloat16)


def to_natural_order():
    row = lax.broadcasted_iota(jnp.int32, (GROUP, GROUP), 0)
    natural = PER_WORD * jnp.bitwise_and(row, LANES - 1) + jnp.right_shift(row, 7)
    column = lax.broadcasted_iota(jnp.int32, (GROUP, GROUP), 1)
    return jnp.where(natural == column, 1.0, 0.0).astype(jnp.bfloat16)


def dot32(a, b):
    return jnp.dot(a, b, preferred_element_type=jnp.float32)


def start_copy(source, target, sem):
    copy = pltpu.make_async_copy(source, target, sem)
    copy.start()
    return copy


def group_of(slot, direct):
    return jnp.bitwise_xor(lax.axis_index("people"), slot) if direct else slot


def sketch_kernel(
    chunk, words_ref, freq_ref, weight_ref, basis_ref, out_ref, order_ref, planes_ref,
    words, freq_here, weight_here, basis_here, words_sem, sems
):
    people = words.shape[0]
    steps = people // chunk
    small = [
        start_copy(freq_ref, freq_here, sems.at[0]),
        start_copy(basis_ref, basis_here, sems.at[1]),
        start_copy(weight_ref, weight_here, sems.at[2]),
    ]
    copies = []
    for step in range(steps):
        rows = pl.ds(step * chunk, chunk)
        copies.append(start_copy(words_ref.at[rows, :], words.at[rows, :], words_sem.at[step]))
    k, markers = basis_here.shape
    per_digit = markers // PER_WORD
    order = to_digit_order()
    for copy in small:
        copy.wait()
    freq = freq_here[...].reshape(1, markers)
    weight = weight_here[...].reshape(1, people)
    scaled = basis_here[...].astype(jnp.float32) * lax.rsqrt(2.0 * freq * (1.0 - freq))
    offset = jnp.sum(scaled * (2.0 * freq), axis=1, keepdims=True)
    high, low = split2(scaled)
    f_parts = split3(jnp.broadcast_to(freq, (8, markers)))
    stacked = jnp.concatenate((high, low) + f_parts, axis=0)
    pieces = [[None] * (markers // GROUP) for _ in range(PER_WORD)]
    for group in range(markers // GROUP):
        moved = dot32(stacked[:, group * GROUP:(group + 1) * GROUP], order)
        for j in range(PER_WORD):
            pieces[j][group] = moved[:2 * k, j * LANES:(j + 1) * LANES].astype(jnp.bfloat16)
        freq_moved = moved[2 * k:2 * k + 8] + moved[2 * k + 8:2 * k + 16] + moved[2 * k + 16:2 * k + 24]
        order_ref[:, group * GROUP:(group + 1) * GROUP] = freq_moved
    arranged = [jnp.concatenate(pieces[j], axis=1) for j in range(PER_WORD)]
    for step in range(steps):
        copies[step].wait()
        rows = pl.ds(step * chunk, chunk)
        planes = digits(words[rows, :])
        total = None
        for j in range(PER_WORD):
            for group in range(markers // GROUP):
                at = group * GROUP + j * LANES
                planes_ref[rows, at:at + LANES] = planes[j][:, group * LANES:(group + 1) * LANES]
            term = lax.dot_general(
                arranged[j], planes[j], (((1,), (1,)), ((), ())), preferred_element_type=jnp.float32
            )
            total = term if total is None else total + term
        out_ref[:, rows] = (total[:k] + total[k:] - offset) * weight[:, step * chunk:(step + 1) * chunk]


def sketch_partial(genotype, freq, weight, basis, chunk):
    people, words = genotype.shape
    k, markers = basis.shape
    return pl.pallas_call(
        functools.partial(sketch_kernel, chunk),
        out_shape=(
            jax.ShapeDtypeStruct((k, people), jnp.float32),
            jax.ShapeDtypeStruct((8, markers), jnp.float32),
            jax.ShapeDtypeStruct((people, markers), jnp.bfloat16),
        ),
        in_specs=[IN_HBM] * 4,
        out_specs=(IN_VMEM,) * 3,
        scratch_shapes=[
            pltpu.VMEM((people, words), jnp.int32),
            pltpu.VMEM(freq.shape, jnp.float32),
            pltpu.VMEM(weight.shape, jnp.float32),
            pltpu.VMEM(basis.shape, jnp.bfloat16),
            pltpu.SemaphoreType.DMA((people // chunk,)),
            pltpu.SemaphoreType.DMA((3,)),
        ],
        compiler_params=pltpu.CompilerParams(vmem_limit_bytes=VMEM_LIMIT),
        name="sketch",
    )(genotype, freq, weight, basis)


def standard(rows, planes_ref, order_ref, span):
    n_rows = rows.shape[0]
    row_sum = jnp.sum(rows, axis=1, keepdims=True)
    raw = dot32(jnp.concatenate(split2(rows), axis=0), planes_ref[:, span])
    freq = order_ref[0:1, span]
    return (raw[:n_rows] + raw[n_rows:] - row_sum * (2.0 * freq)) * lax.rsqrt(2.0 * freq * (1.0 - freq))


def trait_kernel(
    direct, planes_ref, order_ref, residual_ref, weight_ref, chosen_ref, *refs
):
    outs, (pick_ref, total, residual_here, weight_here, chosen_here, sems) = refs[:-6], refs[-6:]
    copies = [
        start_copy(residual_ref, residual_here, sems.at[0]),
        start_copy(weight_ref, weight_here, sems.at[1]),
        start_copy(chosen_ref, chosen_here, sems.at[2]),
    ]
    markers = planes_ref.shape[1]
    for copy in copies:
        copy.wait()
    n_chosen = chosen_here.shape[0]
    chosen = chosen_here[...].reshape(1, n_chosen) - lax.axis_index("markers") * markers
    rows = residual_here[...].astype(jnp.float32) * weight_here[...].reshape(1, -1)
    score = None
    for group in range(markers // GROUP):
        span = slice(group * GROUP, (group + 1) * GROUP)
        row = lax.broadcasted_iota(jnp.int32, (GROUP, 1), 0)
        natural = PER_WORD * jnp.bitwise_and(row, LANES - 1) + jnp.right_shift(row, 7) + group * GROUP
        pick = jnp.where(natural == chosen, 1.0, 0.0).astype(jnp.bfloat16)
        pick_ref[span, :] = pick
        high, low = split2(standard(rows, planes_ref, order_ref, span))
        term = dot32(high, pick) + dot32(low, pick)
        score = term if score is None else score + term
    total[...] = score
    width = n_chosen // len(outs)
    for slot, out in enumerate(outs):
        at = pl.multiple_of(group_of(slot, direct) * width, width)
        out[...] = total[:, pl.ds(at, width)]


def trait_scores(planes, order, residuals, weight, chosen, direct):
    people, markers = planes.shape
    r = residuals.shape[0]
    groups = markers // GROUP
    n_chosen = chosen.shape[0]
    out = pl.pallas_call(
        functools.partial(trait_kernel, direct),
        out_shape=tuple(
            jax.ShapeDtypeStruct((r, n_chosen // groups), jnp.float32) for _ in range(groups)
        ) + (jax.ShapeDtypeStruct((markers, n_chosen), jnp.bfloat16),),
        in_specs=[IN_VMEM] * 2 + [IN_HBM] * 3,
        out_specs=(IN_VMEM,) * (groups + 1),
        scratch_shapes=[
            pltpu.VMEM((r, n_chosen), jnp.float32),
            pltpu.VMEM(residuals.shape, residuals.dtype),
            pltpu.VMEM(weight.shape, jnp.float32),
            pltpu.VMEM(chosen.shape, jnp.int32),
            pltpu.SemaphoreType.DMA((3,)),
        ],
        compiler_params=pltpu.CompilerParams(vmem_limit_bytes=VMEM_LIMIT),
        cost_estimate=pl.CostEstimate(flops=2 * 2 * r * people * markers, bytes_accessed=2 * people * markers, transcendentals=0),
        name="traits",
    )(planes, order, residuals, weight, chosen)
    return list(out[:-1]), out[-1]


def product_kernel(
    direct, first_ref, second_ref, planes_ref, order_ref, pick_ref, residual_ref, weight_ref, *refs
):
    outs = refs[:-7]
    gram_ref, sketch_ref, value, score, residual_here, weight_here, sems = refs[-7:]
    copies = [
        start_copy(residual_ref, residual_here, sems.at[0]),
        start_copy(weight_ref, weight_here, sems.at[1]),
    ]
    sketch = first_ref[...] + second_ref[...]
    sketch_ref[...] = sketch
    k = sketch.shape[0]
    for copy in copies:
        copy.wait()
    rows = jnp.concatenate([sketch, residual_here[...].astype(jnp.float32)], axis=0)
    n_rows = rows.shape[0]
    gram_ref[:, :n_rows] = lax.dot_general(
        sketch, rows, (((1,), (1,)), ((), ())), precision=HIGHEST, preferred_element_type=jnp.float32
    )
    gram_ref[:, n_rows:] = jnp.zeros((k, gram_ref.shape[1] - n_rows), jnp.float32)
    rows = sketch * weight_here[...].reshape(1, -1)
    total = None
    for group in range(len(outs)):
        span = slice(group * GROUP, (group + 1) * GROUP)
        piece = standard(rows, planes_ref, order_ref, span)
        value[:, span] = piece
        high, low = split2(piece)
        both = dot32(jnp.concatenate([high, low], axis=0), pick_ref[span, :])
        term = both[:k] + both[k:]
        total = term if total is None else total + term
    score[...] = total
    width = total.shape[1] // len(outs)
    for slot, out in enumerate(outs):
        group = group_of(slot, direct)
        out[:, :GROUP] = value[:, pl.ds(pl.multiple_of(group * GROUP, GROUP), GROUP)]
        out[:, GROUP:] = score[:, pl.ds(pl.multiple_of(group * width, width), width)]


def products(first, second, planes, order, pick, residuals, weight, direct):
    k, people = first.shape
    markers, n_chosen = pick.shape
    groups = markers // GROUP
    out = pl.pallas_call(
        functools.partial(product_kernel, direct),
        out_shape=tuple(
            jax.ShapeDtypeStruct((k, GROUP + n_chosen // groups), jnp.float32) for _ in range(groups)
        ) + (
            jax.ShapeDtypeStruct((k, LANES), jnp.float32),
            jax.ShapeDtypeStruct((k, people), jnp.float32),
        ),
        in_specs=[IN_VMEM] * 5 + [IN_HBM] * 2,
        out_specs=(IN_VMEM,) * (groups + 2),
        scratch_shapes=[
            pltpu.VMEM((k, markers), jnp.float32),
            pltpu.VMEM((k, n_chosen), jnp.float32),
            pltpu.VMEM(residuals.shape, residuals.dtype),
            pltpu.VMEM(weight.shape, jnp.float32),
            pltpu.SemaphoreType.DMA((2,)),
        ],
        compiler_params=pltpu.CompilerParams(vmem_limit_bytes=VMEM_LIMIT),
        name="products",
    )(first, second, planes, order, pick, residuals, weight)
    return list(out[:-2]), out[-2], out[-1]


def eliminate(system, k):
    row_at = lax.broadcasted_iota(jnp.int32, (k, 1), 0)
    for j in range(k):
        pivot = system[j:j + 1, j:j + 1]
        scaled = system[j:j + 1, :] * lax.rsqrt(pivot)
        factor = system[:, j:j + 1] * lax.rsqrt(pivot)
        updated = system - factor * scaled
        system = jnp.where(row_at == j, scaled, jnp.where(row_at > j, updated, system))
    return system


def factor_kernel(root_people, r, sketch_ref, *refs):
    gram_refs, (components_ref, coefficients_ref, system_ref) = refs[:-3], refs[-3:]
    k = sketch_ref.shape[0]
    row_at = lax.broadcasted_iota(jnp.int32, (k, k), 0)
    column_at = lax.broadcasted_iota(jnp.int32, (k, k), 1)
    identity = jnp.where(row_at == column_at, 1.0, 0.0)
    grams = [ref[...] for ref in gram_refs]
    while len(grams) > 1:
        grams = [a + b for a, b in zip(grams[::2], grams[1::2])]
    system = eliminate(jnp.concatenate([grams[0][:, :k + r], identity], axis=1), k)
    system_ref[...] = system
    coefficients_ref[...] = system[:, k:k + r]
    components_ref[...] = root_people * jnp.dot(
        system[:, k + r:], sketch_ref[...], precision=HIGHEST, preferred_element_type=jnp.float32
    )


def factor(root_people, r, sketch, grams):
    k, people = sketch.shape
    return pl.pallas_call(
        functools.partial(factor_kernel, root_people, r),
        out_shape=(
            jax.ShapeDtypeStruct(sketch.shape, jnp.float32),
            jax.ShapeDtypeStruct((k, r), jnp.float32),
            jax.ShapeDtypeStruct((k, 2 * k + r), jnp.float32),
        ),
        in_specs=[IN_VMEM] * (1 + len(grams)),
        out_specs=(IN_VMEM,) * 3,
        compiler_params=pltpu.CompilerParams(vmem_limit_bytes=VMEM_LIMIT),
        name="factor",
    )(sketch, *grams)


def finish_kernel(root_people, r, digit_order, system_ref, *refs):
    count = (len(refs) - 2) // 2
    parts, scores = refs[:count], refs[count:2 * count]
    next_ref, out_ref = refs[2 * count:]
    k = system_ref.shape[0]
    coefficients = system_ref[:, k:k + r]
    inverse = system_ref[:, k + r:]
    total, score = parts[0][...], scores[0][...]
    for ref in parts[1:]:
        total = total + ref[...]
    for ref in scores[1:]:
        score = score + ref[...]
    solved = jnp.dot(inverse, total, precision=HIGHEST, preferred_element_type=jnp.float32)
    width = next_ref.shape[1]
    basis = solved[:, :width]
    if digit_order:
        order = to_natural_order()
        high, middle, low = split3(basis)
        basis = dot32(high, order) + dot32(middle, order) + dot32(low, order)
    next_ref[...] = basis
    removed = lax.dot_general(
        coefficients, solved[:, width:], (((0,), (0,)), ((), ())),
        precision=HIGHEST, preferred_element_type=jnp.float32,
    )
    out_ref[...] = (score - removed) * (1.0 / root_people)


def finish(root_people, r, digit_order, system, parts, scores):
    k = system.shape[0]
    width = scores[0].shape[1]
    return pl.pallas_call(
        functools.partial(finish_kernel, root_people, r, digit_order),
        out_shape=(
            jax.ShapeDtypeStruct((k, parts[0].shape[1] - width), jnp.float32),
            jax.ShapeDtypeStruct((r, width), jnp.float32),
        ),
        in_specs=[IN_VMEM] * (1 + len(parts) + len(scores)),
        out_specs=(IN_VMEM,) * 2,
        compiler_params=pltpu.CompilerParams(vmem_limit_bytes=VMEM_LIMIT),
        name="finish",
    )(system, *parts, *scores)


def shards(genotype, allele_freq, person_weight, basis, residuals, block_markers):
    people, words = genotype.shape
    markers = words * PER_WORD
    k, r = basis.shape[0], residuals.shape[0]
    marker_count = lax.axis_size("markers")
    people_count = lax.axis_size("people")
    groups = markers // GROUP
    direct = people_count == groups and groups == 4
    sketch, order, planes = sketch_partial(genotype, allele_freq, person_weight, basis, people // 4)
    apart = 1
    while apart * 2 < marker_count:
        sketch = sketch + from_partner(sketch, "markers", apart)
        apart *= 2
    other = from_partner(sketch, "markers", apart)
    scores, pick = trait_scores(planes, order, residuals, person_weight, block_markers, direct)
    if direct:
        scores = scores[:1] + [from_partner(scores[i], "people", i) for i in range(1, groups)]
    parts, gram, sketch = products(sketch, other, planes, order, pick, residuals, person_weight, direct)
    if direct:
        grams = [gram] + [from_partner(gram, "people", i) for i in range(1, groups)]
        parts = parts[:1] + [from_partner(parts[i], "people", i) for i in range(1, groups)]
    else:
        value = jnp.stack([part[:, :GROUP] for part in parts], axis=1)
        value = value.reshape(k, groups, PER_WORD, LANES).swapaxes(2, 3).reshape(k, markers)
        projected = jnp.concatenate([part[:, GROUP:] for part in parts], axis=1)
        score = jnp.concatenate(scores, axis=1)
        value, projected, score, gram = lax.psum((value, projected, score, gram), "people")
        index = lax.axis_index("people")

        def own(whole):
            width = whole.shape[1] // people_count
            return lax.dynamic_slice_in_dim(whole, index * width, width, 1)
        parts = [jnp.concatenate([own(value), own(projected)], axis=1)]
        scores, grams = [own(score)], [gram]
    root_people = math.sqrt(people * people_count)
    components, coefficients, system = factor(root_people, r, sketch, grams)
    basis_own, score_own = finish(root_people, r, direct, system, parts, scores)
    return components, coefficients, basis_own[None], score_own[None]


def solution(mesh):
    placed = (
        P(("cohort", "people"), "markers"),
        P(("cohort", "markers")),
        P(("cohort", "people")),
        P("cohort", "markers"),
        P("cohort", "people"),
        P("markers"),
    )
    return jax.shard_map(
        shards,
        mesh=mesh,
        in_specs=placed,
        out_specs=(
            P("cohort", "people"),
            P("cohort", None),
            P("markers", "cohort", "people"),
            P("markers", "cohort", "people"),
        ),
        check_vma=False,
    )
```

```python
import functools
import math

import jax
import jax.numpy as jnp
from jax import lax
from jax.experimental import pallas as pl
from jax.experimental.pallas import tpu as pltpu
from jax.sharding import PartitionSpec as P

LANES = 128
PER_WORD = 4
GROUP = LANES * PER_WORD
VMEM_LIMIT = 40 * 1024 * 1024
HIGHEST = lax.Precision.HIGHEST
IN_VMEM = pl.BlockSpec(memory_space=pltpu.VMEM)


def from_partner(block, axis, apart):
    count = lax.axis_size(axis)
    route = [(low, low ^ apart) for low in range(count)]
    return lax.ppermute(block, axis, route)


def split2(value):
    high = value.astype(jnp.bfloat16)
    low = (value - high.astype(jnp.float32)).astype(jnp.bfloat16)
    return high, low


def split3(value):
    high, rest = value.astype(jnp.bfloat16), None
    rest = value - high.astype(jnp.float32)
    middle, low = split2(rest)
    return high, middle, low


def digits(words):
    out = []
    for j in range(PER_WORD):
        one = jnp.bitwise_and(jnp.right_shift(words, 2 * j), 3)
        out.append(one.astype(jnp.bfloat16))
    return out


def natural_of_column(shape):
    column = lax.broadcasted_iota(jnp.int32, shape, len(shape) - 1)
    return PER_WORD * jnp.bitwise_and(column, LANES - 1) + jnp.right_shift(column, 7)


def to_digit_order():
    row = lax.broadcasted_iota(jnp.int32, (GROUP, GROUP), 0)
    column = natural_of_column((1, GROUP))
    return jnp.where(row == column, 1.0, 0.0).astype(jnp.bfloat16)


def to_natural_order():
    row = lax.broadcasted_iota(jnp.int32, (GROUP, GROUP), 0)
    natural = PER_WORD * jnp.bitwise_and(row, LANES - 1) + jnp.right_shift(row, 7)
    column = lax.broadcasted_iota(jnp.int32, (GROUP, GROUP), 1)
    return jnp.where(natural == column, 1.0, 0.0).astype(jnp.bfloat16)


def dot32(a, b):
    return jnp.dot(a, b, preferred_element_type=jnp.float32)


def group_of(slot, direct):
    return jnp.bitwise_xor(lax.axis_index("people"), slot) if direct else slot


def sketch_kernel(chunk, scaled_ref, shifted_ref, *refs):
    planes_refs, out_ref = refs[:-1], refs[-1]
    k, markers = scaled_ref.shape
    people = out_ref.shape[1]
    offset = jnp.sum(shifted_ref[...], axis=1, keepdims=True)
    order = to_digit_order()
    stacked = jnp.concatenate(split2(scaled_ref[...]), axis=0)
    pieces = [[] for _ in range(PER_WORD)]
    for group in range(markers // GROUP):
        moved = dot32(stacked[:, group * GROUP:(group + 1) * GROUP], order).astype(jnp.bfloat16)
        for j in range(PER_WORD):
            pieces[j].append(moved[:, j * LANES:(j + 1) * LANES])
    arranged = [jnp.concatenate(pieces[j], axis=1) for j in range(PER_WORD)]
    for at in range(0, people, chunk):
        total = None
        for j in range(PER_WORD):
            term = lax.dot_general(
                arranged[j], planes_refs[j][at:at + chunk, :], (((1,), (1,)), ((), ())),
                preferred_element_type=jnp.float32,
            )
            total = term if total is None else total + term
        out_ref[:, at:at + chunk] = total[:k] + total[k:] - offset


def sketch_partial(scaled, shifted, planes, chunk):
    return pl.pallas_call(
        functools.partial(sketch_kernel, chunk),
        out_shape=jax.ShapeDtypeStruct((scaled.shape[0], planes[0].shape[0]), jnp.float32),
        in_specs=[IN_VMEM] * (2 + len(planes)),
        out_specs=IN_VMEM,
        compiler_params=pltpu.CompilerParams(vmem_limit_bytes=VMEM_LIMIT),
        name="sketch",
    )(scaled, shifted, *planes)


def standard(rows, planes_refs, freq, group):
    n_rows = rows.shape[0]
    row_sum = jnp.sum(rows, axis=1, keepdims=True)
    at = group * LANES
    planes = jnp.concatenate([ref[:, at:at + LANES] for ref in planes_refs], axis=1)
    raw = dot32(jnp.concatenate(split2(rows), axis=0), planes)
    return (raw[:n_rows] + raw[n_rows:] - row_sum * (2.0 * freq)) * lax.rsqrt(2.0 * freq * (1.0 - freq))


def trait_kernel(direct, freq_ref, residual_ref, weight_ref, chosen_ref, *refs):
    planes_refs, outs = refs[:PER_WORD], refs[PER_WORD:-3]
    order_ref, pick_ref, total = refs[-3:]
    markers, n_chosen = pick_ref.shape
    chosen = chosen_ref[...].reshape(1, n_chosen) - lax.axis_index("markers") * markers
    rows = residual_ref[...].astype(jnp.float32) * weight_ref[...].reshape(1, -1)
    freq = jnp.broadcast_to(freq_ref[...].reshape(1, markers), (8, markers))
    freq = jnp.concatenate(split3(freq), axis=0)
    order = to_digit_order()
    score = None
    for group in range(markers // GROUP):
        span = slice(group * GROUP, (group + 1) * GROUP)
        row = lax.broadcasted_iota(jnp.int32, (GROUP, 1), 0)
        natural = PER_WORD * jnp.bitwise_and(row, LANES - 1) + jnp.right_shift(row, 7) + group * GROUP
        pick = jnp.where(natural == chosen, 1.0, 0.0).astype(jnp.bfloat16)
        pick_ref[span, :] = pick
        moved = dot32(freq[:, span], order)
        moved = moved[:8] + moved[8:16] + moved[16:]
        order_ref[:, span] = moved
        high, low = split2(standard(rows, planes_refs, moved[0:1], group))
        term = dot32(high, pick) + dot32(low, pick)
        score = term if score is None else score + term
    total[...] = score
    width = n_chosen // len(outs)
    for slot, out in enumerate(outs):
        at = pl.multiple_of(group_of(slot, direct) * width, width)
        out[...] = total[:, pl.ds(at, width)]


def trait_scores(planes, freq, residuals, weight, chosen, direct):
    people, words = planes[0].shape
    markers = words * PER_WORD
    r = residuals.shape[0]
    groups = markers // GROUP
    n_chosen = chosen.shape[0]
    out = pl.pallas_call(
        functools.partial(trait_kernel, direct),
        out_shape=tuple(
            jax.ShapeDtypeStruct((r, n_chosen // groups), jnp.float32) for _ in range(groups)
        ) + (
            jax.ShapeDtypeStruct((8, markers), jnp.float32),
            jax.ShapeDtypeStruct((markers, n_chosen), jnp.bfloat16),
        ),
        in_specs=[IN_VMEM] * (4 + len(planes)),
        out_specs=(IN_VMEM,) * (groups + 2),
        scratch_shapes=[pltpu.VMEM((r, n_chosen), jnp.float32)],
        compiler_params=pltpu.CompilerParams(vmem_limit_bytes=VMEM_LIMIT),
        cost_estimate=pl.CostEstimate(flops=2 * 2 * r * people * markers, bytes_accessed=2 * people * markers, transcendentals=0),
        name="traits",
    )(freq, residuals, weight, chosen, *planes)
    return out[:-2], out[-2], out[-1]


def product_kernel(direct, first_ref, second_ref, order_ref, pick_ref, residual_ref, weight_ref, *refs):
    planes_refs, refs = refs[:PER_WORD], refs[PER_WORD:]
    sketch_ref, value, score = refs[-3:]
    groups = (len(refs) - 3) // 2
    trait_refs, outs = refs[:groups], refs[groups:2 * groups]
    weight = weight_ref[...].reshape(1, -1)
    sketch = (first_ref[...] + second_ref[...]) * weight
    sketch_ref[...] = sketch
    k = sketch.shape[0]
    rows = sketch * weight
    total = None
    for group in range(groups):
        span = slice(group * GROUP, (group + 1) * GROUP)
        piece = standard(rows, planes_refs, order_ref[0:1, span], group)
        value[:, span] = piece
        both = dot32(jnp.concatenate(split2(piece), axis=0), pick_ref[span, :])
        term = both[:k] + both[k:]
        total = term if total is None else total + term
    score[...] = total
    rows = jnp.concatenate([sketch, residual_ref[...].astype(jnp.float32)], axis=0)
    gram = lax.dot_general(
        sketch, rows, (((1,), (1,)), ((), ())), precision=HIGHEST, preferred_element_type=jnp.float32
    )
    width = total.shape[1] // groups
    for slot, out in enumerate(outs):
        group = group_of(slot, direct)
        at = GROUP
        out[:, :at] = value[:, pl.ds(pl.multiple_of(group * GROUP, GROUP), GROUP)]
        out[:, at:at + width] = score[:, pl.ds(pl.multiple_of(group * width, width), width)]
        at += width
        for first in range(0, trait_refs[slot].shape[0], k):
            out[:, at:at + width] = trait_refs[slot][first:first + k, :]
            at += width
        out[:, at:at + gram.shape[1]] = gram
        if at + gram.shape[1] < out.shape[1]:
            out[:, at + gram.shape[1]:] = jnp.zeros((k, out.shape[1] - at - gram.shape[1]), jnp.float32)


def products(first, second, order, pick, residuals, weight, planes, traits, direct):
    k, people = first.shape
    markers, n_chosen = pick.shape
    groups = markers // GROUP
    r, width = traits[0].shape
    gram_room = -(-(k + r) // LANES) * LANES
    out = pl.pallas_call(
        functools.partial(product_kernel, direct),
        out_shape=tuple(
            jax.ShapeDtypeStruct((k, GROUP + width + r // k * width + gram_room), jnp.float32)
            for _ in range(groups)
        ) + (jax.ShapeDtypeStruct((k, people), jnp.float32),),
        in_specs=[IN_VMEM] * (6 + len(planes) + groups),
        out_specs=(IN_VMEM,) * (groups + 1),
        scratch_shapes=[
            pltpu.VMEM((k, markers), jnp.float32),
            pltpu.VMEM((k, n_chosen), jnp.float32),
        ],
        compiler_params=pltpu.CompilerParams(vmem_limit_bytes=VMEM_LIMIT),
        name="products",
    )(first, second, order, pick, residuals, weight, *planes, *traits)
    return list(out[:-1]), out[-1]


def eliminate(system, k):
    row_at = lax.broadcasted_iota(jnp.int32, (k, 1), 0)
    shape = system.shape
    block = 8
    for start in range(0, k, block):
        columns = [
            jnp.broadcast_to(system[:, j:j + 1], shape) for j in range(start, start + block)
        ]
        for t in range(block):
            j = start + t
            inverse = lax.rsqrt(columns[t][j:j + 1, :])
            factor = columns[t] * inverse
            for s in range(t + 1, block):
                columns[s] = columns[s] - factor * factor[start + s:start + s + 1, :]
            scaled = system[j:j + 1, :] * inverse
            updated = system - factor * scaled
            system = jnp.where(row_at == j, scaled, jnp.where(row_at > j, updated, system))
    return system


def finish_kernel(root_people, k, r, width, score_width, digit_order, sketch_ref, *refs):
    parts, (components_ref, coefficients_ref, next_ref, out_ref) = refs[:-4], refs[-4:]
    row_at = lax.broadcasted_iota(jnp.int32, (k, k), 0)
    column_at = lax.broadcasted_iota(jnp.int32, (k, k), 1)
    identity = jnp.where(row_at == column_at, 1.0, 0.0)
    totals = [ref[...] for ref in parts]
    while len(totals) > 1:
        totals = [a + b for a, b in zip(totals[::2], totals[1::2])]
    total = totals[0]
    traits_at = width + score_width
    gram_at = traits_at + r // k * score_width
    system = eliminate(jnp.concatenate([total[:, gram_at:gram_at + k + r], identity], axis=1), k)
    coefficients = system[:, k:k + r]
    inverse = system[:, k + r:]
    coefficients_ref[...] = coefficients
    components_ref[...] = root_people * jnp.dot(
        inverse, sketch_ref[...], precision=HIGHEST, preferred_element_type=jnp.float32
    )
    solved = jnp.dot(
        inverse, total[:, :traits_at], precision=HIGHEST, preferred_element_type=jnp.float32
    )
    basis = solved[:, :width]
    if digit_order:
        both = dot32(jnp.concatenate(split2(basis), axis=0), to_natural_order())
        basis = both[:k] + both[k:]
    next_ref[...] = basis
    removed = lax.dot_general(
        coefficients, solved[:, width:], (((0,), (0,)), ((), ())),
        precision=HIGHEST, preferred_element_type=jnp.float32,
    )
    for i in range(r // k):
        at = traits_at + i * score_width
        out_ref[i * k:(i + 1) * k, :] = (
            total[:, at:at + score_width] - removed[i * k:(i + 1) * k]
        ) * (1.0 / root_people)


def finish(root_people, r, width, score_width, digit_order, sketch, parts):
    k = sketch.shape[0]
    return pl.pallas_call(
        functools.partial(finish_kernel, root_people, k, r, width, score_width, digit_order),
        out_shape=(
            jax.ShapeDtypeStruct(sketch.shape, jnp.float32),
            jax.ShapeDtypeStruct((k, r), jnp.float32),
            jax.ShapeDtypeStruct((k, width), jnp.float32),
            jax.ShapeDtypeStruct((r, score_width), jnp.float32),
        ),
        in_specs=[IN_VMEM] * (1 + len(parts)),
        out_specs=(IN_VMEM,) * 4,
        compiler_params=pltpu.CompilerParams(vmem_limit_bytes=VMEM_LIMIT),
        name="finish",
    )(sketch, *parts)


def shards(genotype, allele_freq, person_weight, basis, residuals, block_markers):
    people, words = genotype.shape
    markers = words * PER_WORD
    k, r = basis.shape[0], residuals.shape[0]
    marker_count = lax.axis_size("markers")
    people_count = lax.axis_size("people")
    groups = markers // GROUP
    direct = people_count == groups and groups == 4
    score_width = block_markers.shape[0] // people_count
    planes = digits(genotype)
    scaled = basis.astype(jnp.float32) * lax.rsqrt(2.0 * allele_freq * (1.0 - allele_freq))[None, :]
    shifted = scaled * (2.0 * allele_freq)[None, :]
    sketch = sketch_partial(scaled, shifted, planes, people // 4)
    apart = 1
    while apart * 2 < marker_count:
        sketch = sketch + from_partner(sketch, "markers", apart)
        apart *= 2
    other = from_partner(sketch, "markers", apart)
    traits, order, pick = trait_scores(
        planes, allele_freq, residuals, person_weight, block_markers, direct
    )
    parts, sketch = products(
        sketch, other, order, pick, residuals, person_weight, planes, traits, direct
    )
    if direct:
        parts = parts[:1] + [from_partner(parts[i], "people", i) for i in range(1, groups)]
    else:
        part_width = block_markers.shape[0] // groups
        whole = jnp.stack(parts, axis=1)
        value = whole[:, :, :GROUP].reshape(k, groups, PER_WORD, LANES)
        value = value.swapaxes(2, 3).reshape(k, markers)
        ends = [GROUP + i * part_width for i in range(r // k + 2)]
        scores = [whole[:, :, at:at + part_width].reshape(k, -1) for at in ends[:-1]]
        total = lax.psum((value, scores, parts[0][:, ends[-1]:]), "people")
        index = lax.axis_index("people")

        def own(array):
            width = array.shape[1] // people_count
            return lax.dynamic_slice_in_dim(array, index * width, width, 1)
        parts = [jnp.concatenate([own(total[0])] + [own(one) for one in total[1]] + [total[2]], axis=1)]
    components, coefficients, basis_own, score_own = finish(
        math.sqrt(people * people_count), r, markers // people_count, score_width, direct, sketch, parts
    )
    return components, coefficients, basis_own[None], score_own[None]


def solution(mesh):
    placed = (
        P(("cohort", "people"), "markers"),
        P(("cohort", "markers")),
        P(("cohort", "people")),
        P("cohort", "markers"),
        P("cohort", "people"),
        P("markers"),
    )
    return jax.shard_map(
        shards,
        mesh=mesh,
        in_specs=placed,
        out_specs=(
            P("cohort", "people"),
            P("cohort", None),
            P("markers", "cohort", "people"),
            P("markers", "cohort", "people"),
        ),
        check_vma=False,
    )
```

```python
import functools
import math

import jax
import jax.numpy as jnp
from jax import lax
from jax.experimental import pallas as pl
from jax.experimental.pallas import tpu as pltpu
from jax.sharding import PartitionSpec as P

LANES = 128
PER_WORD = 4
GROUP = LANES * PER_WORD
VMEM_LIMIT = 40 * 1024 * 1024
HIGHEST = lax.Precision.HIGHEST
IN_VMEM = pl.BlockSpec(memory_space=pltpu.VMEM)


def from_partner(block, axis, apart):
    count = lax.axis_size(axis)
    route = [(low, low ^ apart) for low in range(count)]
    return lax.ppermute(block, axis, route)


def split2(value):
    high = value.astype(jnp.bfloat16)
    low = (value - high.astype(jnp.float32)).astype(jnp.bfloat16)
    return high, low


def split3(value):
    high, rest = value.astype(jnp.bfloat16), None
    rest = value - high.astype(jnp.float32)
    middle, low = split2(rest)
    return high, middle, low


def digits(words):
    out = []
    for j in range(PER_WORD):
        one = jnp.bitwise_and(jnp.right_shift(words, 2 * j), 3)
        out.append(one.astype(jnp.bfloat16))
    return out


def natural_of_column(shape):
    column = lax.broadcasted_iota(jnp.int32, shape, len(shape) - 1)
    return PER_WORD * jnp.bitwise_and(column, LANES - 1) + jnp.right_shift(column, 7)


def to_digit_order():
    row = lax.broadcasted_iota(jnp.int32, (GROUP, GROUP), 0)
    column = natural_of_column((1, GROUP))
    return jnp.where(row == column, 1.0, 0.0).astype(jnp.bfloat16)


def to_natural_order():
    row = lax.broadcasted_iota(jnp.int32, (GROUP, GROUP), 0)
    natural = PER_WORD * jnp.bitwise_and(row, LANES - 1) + jnp.right_shift(row, 7)
    column = lax.broadcasted_iota(jnp.int32, (GROUP, GROUP), 1)
    return jnp.where(natural == column, 1.0, 0.0).astype(jnp.bfloat16)


def dot32(a, b):
    return jnp.dot(a, b, preferred_element_type=jnp.float32)


def group_of(slot, direct):
    return jnp.bitwise_xor(lax.axis_index("people"), slot) if direct else slot


def sketch_kernel(chunk, scaled_ref, shifted_ref, *refs):
    planes_refs, out_ref = refs[:-1], refs[-1]
    k, markers = scaled_ref.shape
    people = out_ref.shape[1]
    offset = jnp.sum(shifted_ref[...], axis=1, keepdims=True)
    order = to_digit_order()
    stacked = jnp.concatenate(split2(scaled_ref[...]), axis=0)
    pieces = [[] for _ in range(PER_WORD)]
    for group in range(markers // GROUP):
        moved = dot32(stacked[:, group * GROUP:(group + 1) * GROUP], order).astype(jnp.bfloat16)
        for j in range(PER_WORD):
            pieces[j].append(moved[:, j * LANES:(j + 1) * LANES])
    arranged = [jnp.concatenate(pieces[j], axis=1) for j in range(PER_WORD)]
    for at in range(0, people, chunk):
        total = None
        for j in range(PER_WORD):
            term = lax.dot_general(
                arranged[j], planes_refs[j][at:at + chunk, :], (((1,), (1,)), ((), ())),
                preferred_element_type=jnp.float32,
            )
            total = term if total is None else total + term
        out_ref[:, at:at + chunk] = total[:k] + total[k:] - offset


def sketch_partial(scaled, shifted, planes, chunk):
    return pl.pallas_call(
        functools.partial(sketch_kernel, chunk),
        out_shape=jax.ShapeDtypeStruct((scaled.shape[0], planes[0].shape[0]), jnp.float32),
        in_specs=[IN_VMEM] * (2 + len(planes)),
        out_specs=IN_VMEM,
        compiler_params=pltpu.CompilerParams(vmem_limit_bytes=VMEM_LIMIT),
        name="sketch",
    )(scaled, shifted, *planes)


def standard(rows, planes, freq):
    n_rows = rows.shape[0]
    row_sum = jnp.sum(rows, axis=1, keepdims=True)
    raw = dot32(jnp.concatenate(split2(rows), axis=0), planes)
    return (raw[:n_rows] + raw[n_rows:] - row_sum * (2.0 * freq)) * lax.rsqrt(2.0 * freq * (1.0 - freq))


def trait_kernel(direct, freq_ref, residual_ref, weight_ref, chosen_ref, *refs):
    planes_refs, outs = refs[:PER_WORD], refs[PER_WORD:-5]
    order_ref, chosen_freq_ref, gathered_ref, pick_ref, total = refs[-5:]
    people = gathered_ref.shape[0]
    markers, n_chosen = pick_ref.shape
    chosen = chosen_ref[...].reshape(1, n_chosen) - lax.axis_index("markers") * markers
    freq = jnp.broadcast_to(freq_ref[...].reshape(1, markers), (8, markers))
    freq = jnp.concatenate(split3(freq), axis=0)
    order = to_digit_order()
    chosen_freq = None
    for group in range(markers // GROUP):
        span = slice(group * GROUP, (group + 1) * GROUP)
        row = lax.broadcasted_iota(jnp.int32, (GROUP, 1), 0)
        natural = PER_WORD * jnp.bitwise_and(row, LANES - 1) + jnp.right_shift(row, 7) + group * GROUP
        pick = jnp.where(natural == chosen, 1.0, 0.0).astype(jnp.bfloat16)
        pick_ref[span, :] = pick
        moved = dot32(freq[:, span], order)
        order_ref[:, span] = moved[:8] + moved[8:16] + moved[16:]
        term = dot32(moved.astype(jnp.bfloat16), pick)
        chosen_freq = term if chosen_freq is None else chosen_freq + term
    chosen_freq = chosen_freq[:8] + chosen_freq[8:16] + chosen_freq[16:]
    chosen_freq_ref[...] = chosen_freq
    half = people // 2
    for at in range(0, people, half):
        rows = slice(at, at + half)
        planes = jnp.concatenate([
            ref[rows, group * LANES:(group + 1) * LANES]
            for group in range(markers // GROUP) for ref in planes_refs
        ], axis=1)
        gathered_ref[rows, :] = dot32(planes, pick_ref[...]).astype(jnp.bfloat16)
    rows = residual_ref[...].astype(jnp.float32) * weight_ref[...].reshape(1, -1)
    total[...] = standard(rows, gathered_ref[...], chosen_freq[0:1])
    width = n_chosen // len(outs)
    for slot, out in enumerate(outs):
        at = pl.multiple_of(group_of(slot, direct) * width, width)
        out[...] = total[:, pl.ds(at, width)]


def trait_scores(planes, freq, residuals, weight, chosen, direct):
    people, words = planes[0].shape
    markers = words * PER_WORD
    r = residuals.shape[0]
    groups = markers // GROUP
    n_chosen = chosen.shape[0]
    out = pl.pallas_call(
        functools.partial(trait_kernel, direct),
        out_shape=tuple(
            jax.ShapeDtypeStruct((r, n_chosen // groups), jnp.float32) for _ in range(groups)
        ) + (
            jax.ShapeDtypeStruct((8, markers), jnp.float32),
            jax.ShapeDtypeStruct((8, n_chosen), jnp.float32),
            jax.ShapeDtypeStruct((people, n_chosen), jnp.bfloat16),
        ),
        in_specs=[IN_VMEM] * (4 + len(planes)),
        out_specs=(IN_VMEM,) * (groups + 3),
        scratch_shapes=[
            pltpu.VMEM((markers, n_chosen), jnp.bfloat16),
            pltpu.VMEM((r, n_chosen), jnp.float32),
        ],
        compiler_params=pltpu.CompilerParams(vmem_limit_bytes=VMEM_LIMIT),
        cost_estimate=pl.CostEstimate(flops=2 * n_chosen * people * markers, bytes_accessed=2 * people * markers, transcendentals=0),
        name="traits",
    )(freq, residuals, weight, chosen, *planes)
    return out[:-3], out[-3], out[-2], out[-1]


def gram_of(sketch, residual):
    k = sketch.shape[0]
    parts = jnp.concatenate(split3(sketch), axis=0)
    raw = lax.dot_general(
        parts, jnp.concatenate([parts, residual], axis=0), (((1,), (1,)), ((), ())),
        preferred_element_type=jnp.float32,
    )
    block = [[raw[i * k:(i + 1) * k, j * k:(j + 1) * k] for j in range(3)] for i in range(3)]
    small = (block[0][2] + block[2][0]) + block[1][1]
    own = block[0][0] + ((block[0][1] + block[1][0]) + small)
    cross = raw[:k, 3 * k:] + (raw[k:2 * k, 3 * k:] + raw[2 * k:, 3 * k:])
    return jnp.concatenate([own, cross], axis=1)


def write_messages(direct, slots, outs, rows, order_ref, chosen_freq_ref, gathered_ref, planes_refs, trait_refs, gram):
    groups = order_ref.shape[1] // GROUP
    width = gathered_ref.shape[1] // groups
    k = rows.shape[0]
    for slot, out, traits in zip(slots, outs, trait_refs):
        group = group_of(slot, direct)
        words_at = pl.ds(pl.multiple_of(group * LANES, LANES), LANES)
        markers_at = pl.ds(pl.multiple_of(group * GROUP, GROUP), GROUP)
        scores_at = pl.ds(pl.multiple_of(group * width, width), width)
        planes = jnp.concatenate(
            [ref[:, words_at] for ref in planes_refs] + [gathered_ref[:, scores_at]], axis=1
        )
        freq = jnp.concatenate([order_ref[0:1, markers_at], chosen_freq_ref[0:1, scores_at]], axis=1)
        at = GROUP + width
        out[:, :at] = standard(rows, planes, freq)
        for first in range(0, traits.shape[0], k):
            out[:, at:at + width] = traits[first:first + k, :]
            at += width
        out[:, at:at + gram.shape[1]] = gram
        if at + gram.shape[1] < out.shape[1]:
            out[:, at + gram.shape[1]:] = jnp.zeros((k, out.shape[1] - at - gram.shape[1]), jnp.float32)


def far_kernel(direct, slots, first_ref, second_ref, residual_ref, weight_ref, order_ref, chosen_freq_ref, gathered_ref, *refs):
    planes_refs, refs = refs[:PER_WORD], refs[PER_WORD:]
    n = len(slots)
    trait_refs, outs, (sketch_ref, gram_ref) = refs[:n], refs[n:2 * n], refs[2 * n:]
    weight = weight_ref[...].reshape(1, -1)
    sketch = (first_ref[...] + second_ref[...]) * weight
    sketch_ref[...] = sketch
    gram = gram_of(sketch, residual_ref[...])
    gram_ref[...] = gram
    write_messages(
        direct, slots, outs, sketch * weight, order_ref, chosen_freq_ref, gathered_ref, planes_refs, trait_refs, gram
    )


def near_kernel(direct, slots, sketch_ref, gram_ref, weight_ref, order_ref, chosen_freq_ref, gathered_ref, *refs):
    planes_refs, refs = refs[:PER_WORD], refs[PER_WORD:]
    n = len(slots)
    write_messages(
        direct, slots, refs[n:], sketch_ref[...] * weight_ref[...].reshape(1, -1),
        order_ref, chosen_freq_ref, gathered_ref, planes_refs, refs[:n], gram_ref[...],
    )


def product_call(kernel, name, slots, inputs, common, planes, traits, more, direct):
    order, chosen_freq, gathered = common
    people, n_chosen = gathered.shape
    groups = order.shape[1] // GROUP
    k = inputs[0].shape[0]
    r, width = traits[0].shape
    gram_room = -(-(k + r) // LANES) * LANES
    message = jax.ShapeDtypeStruct((k, GROUP + width + r // k * width + gram_room), jnp.float32)
    operands = (*inputs, *common, *planes, *[traits[slot] for slot in slots])
    out_shape = (message,) * len(slots) + more
    columns = len(slots) * (GROUP + width)
    return pl.pallas_call(
        functools.partial(kernel, direct, slots),
        out_shape=out_shape,
        in_specs=[IN_VMEM] * len(operands),
        out_specs=(IN_VMEM,) * len(out_shape),
        compiler_params=pltpu.CompilerParams(vmem_limit_bytes=VMEM_LIMIT),
        cost_estimate=pl.CostEstimate(flops=4 * k * people * columns, bytes_accessed=2 * people * columns, transcendentals=0),
        name=name,
    )(*operands)


def products(first, second, residuals, weight, common, planes, traits, direct):
    k, people = first.shape
    gram = jax.ShapeDtypeStruct((k, k + residuals.shape[0]), jnp.float32)
    slots = tuple(range(len(traits)))
    near, far = slots[:2], slots[2:]
    out = product_call(
        far_kernel, "far", far, (first, second, residuals, weight), common, planes, traits,
        (jax.ShapeDtypeStruct((k, people), jnp.float32), gram), direct,
    )
    parts, sketch, gram = out[:-2], out[-2], out[-1]
    return [*product_call(
        near_kernel, "near", near, (sketch, gram, weight), common, planes, traits, (), direct
    ), *parts], sketch


def eliminate(system, k):
    row_at = lax.broadcasted_iota(jnp.int32, (k, 1), 0)
    shape = system.shape
    block = 8
    for start in range(0, k, block):
        columns = [
            jnp.broadcast_to(system[:, j:j + 1], shape) for j in range(start, start + block)
        ]
        for t in range(block):
            j = start + t
            inverse = lax.rsqrt(columns[t][j:j + 1, :])
            factor = columns[t] * inverse
            for s in range(t + 1, block):
                columns[s] = columns[s] - factor * factor[start + s:start + s + 1, :]
            scaled = system[j:j + 1, :] * inverse
            updated = system - factor * scaled
            system = jnp.where(row_at == j, scaled, jnp.where(row_at > j, updated, system))
    return system


def finish_kernel(root_people, k, r, width, score_width, digit_order, sketch_ref, *refs):
    parts, (components_ref, coefficients_ref, next_ref, out_ref) = refs[:-4], refs[-4:]
    row_at = lax.broadcasted_iota(jnp.int32, (k, k), 0)
    column_at = lax.broadcasted_iota(jnp.int32, (k, k), 1)
    identity = jnp.where(row_at == column_at, 1.0, 0.0)
    totals = [ref[...] for ref in parts]
    while len(totals) > 1:
        totals = [a + b for a, b in zip(totals[::2], totals[1::2])]
    total = totals[0]
    traits_at = width + score_width
    gram_at = traits_at + r // k * score_width
    system = eliminate(jnp.concatenate([total[:, gram_at:gram_at + k + r], identity], axis=1), k)
    coefficients = system[:, k:k + r]
    inverse = system[:, k + r:]
    coefficients_ref[...] = coefficients
    components_ref[...] = root_people * jnp.dot(
        inverse, sketch_ref[...], precision=HIGHEST, preferred_element_type=jnp.float32
    )
    solved = jnp.dot(
        inverse, total[:, :traits_at], precision=HIGHEST, preferred_element_type=jnp.float32
    )
    basis = solved[:, :width]
    if digit_order:
        both = dot32(jnp.concatenate(split2(basis), axis=0), to_natural_order())
        basis = both[:k] + both[k:]
    next_ref[...] = basis
    removed = lax.dot_general(
        coefficients, solved[:, width:], (((0,), (0,)), ((), ())),
        precision=HIGHEST, preferred_element_type=jnp.float32,
    )
    for i in range(r // k):
        at = traits_at + i * score_width
        out_ref[i * k:(i + 1) * k, :] = (
            total[:, at:at + score_width] - removed[i * k:(i + 1) * k]
        ) * (1.0 / root_people)


def finish(root_people, r, width, score_width, digit_order, sketch, parts):
    k = sketch.shape[0]
    return pl.pallas_call(
        functools.partial(finish_kernel, root_people, k, r, width, score_width, digit_order),
        out_shape=(
            jax.ShapeDtypeStruct(sketch.shape, jnp.float32),
            jax.ShapeDtypeStruct((k, r), jnp.float32),
            jax.ShapeDtypeStruct((k, width), jnp.float32),
            jax.ShapeDtypeStruct((r, score_width), jnp.float32),
        ),
        in_specs=[IN_VMEM] * (1 + len(parts)),
        out_specs=(IN_VMEM,) * 4,
        compiler_params=pltpu.CompilerParams(vmem_limit_bytes=VMEM_LIMIT),
        name="finish",
    )(sketch, *parts)


def shards(genotype, allele_freq, person_weight, basis, residuals, block_markers):
    people, words = genotype.shape
    markers = words * PER_WORD
    k, r = basis.shape[0], residuals.shape[0]
    marker_count = lax.axis_size("markers")
    people_count = lax.axis_size("people")
    groups = markers // GROUP
    direct = people_count == groups and groups == 4
    score_width = block_markers.shape[0] // people_count
    planes = digits(genotype)
    scaled = basis.astype(jnp.float32) * lax.rsqrt(2.0 * allele_freq * (1.0 - allele_freq))[None, :]
    shifted = scaled * (2.0 * allele_freq)[None, :]
    sketch = sketch_partial(scaled, shifted, planes, people // 4)
    apart = 1
    while apart * 2 < marker_count:
        sketch = sketch + from_partner(sketch, "markers", apart)
        apart *= 2
    other = from_partner(sketch, "markers", apart)
    traits, *common = trait_scores(
        planes, allele_freq, residuals, person_weight, block_markers, direct
    )
    parts, sketch = products(
        sketch, other, residuals, person_weight, common, planes, traits, direct
    )
    if direct:
        moved = {i: from_partner(parts[i], "people", i) for i in range(groups - 1, 0, -1)}
        parts = [moved[2], moved[3], moved[1], parts[0]]
    else:
        part_width = block_markers.shape[0] // groups
        whole = jnp.stack(parts, axis=1)
        value = whole[:, :, :GROUP].reshape(k, groups, PER_WORD, LANES)
        value = value.swapaxes(2, 3).reshape(k, markers)
        ends = [GROUP + i * part_width for i in range(r // k + 2)]
        scores = [whole[:, :, at:at + part_width].reshape(k, -1) for at in ends[:-1]]
        total = lax.psum((value, scores, parts[0][:, ends[-1]:]), "people")
        index = lax.axis_index("people")

        def own(array):
            width = array.shape[1] // people_count
            return lax.dynamic_slice_in_dim(array, index * width, width, 1)
        parts = [jnp.concatenate([own(total[0])] + [own(one) for one in total[1]] + [total[2]], axis=1)]
    components, coefficients, basis_own, score_own = finish(
        math.sqrt(people * people_count), r, markers // people_count, score_width, direct, sketch, parts
    )
    return components, coefficients, basis_own[None], score_own[None]


def solution(mesh):
    placed = (
        P(("cohort", "people"), "markers"),
        P(("cohort", "markers")),
        P(("cohort", "people")),
        P("cohort", "markers"),
        P("cohort", "people"),
        P("markers"),
    )
    return jax.shard_map(
        shards,
        mesh=mesh,
        in_specs=placed,
        out_specs=(
            P("cohort", "people"),
            P("cohort", None),
            P("markers", "cohort", "people"),
            P("markers", "cohort", "people"),
        ),
        check_vma=False,
    )
```

```python
import functools
import math

import jax
import jax.numpy as jnp
from jax import lax
from jax.experimental import pallas as pl
from jax.experimental.pallas import tpu as pltpu
from jax.sharding import PartitionSpec as P

LANES = 128
PER_WORD = 4
GROUP = LANES * PER_WORD
VMEM_LIMIT = 40 * 1024 * 1024
VMEM_SKETCH = 51 * 1024 * 1024
HIGHEST = lax.Precision.HIGHEST
IN_VMEM = pl.BlockSpec(memory_space=pltpu.VMEM)
IN_HBM = pl.BlockSpec(memory_space=pltpu.HBM)


def from_partner(block, axis, apart):
    count = lax.axis_size(axis)
    route = [(low, low ^ apart) for low in range(count)]
    return lax.ppermute(block, axis, route)


def split2(value):
    high = value.astype(jnp.bfloat16)
    low = (value - high.astype(jnp.float32)).astype(jnp.bfloat16)
    return high, low


def split3(value):
    high, rest = value.astype(jnp.bfloat16), None
    rest = value - high.astype(jnp.float32)
    middle, low = split2(rest)
    return high, middle, low


def digits(words):
    out = []
    for j in range(PER_WORD):
        one = words if j == 0 else jnp.right_shift(words, 2 * j)
        one = one if j == PER_WORD - 1 else jnp.bitwise_and(one, 3)
        out.append(one.astype(jnp.float32).astype(jnp.bfloat16))
    return out


def natural_of_column(shape):
    column = lax.broadcasted_iota(jnp.int32, shape, len(shape) - 1)
    return PER_WORD * jnp.bitwise_and(column, LANES - 1) + jnp.right_shift(column, 7)


def to_digit_order():
    row = lax.broadcasted_iota(jnp.int32, (GROUP, GROUP), 0)
    column = natural_of_column((1, GROUP))
    return jnp.where(row == column, 1.0, 0.0).astype(jnp.bfloat16)


def to_natural_order():
    row = lax.broadcasted_iota(jnp.int32, (GROUP, GROUP), 0)
    natural = PER_WORD * jnp.bitwise_and(row, LANES - 1) + jnp.right_shift(row, 7)
    column = lax.broadcasted_iota(jnp.int32, (GROUP, GROUP), 1)
    return jnp.where(natural == column, 1.0, 0.0).astype(jnp.bfloat16)


def dot32(a, b):
    return jnp.dot(a, b, preferred_element_type=jnp.float32)


def group_of(slot, direct):
    return jnp.bitwise_xor(lax.axis_index("people"), slot) if direct else slot


def sketch_kernel(cuts, words_ref, basis_ref, freq_ref, out_ref, half_ref, held, sems):
    copies = [
        pltpu.make_async_copy(
            words_ref.at[pl.ds(low, high - low), :], held.at[pl.ds(low, high - low), :], sems.at[i]
        )
        for i, (low, high) in enumerate(zip(cuts, cuts[1:]))
    ]
    for copy in copies:
        copy.start()
    k, markers = basis_ref.shape
    freq = freq_ref[...].reshape(1, markers)
    scaled = basis_ref[...].astype(jnp.float32) * lax.rsqrt(2.0 * freq * (1.0 - freq))
    offset = jnp.sum(scaled * (2.0 * freq), axis=1, keepdims=True)
    order = to_digit_order()
    stacked = jnp.concatenate(split2(scaled), axis=0)
    pieces = [[] for _ in range(PER_WORD)]
    for group in range(markers // GROUP):
        moved = dot32(stacked[:, group * GROUP:(group + 1) * GROUP], order).astype(jnp.bfloat16)
        for j in range(PER_WORD):
            pieces[j].append(moved[:, j * LANES:(j + 1) * LANES])
    arranged = jnp.concatenate([piece for one in pieces for piece in one], axis=1)
    for copy, low, high in zip(copies, cuts, cuts[1:]):
        copy.wait()
        words = held[low:high, :]
        half_ref[low:high, :] = words.astype(jnp.float32).astype(jnp.bfloat16)
        total = lax.dot_general(
            arranged, jnp.concatenate(digits(words), axis=1), (((1,), (1,)), ((), ())),
            preferred_element_type=jnp.float32,
        )
        out_ref[:, low:high] = total[:k] + total[k:] - offset


def sketch_partial(genotype, basis, freq):
    people = genotype.shape[0]
    cuts = (0, people // 3, people)
    return pl.pallas_call(
        functools.partial(sketch_kernel, cuts),
        out_shape=(
            jax.ShapeDtypeStruct((basis.shape[0], people), jnp.float32),
            jax.ShapeDtypeStruct(genotype.shape, jnp.bfloat16),
        ),
        in_specs=[IN_HBM, IN_VMEM, IN_VMEM],
        out_specs=(IN_VMEM,) * 2,
        scratch_shapes=[
            pltpu.VMEM(genotype.shape, genotype.dtype),
            pltpu.SemaphoreType.DMA((len(cuts) - 1,)),
        ],
        compiler_params=pltpu.CompilerParams(vmem_limit_bytes=VMEM_SKETCH),
        name="sketch",
    )(genotype, basis, freq)


def standard(rows, planes, freq):
    n_rows = rows.shape[0]
    row_sum = jnp.sum(rows, axis=1, keepdims=True)
    raw = dot32(jnp.concatenate(split2(rows), axis=0), planes)
    return (raw[:n_rows] + raw[n_rows:] - row_sum * (2.0 * freq)) * lax.rsqrt(2.0 * freq * (1.0 - freq))


def moved_freq(freq_ref, group, order):
    markers = freq_ref.shape[0]
    freq = jnp.broadcast_to(freq_ref[...].reshape(1, markers), (8, markers))
    return dot32(jnp.concatenate(split3(freq[:, group * GROUP:(group + 1) * GROUP]), axis=0), order)


def trait_kernel(direct, half_ref, freq_ref, residual_ref, weight_ref, chosen_ref, *refs):
    outs, (chosen_freq_ref, gathered_ref, total) = refs[:-3], refs[-3:]
    people, words = half_ref.shape
    markers, n_chosen = PER_WORD * words, gathered_ref.shape[1]
    chosen = chosen_ref[...].reshape(1, n_chosen) - lax.axis_index("markers") * markers
    digit = jnp.bitwise_and(chosen, PER_WORD - 1)
    row = lax.broadcasted_iota(jnp.int32, (words, 1), 0)
    pick = jnp.where(row == jnp.right_shift(chosen, 2), 1.0, 0.0).astype(jnp.bfloat16)
    word = dot32(half_ref[...], pick).astype(jnp.int32)
    word = jnp.bitwise_and(jnp.right_shift(word, 2 * digit), 3)
    gathered = word.astype(jnp.float32).astype(jnp.bfloat16)
    gathered_ref[...] = gathered
    order = to_digit_order()
    moved = [moved_freq(freq_ref, group, order) for group in range(markers // GROUP)]
    moved = jnp.concatenate([
        jnp.concatenate([one[:, j * LANES:(j + 1) * LANES] for one in moved], axis=1)
        for j in range(PER_WORD)
    ], axis=0)
    moved = dot32(moved.astype(jnp.bfloat16), pick)
    chosen_freq = jnp.zeros((8, n_chosen), jnp.float32)
    for j in range(PER_WORD):
        one = moved[24 * j:24 * (j + 1)]
        chosen_freq = jnp.where(digit == j, one[:8] + one[8:16] + one[16:], chosen_freq)
    chosen_freq_ref[...] = chosen_freq
    rows = residual_ref[...].astype(jnp.float32) * weight_ref[...].reshape(1, -1)
    total[...] = standard(rows, gathered, chosen_freq[0:1])
    width = n_chosen // 4 if direct else n_chosen

    def chunk(slot):
        at = pl.multiple_of(group_of(slot, direct) * width, width)
        return total[:, pl.ds(at, width)]
    if direct:
        sent, kept_own, kept_far = outs
        sent[:, :width] = chunk(1)
        sent[:, width:] = chunk(2)
        kept_own[...] = chunk(0)
        kept_far[...] = chunk(3)
    else:
        outs[0][...] = total[...]


def trait_scores(half, freq, residuals, weight, chosen, direct):
    people, words = half.shape
    r, n_chosen = residuals.shape[0], chosen.shape[0]
    width = n_chosen // 4
    widths = (2 * width, width, width) if direct else (n_chosen,)
    out = pl.pallas_call(
        functools.partial(trait_kernel, direct),
        out_shape=tuple(jax.ShapeDtypeStruct((r, one), jnp.float32) for one in widths) + (
            jax.ShapeDtypeStruct((8, n_chosen), jnp.float32),
            jax.ShapeDtypeStruct((people, n_chosen), jnp.bfloat16),
        ),
        in_specs=[IN_VMEM] * 5,
        out_specs=(IN_VMEM,) * (len(widths) + 2),
        scratch_shapes=[pltpu.VMEM((r, n_chosen), jnp.float32)],
        compiler_params=pltpu.CompilerParams(vmem_limit_bytes=VMEM_LIMIT),
        cost_estimate=pl.CostEstimate(flops=2 * n_chosen * people * (words + 2 * r), bytes_accessed=2 * people * (words + n_chosen), transcendentals=0),
        name="traits",
    )(half, freq, residuals, weight, chosen)
    return out[:-2], out[-2:]


def decode_kernel(half_ref, freq_ref, planes_ref, order_ref):
    order = to_digit_order()
    for group in range(order_ref.shape[1] // GROUP):
        span = slice(group * GROUP, (group + 1) * GROUP)
        word = half_ref[:, group * LANES:(group + 1) * LANES].astype(jnp.float32).astype(jnp.int32)
        planes_ref[:, span] = jnp.concatenate(digits(word), axis=1)
        moved = moved_freq(freq_ref, group, order)
        order_ref[:, span] = moved[:8] + moved[8:16] + moved[16:]


def decode(half, freq):
    people, words = half.shape
    markers = words * PER_WORD
    return pl.pallas_call(
        decode_kernel,
        out_shape=(
            jax.ShapeDtypeStruct((people, markers), jnp.bfloat16),
            jax.ShapeDtypeStruct((8, markers), jnp.float32),
        ),
        in_specs=[IN_VMEM] * 2,
        out_specs=(IN_VMEM,) * 2,
        compiler_params=pltpu.CompilerParams(vmem_limit_bytes=VMEM_LIMIT),
        cost_estimate=pl.CostEstimate(flops=people * markers * 16, bytes_accessed=4 * people * markers, transcendentals=0),
        name="decode",
    )(half, freq)


def gram_of(sketch, residual):
    k = sketch.shape[0]
    parts = jnp.concatenate(split3(sketch), axis=0)
    raw = lax.dot_general(
        parts, jnp.concatenate([parts, residual], axis=0), (((1,), (1,)), ((), ())),
        preferred_element_type=jnp.float32,
    )
    block = [[raw[i * k:(i + 1) * k, j * k:(j + 1) * k] for j in range(3)] for i in range(3)]
    small = (block[0][2] + block[2][0]) + block[1][1]
    own = block[0][0] + ((block[0][1] + block[1][0]) + small)
    cross = raw[:k, 3 * k:] + (raw[k:2 * k, 3 * k:] + raw[2 * k:, 3 * k:])
    return jnp.concatenate([own, cross], axis=1)


def write_messages(direct, slots, outs, rows, planes_ref, order_ref, chosen_freq_ref, gathered_ref, gram):
    groups = order_ref.shape[1] // GROUP
    width = gathered_ref.shape[1] // groups
    k = rows.shape[0]
    for slot, out in zip(slots, outs):
        group = group_of(slot, direct)
        markers_at = pl.ds(pl.multiple_of(group * GROUP, GROUP), GROUP)
        scores_at = pl.ds(pl.multiple_of(group * width, width), width)
        planes = jnp.concatenate([planes_ref[:, markers_at], gathered_ref[:, scores_at]], axis=1)
        freq = jnp.concatenate([order_ref[0:1, markers_at], chosen_freq_ref[0:1, scores_at]], axis=1)
        at = GROUP + width
        out[:, :at] = standard(rows, planes, freq)
        out[:, at:at + gram.shape[1]] = gram
        end = at + padded(gram.shape[1])
        if at + gram.shape[1] < end:
            out[:, at + gram.shape[1]:end] = jnp.zeros((k, end - at - gram.shape[1]), jnp.float32)


def write_traits(out, mine, other, k):
    r, width = mine.shape
    at = out.shape[1] - r // k * width
    for i in range(r // k):
        out[:, at + i * width:at + (i + 1) * width] = mine[i * k:(i + 1) * k] + other[i * k:(i + 1) * k]


def far_kernel(direct, first_ref, second_ref, residual_ref, weight_ref, planes_ref, order_ref, chosen_freq_ref, gathered_ref, *refs):
    trait_refs, (out_a, out_b, sketch_ref, gram_ref) = refs[:-4], refs[-4:]
    weight = weight_ref[...].reshape(1, -1)
    sketch = (first_ref[...] + second_ref[...]) * weight
    sketch_ref[...] = sketch
    gram = gram_of(sketch, residual_ref[...])
    gram_ref[...] = gram
    write_messages(
        direct, (2, 3), (out_a, out_b), sketch * weight, planes_ref, order_ref, chosen_freq_ref, gathered_ref, gram
    )
    if direct:
        width = trait_refs[0].shape[1]
        write_traits(out_b, trait_refs[0][...], trait_refs[1][:, width:], sketch.shape[0])


def near_kernel(direct, sketch_ref, gram_ref, weight_ref, planes_ref, order_ref, chosen_freq_ref, gathered_ref, *refs):
    trait_refs, (out_a, out_b) = refs[:-2], refs[-2:]
    write_messages(
        direct, (0, 1), (out_a, out_b), sketch_ref[...] * weight_ref[...].reshape(1, -1),
        planes_ref, order_ref, chosen_freq_ref, gathered_ref, gram_ref[...],
    )
    if direct:
        width = trait_refs[0].shape[1]
        write_traits(out_a, trait_refs[0][...], trait_refs[1][:, :width], sketch_ref.shape[0])


def padded(width):
    return -(-width // LANES) * LANES


def product_call(kernel, name, inputs, common, traits, widths, more, direct):
    _, order, _, gathered = common
    people = gathered.shape[0]
    k = inputs[0].shape[0]
    operands = (*inputs, *common, *traits)
    out_shape = tuple(jax.ShapeDtypeStruct((k, width), jnp.float32) for width in widths) + more
    return pl.pallas_call(
        functools.partial(kernel, direct),
        out_shape=out_shape,
        in_specs=[IN_VMEM] * len(operands),
        out_specs=(IN_VMEM,) * len(out_shape),
        compiler_params=pltpu.CompilerParams(vmem_limit_bytes=VMEM_LIMIT),
        cost_estimate=pl.CostEstimate(flops=4 * k * people * sum(widths), bytes_accessed=2 * people * sum(widths), transcendentals=0),
        name=name,
    )(*operands)


def products(first, second, residuals, weight, common, traits, swapped, direct):
    k, people = first.shape
    r = traits[0].shape[0]
    width = common[-1].shape[1] // 4
    plain = GROUP + width + padded(k + r)
    longer = plain + (r // k * width if direct else 0)
    out_a, out_b, sketch, gram = product_call(
        far_kernel, "far", (first, second, residuals, weight), common,
        (traits[2], swapped) if direct else (), (plain, longer),
        (jax.ShapeDtypeStruct((k, people), jnp.float32), jax.ShapeDtypeStruct((k, k + r), jnp.float32)), direct,
    )
    own, near = product_call(
        near_kernel, "near", (sketch, gram, weight), common,
        (traits[1], swapped) if direct else (), (longer, plain), (), direct,
    )
    return [own, near, out_a, out_b], sketch


def eliminate(system, k):
    row_at = lax.broadcasted_iota(jnp.int32, (k, 1), 0)
    shape = system.shape
    block = 8
    for start in range(0, k, block):
        columns = [
            jnp.broadcast_to(system[:, j:j + 1], shape) for j in range(start, start + block)
        ]
        for t in range(block):
            j = start + t
            inverse = lax.rsqrt(columns[t][j:j + 1, :])
            factor = columns[t] * inverse
            for s in range(t + 1, block):
                columns[s] = columns[s] - factor * factor[start + s:start + s + 1, :]
            scaled = system[j:j + 1, :] * inverse
            updated = system - factor * scaled
            system = jnp.where(row_at == j, scaled, jnp.where(row_at > j, updated, system))
    return system


def finish_kernel(root_people, k, r, width, score_width, digit_order, sketch_ref, tail_ref, *refs):
    parts, (components_ref, coefficients_ref, next_ref, out_ref) = refs[:-4], refs[-4:]
    row_at = lax.broadcasted_iota(jnp.int32, (k, k), 0)
    column_at = lax.broadcasted_iota(jnp.int32, (k, k), 1)
    identity = jnp.where(row_at == column_at, 1.0, 0.0)
    gram_at = width + score_width
    trait_at = gram_at + padded(k + r)
    total = parts[0][:, :trait_at]
    traits = parts[0][:, trait_at:]
    for ref in parts[1:]:
        total = total + ref[...]
    if len(parts) > 1:
        traits = traits + tail_ref[:, trait_at:]
    system = eliminate(jnp.concatenate([total[:, gram_at:gram_at + k + r], identity], axis=1), k)
    coefficients = system[:, k:k + r]
    inverse = system[:, k + r:]
    coefficients_ref[...] = coefficients
    components_ref[...] = root_people * jnp.dot(
        inverse, sketch_ref[...], precision=HIGHEST, preferred_element_type=jnp.float32
    )
    solved = jnp.dot(
        inverse, total[:, :gram_at], precision=HIGHEST, preferred_element_type=jnp.float32
    )
    basis = solved[:, :width]
    if digit_order:
        both = dot32(jnp.concatenate(split2(basis), axis=0), to_natural_order())
        basis = both[:k] + both[k:]
    next_ref[...] = basis
    removed = lax.dot_general(
        coefficients, solved[:, width:], (((0,), (0,)), ((), ())),
        precision=HIGHEST, preferred_element_type=jnp.float32,
    )
    for i in range(r // k):
        out_ref[i * k:(i + 1) * k, :] = (
            traits[:, i * score_width:(i + 1) * score_width] - removed[i * k:(i + 1) * k]
        ) * (1.0 / root_people)


def finish(root_people, r, width, score_width, digit_order, sketch, tail, parts):
    k = sketch.shape[0]
    return pl.pallas_call(
        functools.partial(finish_kernel, root_people, k, r, width, score_width, digit_order),
        out_shape=(
            jax.ShapeDtypeStruct(sketch.shape, jnp.float32),
            jax.ShapeDtypeStruct((k, r), jnp.float32),
            jax.ShapeDtypeStruct((k, width), jnp.float32),
            jax.ShapeDtypeStruct((r, score_width), jnp.float32),
        ),
        in_specs=[IN_VMEM] * (2 + len(parts)),
        out_specs=(IN_VMEM,) * 4,
        compiler_params=pltpu.CompilerParams(vmem_limit_bytes=VMEM_LIMIT),
        name="finish",
    )(sketch, tail, *parts)


def shards(genotype, allele_freq, person_weight, basis, residuals, block_markers):
    people, words = genotype.shape
    markers = words * PER_WORD
    k, r = basis.shape[0], residuals.shape[0]
    marker_count = lax.axis_size("markers")
    people_count = lax.axis_size("people")
    groups = markers // GROUP
    direct = people_count == groups and groups == 4
    score_width = block_markers.shape[0] // people_count
    sketch, half = sketch_partial(genotype, basis, allele_freq)
    apart = 1
    while apart * 2 < marker_count:
        sketch = sketch + from_partner(sketch, "markers", apart)
        apart *= 2
    other = from_partner(sketch, "markers", apart)
    traits, (chosen_freq, gathered) = trait_scores(
        half, allele_freq, residuals, person_weight, block_markers, direct
    )
    swapped = from_partner(traits[0], "people", 1) if direct else None
    planes, order = decode(half, allele_freq)
    parts, sketch = products(
        sketch, other, residuals, person_weight, (planes, order, chosen_freq, gathered), traits, swapped, direct
    )
    if direct:
        near, far, tail = [from_partner(parts[i], "people", i) for i in range(1, groups)]
        parts = [parts[0], near, far + tail[:, :far.shape[1]]]
    else:
        whole = jnp.stack(parts, axis=1)
        part_width = block_markers.shape[0] // groups
        value = whole[:, :, :GROUP].reshape(k, groups, PER_WORD, LANES)
        value = value.swapaxes(2, 3).reshape(k, markers)
        projected = whole[:, :, GROUP:GROUP + part_width].reshape(k, -1)
        gram = parts[0][:, GROUP + part_width:]
        value, projected, traits, gram = lax.psum((value, projected, traits[0], gram), "people")
        index = lax.axis_index("people")

        def own(array):
            width = array.shape[1] // people_count
            return lax.dynamic_slice_in_dim(array, index * width, width, 1)
        traits = own(traits)
        tail = jnp.concatenate(
            [own(value), own(projected), gram] + [traits[i * k:(i + 1) * k] for i in range(r // k)], axis=1
        )
        parts = [tail]
    components, coefficients, basis_own, score_own = finish(
        math.sqrt(people * people_count), r, markers // people_count, score_width, direct, sketch, tail, parts
    )
    return components, coefficients, basis_own[None], score_own[None]


def solution(mesh):
    placed = (
        P(("cohort", "people"), "markers"),
        P(("cohort", "markers")),
        P(("cohort", "people")),
        P("cohort", "markers"),
        P("cohort", "people"),
        P("markers"),
    )
    return jax.shard_map(
        shards,
        mesh=mesh,
        in_specs=placed,
        out_specs=(
            P("cohort", "people"),
            P("cohort", None),
            P("markers", "cohort", "people"),
            P("markers", "cohort", "people"),
        ),
        check_vma=False,
    )
```

```python
import functools
import math

import jax
import jax.numpy as jnp
from jax import lax
from jax.experimental import pallas as pl
from jax.experimental.pallas import tpu as pltpu
from jax.sharding import PartitionSpec as P

LANES = 128
PER_WORD = 4
GROUP = LANES * PER_WORD
CUT = 128
VMEM_LIMIT = 40 * 1024 * 1024
VMEM_SKETCH = 51 * 1024 * 1024
HIGHEST = lax.Precision.HIGHEST
IN_VMEM = pl.BlockSpec(memory_space=pltpu.VMEM)
IN_HBM = pl.BlockSpec(memory_space=pltpu.HBM)


def from_partner(block, axis, apart):
    count = lax.axis_size(axis)
    route = [(low, low ^ apart) for low in range(count)]
    return lax.ppermute(block, axis, route)


def split2(value):
    high = value.astype(jnp.bfloat16)
    low = (value - high.astype(jnp.float32)).astype(jnp.bfloat16)
    return high, low


def split3(value):
    high, rest = value.astype(jnp.bfloat16), None
    rest = value - high.astype(jnp.float32)
    middle, low = split2(rest)
    return high, middle, low


def digits(words):
    out = []
    for j in range(PER_WORD):
        one = words if j == 0 else jnp.right_shift(words, 2 * j)
        one = one if j == PER_WORD - 1 else jnp.bitwise_and(one, 3)
        out.append(one.astype(jnp.float32).astype(jnp.bfloat16))
    return out


def natural_of_column(shape):
    column = lax.broadcasted_iota(jnp.int32, shape, len(shape) - 1)
    return PER_WORD * jnp.bitwise_and(column, LANES - 1) + jnp.right_shift(column, 7)


def to_digit_order():
    row = lax.broadcasted_iota(jnp.int32, (GROUP, GROUP), 0)
    column = natural_of_column((1, GROUP))
    return jnp.where(row == column, 1.0, 0.0).astype(jnp.bfloat16)


def to_natural_order():
    row = lax.broadcasted_iota(jnp.int32, (GROUP, GROUP), 0)
    natural = PER_WORD * jnp.bitwise_and(row, LANES - 1) + jnp.right_shift(row, 7)
    column = lax.broadcasted_iota(jnp.int32, (GROUP, GROUP), 1)
    return jnp.where(natural == column, 1.0, 0.0).astype(jnp.bfloat16)


def dot32(a, b):
    return jnp.dot(a, b, preferred_element_type=jnp.float32)


def group_of(slot, direct):
    return jnp.bitwise_xor(lax.axis_index("people"), slot) if direct else slot


def load_kernel(words_ref, half_ref, held, sems):
    parts = sems.shape[0]
    rows = held.shape[0] // parts
    copies = []
    for part in range(parts):
        at = pl.ds(part * rows, rows)
        copies.append(pltpu.make_async_copy(words_ref.at[at, :], held.at[at, :], sems.at[part]))
        copies[-1].start()
    for part, copy in enumerate(copies):
        copy.wait()
        at = slice(part * rows, (part + 1) * rows)
        half_ref[at, :] = held[at, :].astype(jnp.float32).astype(jnp.bfloat16)


def load_words(genotype):
    parts = 3
    return pl.pallas_call(
        load_kernel,
        out_shape=jax.ShapeDtypeStruct(genotype.shape, jnp.bfloat16),
        in_specs=[IN_HBM],
        out_specs=IN_VMEM,
        scratch_shapes=[pltpu.VMEM(genotype.shape, genotype.dtype), pltpu.SemaphoreType.DMA((parts,))],
        compiler_params=pltpu.CompilerParams(vmem_limit_bytes=VMEM_SKETCH),
        cost_estimate=pl.CostEstimate(flops=0, bytes_accessed=6 * genotype.size, transcendentals=0),
        name="load",
    )(genotype)


def sketch_kernel(half_ref, basis_ref, freq_ref, out_ref):
    k, markers = basis_ref.shape
    freq = freq_ref[...].reshape(1, markers)
    scaled = basis_ref[...].astype(jnp.float32) * lax.rsqrt(2.0 * freq * (1.0 - freq))
    offset = jnp.sum(scaled * (2.0 * freq), axis=1, keepdims=True)
    order = to_digit_order()
    stacked = jnp.concatenate(split2(scaled), axis=0)
    pieces = [[] for _ in range(PER_WORD)]
    for group in range(markers // GROUP):
        moved = dot32(stacked[:, group * GROUP:(group + 1) * GROUP], order).astype(jnp.bfloat16)
        for j in range(PER_WORD):
            pieces[j].append(moved[:, j * LANES:(j + 1) * LANES])
    arranged = jnp.concatenate([piece for one in pieces for piece in one], axis=1)
    words = half_ref[...].astype(jnp.float32).astype(jnp.int32)
    total = lax.dot_general(
        arranged, jnp.concatenate(digits(words), axis=1), (((1,), (1,)), ((), ())),
        preferred_element_type=jnp.float32,
    )
    out_ref[...] = total[:k] + total[k:] - offset


def sketch_partial(half, basis, freq):
    return pl.pallas_call(
        sketch_kernel,
        out_shape=jax.ShapeDtypeStruct((basis.shape[0], half.shape[0]), jnp.float32),
        in_specs=[IN_VMEM] * 3,
        out_specs=IN_VMEM,
        compiler_params=pltpu.CompilerParams(vmem_limit_bytes=VMEM_LIMIT),
        name="sketch",
    )(half, basis, freq)


def standard(rows, planes, freq):
    n_rows = rows.shape[0]
    row_sum = jnp.sum(rows, axis=1, keepdims=True)
    raw = dot32(jnp.concatenate(split2(rows), axis=0), planes)
    return (raw[:n_rows] + raw[n_rows:] - row_sum * (2.0 * freq)) * lax.rsqrt(2.0 * freq * (1.0 - freq))


def moved_freq(freq_ref, group, order):
    markers = freq_ref.shape[0]
    freq = jnp.broadcast_to(freq_ref[...].reshape(1, markers), (8, markers))
    return dot32(jnp.concatenate(split3(freq[:, group * GROUP:(group + 1) * GROUP]), axis=0), order)


def trait_kernel(direct, half_ref, freq_ref, residual_ref, weight_ref, chosen_ref, *refs):
    outs, (chosen_freq_ref, gathered_ref, total) = refs[:-3], refs[-3:]
    people, words = half_ref.shape
    markers, n_chosen = PER_WORD * words, gathered_ref.shape[1]
    chosen = chosen_ref[...].reshape(1, n_chosen) - lax.axis_index("markers") * markers
    digit = jnp.bitwise_and(chosen, PER_WORD - 1)
    row = lax.broadcasted_iota(jnp.int32, (words, 1), 0)
    pick = jnp.where(row == jnp.right_shift(chosen, 2), 1.0, 0.0).astype(jnp.bfloat16)
    word = dot32(half_ref[...], pick).astype(jnp.int32)
    word = jnp.bitwise_and(jnp.right_shift(word, 2 * digit), 3)
    gathered = word.astype(jnp.float32).astype(jnp.bfloat16)
    gathered_ref[...] = gathered
    order = to_digit_order()
    moved = [moved_freq(freq_ref, group, order) for group in range(markers // GROUP)]
    moved = jnp.concatenate([
        jnp.concatenate([one[:, j * LANES:(j + 1) * LANES] for one in moved], axis=1)
        for j in range(PER_WORD)
    ], axis=0)
    moved = dot32(moved.astype(jnp.bfloat16), pick)
    chosen_freq = jnp.zeros((8, n_chosen), jnp.float32)
    for j in range(PER_WORD):
        one = moved[24 * j:24 * (j + 1)]
        chosen_freq = jnp.where(digit == j, one[:8] + one[8:16] + one[16:], chosen_freq)
    chosen_freq_ref[...] = chosen_freq
    rows = residual_ref[...].astype(jnp.float32) * weight_ref[...].reshape(1, -1)
    total[...] = standard(rows, gathered, chosen_freq[0:1])
    width = n_chosen // 4 if direct else n_chosen

    def chunk(slot):
        at = pl.multiple_of(group_of(slot, direct) * width, width)
        return total[:, pl.ds(at, width)]
    if direct:
        sent, kept_own, kept_far = outs
        sent[:, :width] = chunk(1)
        sent[:, width:] = chunk(2)
        kept_own[...] = chunk(0)
        kept_far[...] = chunk(3)
    else:
        outs[0][...] = total[...]


def trait_scores(half, freq, residuals, weight, chosen, direct):
    people, words = half.shape
    r, n_chosen = residuals.shape[0], chosen.shape[0]
    width = n_chosen // 4
    widths = (2 * width, width, width) if direct else (n_chosen,)
    out = pl.pallas_call(
        functools.partial(trait_kernel, direct),
        out_shape=tuple(jax.ShapeDtypeStruct((r, one), jnp.float32) for one in widths) + (
            jax.ShapeDtypeStruct((8, n_chosen), jnp.float32),
            jax.ShapeDtypeStruct((people, n_chosen), jnp.bfloat16),
        ),
        in_specs=[IN_VMEM] * 5,
        out_specs=(IN_VMEM,) * (len(widths) + 2),
        scratch_shapes=[pltpu.VMEM((r, n_chosen), jnp.float32)],
        compiler_params=pltpu.CompilerParams(vmem_limit_bytes=VMEM_LIMIT),
        cost_estimate=pl.CostEstimate(flops=2 * n_chosen * people * (words + 2 * r), bytes_accessed=2 * people * (words + n_chosen), transcendentals=0),
        name="traits",
    )(half, freq, residuals, weight, chosen)
    return out[:-2], out[-2:]


def decode_kernel(half_ref, freq_ref, planes_ref, order_ref):
    order = to_digit_order()
    for group in range(order_ref.shape[1] // GROUP):
        span = slice(group * GROUP, (group + 1) * GROUP)
        word = half_ref[:, group * LANES:(group + 1) * LANES].astype(jnp.float32).astype(jnp.int32)
        planes_ref[:, span] = jnp.concatenate(digits(word), axis=1)
        moved = moved_freq(freq_ref, group, order)
        order_ref[:, span] = moved[:8] + moved[8:16] + moved[16:]


def decode(half, freq):
    people, words = half.shape
    markers = words * PER_WORD
    return pl.pallas_call(
        decode_kernel,
        out_shape=(
            jax.ShapeDtypeStruct((people, markers), jnp.bfloat16),
            jax.ShapeDtypeStruct((8, markers), jnp.float32),
        ),
        in_specs=[IN_VMEM] * 2,
        out_specs=(IN_VMEM,) * 2,
        compiler_params=pltpu.CompilerParams(vmem_limit_bytes=VMEM_LIMIT),
        cost_estimate=pl.CostEstimate(flops=people * markers * 16, bytes_accessed=4 * people * markers, transcendentals=0),
        name="decode",
    )(half, freq)


def gram_of(sketch, residual):
    k = sketch.shape[0]
    parts = jnp.concatenate(split3(sketch), axis=0)
    raw = lax.dot_general(
        parts, jnp.concatenate([parts, residual], axis=0), (((1,), (1,)), ((), ())),
        preferred_element_type=jnp.float32,
    )
    block = [[raw[i * k:(i + 1) * k, j * k:(j + 1) * k] for j in range(3)] for i in range(3)]
    small = (block[0][2] + block[2][0]) + block[1][1]
    own = block[0][0] + ((block[0][1] + block[1][0]) + small)
    cross = raw[:k, 3 * k:] + (raw[k:2 * k, 3 * k:] + raw[2 * k:, 3 * k:])
    return jnp.concatenate([own, cross], axis=1)


def padded(width):
    return -(-width // LANES) * LANES


def chunk_of(slot, direct, rows, planes_ref, order_ref, chosen_freq_ref, gathered_ref):
    width = gathered_ref.shape[1] // (order_ref.shape[1] // GROUP)
    group = group_of(slot, direct)
    markers_at = pl.ds(pl.multiple_of(group * GROUP, GROUP), GROUP)
    scores_at = pl.ds(pl.multiple_of(group * width, width), width)
    planes = jnp.concatenate([planes_ref[:, markers_at], gathered_ref[:, scores_at]], axis=1)
    freq = jnp.concatenate([order_ref[0:1, markers_at], chosen_freq_ref[0:1, scores_at]], axis=1)
    return standard(rows, planes, freq)


def far_kernel(direct, first_ref, second_ref, residual_ref, weight_ref, *refs):
    common, refs = refs[:4], refs[4:]
    trait_refs, refs = (refs[:2], refs[2:]) if direct else ((), refs)
    relay_ref, straight_ref, kept_ref, across_ref, sketch_ref, gram_ref = refs[:6]
    weight = weight_ref[...].reshape(1, -1)
    sketch = (first_ref[...] + second_ref[...]) * weight
    sketch_ref[...] = sketch
    gram = gram_of(sketch, residual_ref[...])
    k, room = gram.shape[0], gram_ref.shape[1] - gram.shape[1]
    if room:
        gram = jnp.concatenate([gram, jnp.zeros((k, room), jnp.float32)], axis=1)
    gram_ref[...] = gram
    cut = relay_ref.shape[1] - gram.shape[1]
    rows = sketch * weight
    for slot, low_ref, high_ref in ((2, relay_ref, straight_ref), (3, kept_ref, across_ref)):
        chunk = chunk_of(slot, direct, rows, *common)
        low_ref[:, :cut] = chunk[:, :cut]
        low_ref[:, cut:] = gram
        high_ref[...] = chunk[:, cut:]
    if direct:
        add_pairs(refs[6], *trait_refs)


def add_pairs(out, mine, other):
    k, (r, width) = out.shape[0], mine.shape
    pair = mine[...] + other[:, width:]
    for i in range(r // k):
        out[:, i * width:(i + 1) * width] = pair[i * k:(i + 1) * k]


def chunk_kernel(direct, slots, sketch_ref, weight_ref, gram_ref, *refs):
    common, outs = refs[:4], refs[4:]
    rows = sketch_ref[...] * weight_ref[...].reshape(1, -1)
    for slot, out in zip(slots, outs):
        chunk = chunk_of(slot, direct, rows, *common)
        out[:, :chunk.shape[1]] = chunk
        out[:, chunk.shape[1]:] = gram_ref[...]


def product_call(kernel, name, inputs, common, widths, people):
    k = inputs[0].shape[0]
    operands = (*inputs, *common)
    return pl.pallas_call(
        kernel,
        out_shape=tuple(jax.ShapeDtypeStruct((k, width), jnp.float32) for width in widths),
        in_specs=[IN_VMEM] * len(operands),
        out_specs=(IN_VMEM,) * len(widths),
        compiler_params=pltpu.CompilerParams(vmem_limit_bytes=VMEM_LIMIT),
        cost_estimate=pl.CostEstimate(flops=4 * k * people * sum(widths), bytes_accessed=2 * people * sum(widths), transcendentals=0),
        name=name,
    )(*operands)


def eliminate(system, k):
    row_at = lax.broadcasted_iota(jnp.int32, (k, 1), 0)
    shape = system.shape
    block = 8
    for start in range(0, k, block):
        columns = [
            jnp.broadcast_to(system[:, j:j + 1], shape) for j in range(start, start + block)
        ]
        for t in range(block):
            j = start + t
            inverse = lax.rsqrt(columns[t][j:j + 1, :])
            factor = columns[t] * inverse
            for s in range(t + 1, block):
                columns[s] = columns[s] - factor * factor[start + s:start + s + 1, :]
            scaled = system[j:j + 1, :] * inverse
            updated = system - factor * scaled
            system = jnp.where(row_at == j, scaled, jnp.where(row_at > j, updated, system))
    return system


def finish_kernel(root_people, r, width, digit_order, sketch_ref, own_ref, kept_ref, *refs):
    more, (components_ref, coefficients_ref, next_ref, out_ref) = refs[:-4], refs[-4:]
    k = sketch_ref.shape[0]
    score_width = out_ref.shape[1]
    total = own_ref[...]
    traits = [kept_ref[i * k:(i + 1) * k, :] for i in range(r // k)]
    gram_at = width + score_width
    if more:
        swapped_ref, near_ref, relayed_ref, straight_ref, across_ref = more
        total = total + near_ref[...]
        cut = gram_at - straight_ref.shape[1]
        at = cut + total.shape[1] - gram_at
        total = jnp.concatenate([
            total[:, :cut] + relayed_ref[:, :cut],
            total[:, cut:gram_at] + (straight_ref[...] + across_ref[...]),
            total[:, gram_at:] + relayed_ref[:, cut:at],
        ], axis=1)
        traits = [
            one + swapped_ref[i * k:(i + 1) * k, :score_width]
            + relayed_ref[:, at + i * score_width:at + (i + 1) * score_width]
            for i, one in enumerate(traits)
        ]
    row_at = lax.broadcasted_iota(jnp.int32, (k, k), 0)
    column_at = lax.broadcasted_iota(jnp.int32, (k, k), 1)
    identity = jnp.where(row_at == column_at, 1.0, 0.0)
    system = eliminate(jnp.concatenate([total[:, gram_at:gram_at + k + r], identity], axis=1), k)
    coefficients = system[:, k:k + r]
    inverse = system[:, k + r:]
    coefficients_ref[...] = coefficients
    components_ref[...] = root_people * jnp.dot(
        inverse, sketch_ref[...], precision=HIGHEST, preferred_element_type=jnp.float32
    )
    solved = jnp.dot(inverse, total[:, :gram_at], precision=HIGHEST, preferred_element_type=jnp.float32)
    basis = solved[:, :width]
    if digit_order:
        both = dot32(jnp.concatenate(split2(basis), axis=0), to_natural_order())
        basis = both[:k] + both[k:]
    next_ref[...] = basis
    removed = lax.dot_general(
        coefficients, solved[:, width:], (((0,), (0,)), ((), ())),
        precision=HIGHEST, preferred_element_type=jnp.float32,
    )
    for i, one in enumerate(traits):
        out_ref[i * k:(i + 1) * k, :] = (one - removed[i * k:(i + 1) * k]) * (1.0 / root_people)


def finish(root_people, width, digit_order, sketch, own, kept, more):
    k = sketch.shape[0]
    r = kept.shape[0]
    return pl.pallas_call(
        functools.partial(finish_kernel, root_people, r, width, digit_order),
        out_shape=(
            jax.ShapeDtypeStruct(sketch.shape, jnp.float32),
            jax.ShapeDtypeStruct((k, r), jnp.float32),
            jax.ShapeDtypeStruct((k, width), jnp.float32),
            jax.ShapeDtypeStruct(kept.shape, jnp.float32),
        ),
        in_specs=[IN_VMEM] * (3 + len(more)),
        out_specs=(IN_VMEM,) * 4,
        compiler_params=pltpu.CompilerParams(vmem_limit_bytes=VMEM_LIMIT),
        name="finish",
    )(sketch, own, kept, *more)


def shards(genotype, allele_freq, person_weight, basis, residuals, block_markers):
    people, words = genotype.shape
    markers = words * PER_WORD
    k, r = basis.shape[0], residuals.shape[0]
    marker_count = lax.axis_size("markers")
    people_count = lax.axis_size("people")
    groups = markers // GROUP
    direct = people_count == groups and groups == 4
    half = load_words(genotype)
    sketch = sketch_partial(half, basis, allele_freq)
    apart = 1
    while apart * 2 < marker_count:
        sketch = sketch + from_partner(sketch, "markers", apart)
        apart *= 2
    other = from_partner(sketch, "markers", apart)
    traits, (chosen_freq, gathered) = trait_scores(
        half, allele_freq, residuals, person_weight, block_markers, direct
    )
    swapped = from_partner(traits[0], "people", 1) if direct else None
    planes, order = decode(half, allele_freq)
    common = planes, order, chosen_freq, gathered
    width = GROUP + gathered.shape[1] // groups
    room = padded(k + r)
    relay, straight, kept, across, sketch, gram, *pair = product_call(
        functools.partial(far_kernel, direct), "far", (sketch, other, residuals, person_weight),
        common + ((traits[2], swapped) if direct else ()),
        (CUT + room, width - CUT, CUT + room, width - CUT, people, room) + ((r // k * (width - GROUP),) if direct else ()),
        people,
    )

    def chunks(name, *slots):
        return product_call(
            functools.partial(chunk_kernel, direct, slots), name, (sketch, person_weight, gram), common,
            (width + room,) * len(slots), people,
        )
    if direct:
        relay = from_partner(relay, "people", 1)
        straight = from_partner(straight, "people", 2)
        across = from_partner(across, "people", 3)
        near, = chunks("near", 1)
        near = from_partner(near, "people", 1)
        relayed = jnp.concatenate([kept + relay] + pair, axis=1)
        relayed = from_partner(relayed, "people", 3)
        own, = chunks("own", 0)
        kept, more = traits[1], (swapped, near, relayed, straight, across)
    else:
        first, second = chunks("near", 0, 1)
        gram = lax.psum(gram, "people")
        whole = jnp.stack([
            first[:, :width], second[:, :width], jnp.concatenate([relay[:, :CUT], straight], axis=1),
            jnp.concatenate([kept[:, :CUT], across], axis=1),
        ], axis=1)
        value = whole[:, :, :GROUP].reshape(k, groups, PER_WORD, LANES)
        value = value.swapaxes(2, 3).reshape(k, markers)
        projected = whole[:, :, GROUP:].reshape(k, -1)
        value, projected, kept = lax.psum((value, projected, traits[0]), "people")
        index = lax.axis_index("people")

        def own_part(array):
            part = array.shape[1] // people_count
            return lax.dynamic_slice_in_dim(array, index * part, part, 1)
        own = jnp.concatenate([own_part(value), own_part(projected), gram], axis=1)
        kept, more = own_part(kept), ()
    components, coefficients, basis_own, score_own = finish(
        math.sqrt(people * people_count), markers // people_count, direct, sketch, own, kept, more
    )
    return components, coefficients, basis_own[None], score_own[None]


def solution(mesh):
    placed = (
        P(("cohort", "people"), "markers"),
        P(("cohort", "markers")),
        P(("cohort", "people")),
        P("cohort", "markers"),
        P("cohort", "people"),
        P("markers"),
    )
    return jax.shard_map(
        shards,
        mesh=mesh,
        in_specs=placed,
        out_specs=(
            P("cohort", "people"),
            P("cohort", None),
            P("markers", "cohort", "people"),
            P("markers", "cohort", "people"),
        ),
        check_vma=False,
    )
```

```python
import functools
import math

import jax
import jax.numpy as jnp
from jax import lax
from jax.experimental import pallas as pl
from jax.experimental.pallas import tpu as pltpu
from jax.sharding import PartitionSpec as P

LANES = 128
PER_WORD = 4
GROUP = LANES * PER_WORD
CUT = 128
FAR, ACROSS = 3, 2
VMEM_LIMIT = 40 * 1024 * 1024
VMEM_SKETCH = 51 * 1024 * 1024
HIGHEST = lax.Precision.HIGHEST
IN_VMEM = pl.BlockSpec(memory_space=pltpu.VMEM)
IN_HBM = pl.BlockSpec(memory_space=pltpu.HBM)


def from_partner(block, axis, apart):
    count = lax.axis_size(axis)
    route = [(low, low ^ apart) for low in range(count)]
    return lax.ppermute(block, axis, route)


def split2(value):
    high = value.astype(jnp.bfloat16)
    low = (value - high.astype(jnp.float32)).astype(jnp.bfloat16)
    return high, low


def split3(value):
    high, rest = value.astype(jnp.bfloat16), None
    rest = value - high.astype(jnp.float32)
    middle, low = split2(rest)
    return high, middle, low


def digits(words):
    out = []
    for j in range(PER_WORD):
        one = words if j == 0 else jnp.right_shift(words, 2 * j)
        one = one if j == PER_WORD - 1 else jnp.bitwise_and(one, 3)
        out.append(one.astype(jnp.float32).astype(jnp.bfloat16))
    return out


def natural_of_column(shape):
    column = lax.broadcasted_iota(jnp.int32, shape, len(shape) - 1)
    return PER_WORD * jnp.bitwise_and(column, LANES - 1) + jnp.right_shift(column, 7)


def to_digit_order():
    row = lax.broadcasted_iota(jnp.int32, (GROUP, GROUP), 0)
    column = natural_of_column((1, GROUP))
    return jnp.where(row == column, 1.0, 0.0).astype(jnp.bfloat16)


def to_natural_order():
    row = lax.broadcasted_iota(jnp.int32, (GROUP, GROUP), 0)
    natural = PER_WORD * jnp.bitwise_and(row, LANES - 1) + jnp.right_shift(row, 7)
    column = lax.broadcasted_iota(jnp.int32, (GROUP, GROUP), 1)
    return jnp.where(natural == column, 1.0, 0.0).astype(jnp.bfloat16)


def dot32(a, b):
    return jnp.dot(a, b, preferred_element_type=jnp.float32)


def group_of(slot, direct):
    return jnp.bitwise_xor(lax.axis_index("people"), slot) if direct else slot


def load_kernel(words_ref, half_ref, held, sems):
    parts = sems.shape[0]
    rows = held.shape[0] // parts
    copies = []
    for part in range(parts):
        at = pl.ds(part * rows, rows)
        copies.append(pltpu.make_async_copy(words_ref.at[at, :], held.at[at, :], sems.at[part]))
        copies[-1].start()
    for part, copy in enumerate(copies):
        copy.wait()
        at = slice(part * rows, (part + 1) * rows)
        half_ref[at, :] = held[at, :].astype(jnp.float32).astype(jnp.bfloat16)


def load_words(genotype):
    parts = 3
    return pl.pallas_call(
        load_kernel,
        out_shape=jax.ShapeDtypeStruct(genotype.shape, jnp.bfloat16),
        in_specs=[IN_HBM],
        out_specs=IN_VMEM,
        scratch_shapes=[pltpu.VMEM(genotype.shape, genotype.dtype), pltpu.SemaphoreType.DMA((parts,))],
        compiler_params=pltpu.CompilerParams(vmem_limit_bytes=VMEM_SKETCH),
        cost_estimate=pl.CostEstimate(flops=0, bytes_accessed=6 * genotype.size, transcendentals=0),
        name="load",
    )(genotype)


def sketch_kernel(half_ref, basis_ref, freq_ref, out_ref):
    k, markers = basis_ref.shape
    freq = freq_ref[...].reshape(1, markers)
    scaled = basis_ref[...].astype(jnp.float32) * lax.rsqrt(2.0 * freq * (1.0 - freq))
    offset = jnp.sum(scaled * (2.0 * freq), axis=1, keepdims=True)
    order = to_digit_order()
    stacked = jnp.concatenate(split2(scaled), axis=0)
    pieces = [[] for _ in range(PER_WORD)]
    for group in range(markers // GROUP):
        moved = dot32(stacked[:, group * GROUP:(group + 1) * GROUP], order).astype(jnp.bfloat16)
        for j in range(PER_WORD):
            pieces[j].append(moved[:, j * LANES:(j + 1) * LANES])
    arranged = jnp.concatenate([piece for one in pieces for piece in one], axis=1)
    words = half_ref[...].astype(jnp.float32).astype(jnp.int32)
    total = lax.dot_general(
        arranged, jnp.concatenate(digits(words), axis=1), (((1,), (1,)), ((), ())),
        preferred_element_type=jnp.float32,
    )
    out_ref[...] = total[:k] + total[k:] - offset


def sketch_partial(half, basis, freq):
    return pl.pallas_call(
        sketch_kernel,
        out_shape=jax.ShapeDtypeStruct((basis.shape[0], half.shape[0]), jnp.float32),
        in_specs=[IN_VMEM] * 3,
        out_specs=IN_VMEM,
        compiler_params=pltpu.CompilerParams(vmem_limit_bytes=VMEM_LIMIT),
        name="sketch",
    )(half, basis, freq)


def standard(rows, planes, freq):
    n_rows = rows.shape[0]
    row_sum = jnp.sum(rows, axis=1, keepdims=True)
    raw = dot32(jnp.concatenate(split2(rows), axis=0), planes)
    return (raw[:n_rows] + raw[n_rows:] - row_sum * (2.0 * freq)) * lax.rsqrt(2.0 * freq * (1.0 - freq))


def moved_freq(freq_ref, group, order):
    markers = freq_ref.shape[0]
    freq = jnp.broadcast_to(freq_ref[...].reshape(1, markers), (8, markers))
    return dot32(jnp.concatenate(split3(freq[:, group * GROUP:(group + 1) * GROUP]), axis=0), order)


def trait_kernel(direct, half_ref, freq_ref, residual_ref, weight_ref, chosen_ref, *refs):
    outs, (chosen_freq_ref, gathered_ref, total) = refs[:-3], refs[-3:]
    people, words = half_ref.shape
    markers, n_chosen = PER_WORD * words, gathered_ref.shape[1]
    chosen = chosen_ref[...].reshape(1, n_chosen) - lax.axis_index("markers") * markers
    digit = jnp.bitwise_and(chosen, PER_WORD - 1)
    row = lax.broadcasted_iota(jnp.int32, (words, 1), 0)
    pick = jnp.where(row == jnp.right_shift(chosen, 2), 1.0, 0.0).astype(jnp.bfloat16)
    word = dot32(half_ref[...], pick).astype(jnp.int32)
    word = jnp.bitwise_and(jnp.right_shift(word, 2 * digit), 3)
    gathered = word.astype(jnp.float32).astype(jnp.bfloat16)
    gathered_ref[...] = gathered
    order = to_digit_order()
    moved = [moved_freq(freq_ref, group, order) for group in range(markers // GROUP)]
    moved = jnp.concatenate([
        jnp.concatenate([one[:, j * LANES:(j + 1) * LANES] for one in moved], axis=1)
        for j in range(PER_WORD)
    ], axis=0)
    moved = dot32(moved.astype(jnp.bfloat16), pick)
    chosen_freq = jnp.zeros((8, n_chosen), jnp.float32)
    for j in range(PER_WORD):
        one = moved[24 * j:24 * (j + 1)]
        chosen_freq = jnp.where(digit == j, one[:8] + one[8:16] + one[16:], chosen_freq)
    chosen_freq_ref[...] = chosen_freq
    rows = residual_ref[...].astype(jnp.float32) * weight_ref[...].reshape(1, -1)
    total[...] = standard(rows, gathered, chosen_freq[0:1])
    k = outs[0].shape[0]
    r, width = rows.shape[0], n_chosen // len(outs)
    for slot, out in enumerate(outs):
        at = pl.multiple_of(group_of(slot, direct) * width, width)
        for i in range(r // k):
            out[:, i * width:(i + 1) * width] = total[i * k:(i + 1) * k, pl.ds(at, width)]


def trait_scores(half, freq, residuals, weight, chosen, k, direct):
    people, words = half.shape
    groups = words // LANES
    r, n_chosen = residuals.shape[0], chosen.shape[0]
    out = pl.pallas_call(
        functools.partial(trait_kernel, direct),
        out_shape=(jax.ShapeDtypeStruct((k, r // k * n_chosen // groups), jnp.float32),) * groups + (
            jax.ShapeDtypeStruct((8, n_chosen), jnp.float32),
            jax.ShapeDtypeStruct((people, n_chosen), jnp.bfloat16),
        ),
        in_specs=[IN_VMEM] * 5,
        out_specs=(IN_VMEM,) * (groups + 2),
        scratch_shapes=[pltpu.VMEM((r, n_chosen), jnp.float32)],
        compiler_params=pltpu.CompilerParams(vmem_limit_bytes=VMEM_LIMIT),
        cost_estimate=pl.CostEstimate(flops=2 * n_chosen * people * (words + 2 * r), bytes_accessed=2 * people * (words + n_chosen), transcendentals=0),
        name="traits",
    )(half, freq, residuals, weight, chosen)
    return out[:-2], out[-2:]


def decode_kernel(half_ref, freq_ref, planes_ref, order_ref):
    order = to_digit_order()
    for group in range(order_ref.shape[1] // GROUP):
        span = slice(group * GROUP, (group + 1) * GROUP)
        word = half_ref[:, group * LANES:(group + 1) * LANES].astype(jnp.float32).astype(jnp.int32)
        planes_ref[:, span] = jnp.concatenate(digits(word), axis=1)
        moved = moved_freq(freq_ref, group, order)
        order_ref[:, span] = moved[:8] + moved[8:16] + moved[16:]


def decode(half, freq):
    people, words = half.shape
    markers = words * PER_WORD
    return pl.pallas_call(
        decode_kernel,
        out_shape=(
            jax.ShapeDtypeStruct((people, markers), jnp.bfloat16),
            jax.ShapeDtypeStruct((8, markers), jnp.float32),
        ),
        in_specs=[IN_VMEM] * 2,
        out_specs=(IN_VMEM,) * 2,
        compiler_params=pltpu.CompilerParams(vmem_limit_bytes=VMEM_LIMIT),
        cost_estimate=pl.CostEstimate(flops=people * markers * 16, bytes_accessed=4 * people * markers, transcendentals=0),
        name="decode",
    )(half, freq)


def gram_of(sketch, residual):
    k = sketch.shape[0]
    parts = jnp.concatenate(split3(sketch), axis=0)
    raw = lax.dot_general(
        parts, jnp.concatenate([parts, residual], axis=0), (((1,), (1,)), ((), ())),
        preferred_element_type=jnp.float32,
    )
    block = [[raw[i * k:(i + 1) * k, j * k:(j + 1) * k] for j in range(3)] for i in range(3)]
    small = (block[0][2] + block[2][0]) + block[1][1]
    own = block[0][0] + ((block[0][1] + block[1][0]) + small)
    cross = raw[:k, 3 * k:] + (raw[k:2 * k, 3 * k:] + raw[2 * k:, 3 * k:])
    return jnp.concatenate([own, cross], axis=1)


def padded(width):
    return -(-width // LANES) * LANES


def chunk_of(slot, direct, rows, planes_ref, order_ref, chosen_freq_ref, gathered_ref):
    width = gathered_ref.shape[1] // (order_ref.shape[1] // GROUP)
    group = group_of(slot, direct)
    markers_at = pl.ds(pl.multiple_of(group * GROUP, GROUP), GROUP)
    scores_at = pl.ds(pl.multiple_of(group * width, width), width)
    planes = jnp.concatenate([planes_ref[:, markers_at], gathered_ref[:, scores_at]], axis=1)
    freq = jnp.concatenate([order_ref[0:1, markers_at], chosen_freq_ref[0:1, scores_at]], axis=1)
    return standard(rows, planes, freq)


def far_kernel(direct, first_ref, second_ref, residual_ref, weight_ref, *refs):
    common, trait_refs, refs = refs[:4], refs[4:6], refs[6:]
    relay_ref, straight_ref, kept_ref, across_ref, sketch_ref, gram_ref = refs
    weight = weight_ref[...].reshape(1, -1)
    sketch = (first_ref[...] + second_ref[...]) * weight
    sketch_ref[...] = sketch
    gram = gram_of(sketch, residual_ref[...])
    k, room = gram.shape[0], gram_ref.shape[1] - gram.shape[1]
    if room:
        gram = jnp.concatenate([gram, jnp.zeros((k, room), jnp.float32)], axis=1)
    gram_ref[...] = gram
    rows = sketch * weight
    for slot, low_ref, high_ref, trait_ref in (
        (FAR, relay_ref, straight_ref, trait_refs[0]), (ACROSS, kept_ref, across_ref, trait_refs[1])
    ):
        chunk = chunk_of(slot, direct, rows, *common)
        low_ref[:, :CUT] = chunk[:, :CUT]
        low_ref[:, CUT:CUT + gram.shape[1]] = gram
        low_ref[:, CUT + gram.shape[1]:] = trait_ref[...]
        high_ref[...] = chunk[:, CUT:]


def chunk_kernel(direct, slots, sketch_ref, weight_ref, gram_ref, *refs):
    n = len(slots)
    common, trait_refs, outs = refs[:4], refs[4:4 + n], refs[4 + n:]
    rows = sketch_ref[...] * weight_ref[...].reshape(1, -1)
    for slot, trait_ref, out in zip(slots, trait_refs, outs):
        chunk = chunk_of(slot, direct, rows, *common)
        at = chunk.shape[1] + gram_ref.shape[1]
        out[:, :chunk.shape[1]] = chunk
        out[:, chunk.shape[1]:at] = gram_ref[...]
        out[:, at:] = trait_ref[...]


def product_call(kernel, name, inputs, common, widths, people):
    k = inputs[0].shape[0]
    operands = (*inputs, *common)
    return pl.pallas_call(
        kernel,
        out_shape=tuple(jax.ShapeDtypeStruct((k, width), jnp.float32) for width in widths),
        in_specs=[IN_VMEM] * len(operands),
        out_specs=(IN_VMEM,) * len(widths),
        compiler_params=pltpu.CompilerParams(vmem_limit_bytes=VMEM_LIMIT),
        cost_estimate=pl.CostEstimate(flops=4 * k * people * sum(widths), bytes_accessed=2 * people * sum(widths), transcendentals=0),
        name=name,
    )(*operands)


def eliminate(system, k):
    row_at = lax.broadcasted_iota(jnp.int32, (k, 1), 0)
    shape = system.shape
    block = 8
    for start in range(0, k, block):
        columns = [
            jnp.broadcast_to(system[:, j:j + 1], shape) for j in range(start, start + block)
        ]
        for t in range(block):
            j = start + t
            inverse = lax.rsqrt(columns[t][j:j + 1, :])
            factor = columns[t] * inverse
            for s in range(t + 1, block):
                columns[s] = columns[s] - factor * factor[start + s:start + s + 1, :]
            scaled = system[j:j + 1, :] * inverse
            updated = system - factor * scaled
            system = jnp.where(row_at == j, scaled, jnp.where(row_at > j, updated, system))
    return system


def finish_kernel(root_people, r, width, digit_order, sketch_ref, own_ref, *refs):
    more, (components_ref, coefficients_ref, next_ref, out_ref) = refs[:-4], refs[-4:]
    k = sketch_ref.shape[0]
    score_width = out_ref.shape[1]
    gram_at = width + score_width
    trait_at = own_ref.shape[1] - r // k * score_width
    total = own_ref[...]
    if more:
        near_ref, relay_ref, relayed_ref, straight_ref, across_ref = more
        total = total + jnp.concatenate([near_ref[...], relay_ref[:, relayed_ref.shape[1]:]], axis=1)
        total = jnp.concatenate([
            total[:, :CUT] + relayed_ref[:, :CUT],
            total[:, CUT:gram_at] + (straight_ref[...] + across_ref[...]),
            total[:, gram_at:] + relayed_ref[:, CUT:],
        ], axis=1)
    row_at = lax.broadcasted_iota(jnp.int32, (k, k), 0)
    column_at = lax.broadcasted_iota(jnp.int32, (k, k), 1)
    identity = jnp.where(row_at == column_at, 1.0, 0.0)
    system = eliminate(jnp.concatenate([total[:, gram_at:gram_at + k + r], identity], axis=1), k)
    coefficients = system[:, k:k + r]
    inverse = system[:, k + r:]
    coefficients_ref[...] = coefficients
    components_ref[...] = root_people * jnp.dot(
        inverse, sketch_ref[...], precision=HIGHEST, preferred_element_type=jnp.float32
    )
    solved = jnp.dot(inverse, total[:, :gram_at], precision=HIGHEST, preferred_element_type=jnp.float32)
    basis = solved[:, :width]
    if digit_order:
        both = dot32(jnp.concatenate(split2(basis), axis=0), to_natural_order())
        basis = both[:k] + both[k:]
    next_ref[...] = basis
    removed = lax.dot_general(
        coefficients, solved[:, width:], (((0,), (0,)), ((), ())),
        precision=HIGHEST, preferred_element_type=jnp.float32,
    )
    for i in range(r // k):
        at = trait_at + i * score_width
        out_ref[i * k:(i + 1) * k, :] = (
            total[:, at:at + score_width] - removed[i * k:(i + 1) * k]
        ) * (1.0 / root_people)


def finish(root_people, r, width, score_width, digit_order, sketch, own, more):
    k = sketch.shape[0]
    return pl.pallas_call(
        functools.partial(finish_kernel, root_people, r, width, digit_order),
        out_shape=(
            jax.ShapeDtypeStruct(sketch.shape, jnp.float32),
            jax.ShapeDtypeStruct((k, r), jnp.float32),
            jax.ShapeDtypeStruct((k, width), jnp.float32),
            jax.ShapeDtypeStruct((r, score_width), jnp.float32),
        ),
        in_specs=[IN_VMEM] * (2 + len(more)),
        out_specs=(IN_VMEM,) * 4,
        compiler_params=pltpu.CompilerParams(vmem_limit_bytes=VMEM_LIMIT),
        name="finish",
    )(sketch, own, *more)


def shards(genotype, allele_freq, person_weight, basis, residuals, block_markers):
    people, words = genotype.shape
    markers = words * PER_WORD
    k, r = basis.shape[0], residuals.shape[0]
    marker_count = lax.axis_size("markers")
    people_count = lax.axis_size("people")
    groups = markers // GROUP
    direct = people_count == groups and groups == 4
    half = load_words(genotype)
    sketch = sketch_partial(half, basis, allele_freq)
    apart = 1
    while apart * 2 < marker_count:
        sketch = sketch + from_partner(sketch, "markers", apart)
        apart *= 2
    other = from_partner(sketch, "markers", apart)
    traits, (chosen_freq, gathered) = trait_scores(
        half, allele_freq, residuals, person_weight, block_markers, k, direct
    )
    planes, order = decode(half, allele_freq)
    common = planes, order, chosen_freq, gathered
    part_width = gathered.shape[1] // groups
    width = GROUP + part_width
    room = padded(k + r)
    low, high = CUT + room + traits[0].shape[1], width - CUT
    relay, straight, kept, across, sketch, gram = product_call(
        functools.partial(far_kernel, direct), "far", (sketch, other, residuals, person_weight),
        common + (traits[FAR], traits[ACROSS]), (low, high, low, high, people, room), people,
    )

    def chunks(name, *slots):
        return product_call(
            functools.partial(chunk_kernel, direct, slots), name, (sketch, person_weight, gram),
            common + tuple(traits[slot] for slot in slots),
            (width + room + traits[0].shape[1],) * len(slots), people,
        )
    if direct:
        relay = from_partner(jnp.concatenate([relay, traits[1]], axis=1), "people", 1)
        straight = from_partner(straight, "people", FAR)
        across = from_partner(across, "people", ACROSS)
        near, = chunks("near", 1)
        near = from_partner(near[:, :width + room], "people", 1)
        relayed = from_partner(kept + relay[:, :low], "people", ACROSS)
        own, = chunks("own", 0)
        more = near, relay, relayed, straight, across
    else:
        first, second = chunks("near", 0, 1)
        pieces = {
            0: first, 1: second,
            FAR: jnp.concatenate([relay[:, :CUT], straight, relay[:, CUT:]], axis=1),
            ACROSS: jnp.concatenate([kept[:, :CUT], across, kept[:, CUT:]], axis=1),
        }
        whole = jnp.stack([pieces[slot] for slot in range(groups)], axis=1)
        value = whole[:, :, :GROUP].reshape(k, groups, PER_WORD, LANES)
        value = value.swapaxes(2, 3).reshape(k, markers)
        ends = [GROUP] + [width + room + i * part_width for i in range(r // k)]
        scores = [whole[:, :, at:at + part_width].reshape(k, -1) for at in ends]
        value, scores, gram = lax.psum((value, scores, gram), "people")
        index = lax.axis_index("people")

        def own_part(array):
            part = array.shape[1] // people_count
            return lax.dynamic_slice_in_dim(array, index * part, part, 1)
        scores = [own_part(one) for one in scores]
        own = jnp.concatenate([own_part(value), scores[0], gram] + scores[1:], axis=1)
        more = ()
    components, coefficients, basis_own, score_own = finish(
        math.sqrt(people * people_count), r, markers // people_count, block_markers.shape[0] // people_count,
        direct, sketch, own, more
    )
    return components, coefficients, basis_own[None], score_own[None]


def solution(mesh):
    placed = (
        P(("cohort", "people"), "markers"),
        P(("cohort", "markers")),
        P(("cohort", "people")),
        P("cohort", "markers"),
        P("cohort", "people"),
        P("markers"),
    )
    return jax.shard_map(
        shards,
        mesh=mesh,
        in_specs=placed,
        out_specs=(
            P("cohort", "people"),
            P("cohort", None),
            P("markers", "cohort", "people"),
            P("markers", "cohort", "people"),
        ),
        check_vma=False,
    )
```

```python
import functools
import math

import jax
import jax.numpy as jnp
from jax import lax
from jax.experimental import pallas as pl
from jax.experimental.pallas import tpu as pltpu
from jax.sharding import PartitionSpec as P

LANES = 128
PER_WORD = 4
GROUP = LANES * PER_WORD
CUT = 128
FAR, ACROSS = 3, 2
VMEM_LIMIT = 40 * 1024 * 1024
VMEM_SKETCH = 51 * 1024 * 1024
HIGHEST = lax.Precision.HIGHEST
IN_VMEM = pl.BlockSpec(memory_space=pltpu.VMEM)
IN_HBM = pl.BlockSpec(memory_space=pltpu.HBM)


def from_partner(block, axis, apart):
    count = lax.axis_size(axis)
    route = [(low, low ^ apart) for low in range(count)]
    return lax.ppermute(block, axis, route)


def split2(value):
    high = value.astype(jnp.bfloat16)
    low = (value - high.astype(jnp.float32)).astype(jnp.bfloat16)
    return high, low


def split3(value):
    high, rest = value.astype(jnp.bfloat16), None
    rest = value - high.astype(jnp.float32)
    middle, low = split2(rest)
    return high, middle, low


def digits(words):
    out = []
    for j in range(PER_WORD):
        one = words if j == 0 else jnp.right_shift(words, 2 * j)
        one = one if j == PER_WORD - 1 else jnp.bitwise_and(one, 3)
        out.append(one.astype(jnp.float32).astype(jnp.bfloat16))
    return out


def natural_of_column(shape):
    column = lax.broadcasted_iota(jnp.int32, shape, len(shape) - 1)
    return PER_WORD * jnp.bitwise_and(column, LANES - 1) + jnp.right_shift(column, 7)


def to_digit_order():
    row = lax.broadcasted_iota(jnp.int32, (GROUP, GROUP), 0)
    column = natural_of_column((1, GROUP))
    return jnp.where(row == column, 1.0, 0.0).astype(jnp.bfloat16)


def to_natural_order():
    row = lax.broadcasted_iota(jnp.int32, (GROUP, GROUP), 0)
    natural = PER_WORD * jnp.bitwise_and(row, LANES - 1) + jnp.right_shift(row, 7)
    column = lax.broadcasted_iota(jnp.int32, (GROUP, GROUP), 1)
    return jnp.where(natural == column, 1.0, 0.0).astype(jnp.bfloat16)


def dot32(a, b):
    return jnp.dot(a, b, preferred_element_type=jnp.float32)


def group_of(slot, direct):
    return jnp.bitwise_xor(lax.axis_index("people"), slot) if direct else slot


def load_kernel(words_ref, half_ref, order_ref, back_ref, held, sems):
    parts = sems.shape[0]
    rows = held.shape[0] // parts
    copies = []
    for part in range(parts):
        at = pl.ds(part * rows, rows)
        copies.append(pltpu.make_async_copy(words_ref.at[at, :], held.at[at, :], sems.at[part]))
        copies[-1].start()
    order_ref[...] = to_digit_order()
    back_ref[...] = to_natural_order()
    for part, copy in enumerate(copies):
        copy.wait()
        at = slice(part * rows, (part + 1) * rows)
        half_ref[at, :] = held[at, :].astype(jnp.float32).astype(jnp.bfloat16)


def load_words(genotype):
    parts = 3
    return pl.pallas_call(
        load_kernel,
        out_shape=(
            jax.ShapeDtypeStruct(genotype.shape, jnp.bfloat16),
            jax.ShapeDtypeStruct((GROUP, GROUP), jnp.bfloat16),
            jax.ShapeDtypeStruct((GROUP, GROUP), jnp.bfloat16),
        ),
        in_specs=[IN_HBM],
        out_specs=(IN_VMEM,) * 3,
        scratch_shapes=[pltpu.VMEM(genotype.shape, genotype.dtype), pltpu.SemaphoreType.DMA((parts,))],
        compiler_params=pltpu.CompilerParams(vmem_limit_bytes=VMEM_SKETCH),
        cost_estimate=pl.CostEstimate(flops=0, bytes_accessed=6 * genotype.size, transcendentals=0),
        name="load",
    )(genotype)


def sketch_kernel(half_ref, to_digits_ref, basis_ref, freq_ref, out_ref):
    k, markers = basis_ref.shape
    freq = freq_ref[...].reshape(1, markers)
    scaled = basis_ref[...].astype(jnp.float32) * lax.rsqrt(2.0 * freq * (1.0 - freq))
    offset = jnp.sum(scaled * (2.0 * freq), axis=1, keepdims=True)
    order = to_digits_ref[...]
    stacked = jnp.concatenate(split2(scaled), axis=0)
    pieces = [[] for _ in range(PER_WORD)]
    for group in range(markers // GROUP):
        moved = dot32(stacked[:, group * GROUP:(group + 1) * GROUP], order).astype(jnp.bfloat16)
        for j in range(PER_WORD):
            pieces[j].append(moved[:, j * LANES:(j + 1) * LANES])
    arranged = jnp.concatenate([piece for one in pieces for piece in one], axis=1)
    words = half_ref[...].astype(jnp.float32).astype(jnp.int32)
    total = lax.dot_general(
        arranged, jnp.concatenate(digits(words), axis=1), (((1,), (1,)), ((), ())),
        preferred_element_type=jnp.float32,
    )
    out_ref[...] = total[:k] + total[k:] - offset


def sketch_partial(half, to_digits, basis, freq):
    return pl.pallas_call(
        sketch_kernel,
        out_shape=jax.ShapeDtypeStruct((basis.shape[0], half.shape[0]), jnp.float32),
        in_specs=[IN_VMEM] * 4,
        out_specs=IN_VMEM,
        compiler_params=pltpu.CompilerParams(vmem_limit_bytes=VMEM_LIMIT),
        name="sketch",
    )(half, to_digits, basis, freq)


def standard(rows, planes, freq):
    n_rows = rows.shape[0]
    row_sum = jnp.sum(rows, axis=1, keepdims=True)
    raw = dot32(jnp.concatenate(split2(rows), axis=0), planes)
    return (raw[:n_rows] + raw[n_rows:] - row_sum * (2.0 * freq)) * lax.rsqrt(2.0 * freq * (1.0 - freq))


def moved_freq(freq_ref, group, order):
    markers = freq_ref.shape[0]
    freq = jnp.broadcast_to(freq_ref[...].reshape(1, markers), (8, markers))
    return dot32(jnp.concatenate(split3(freq[:, group * GROUP:(group + 1) * GROUP]), axis=0), order)


def trait_kernel(direct, half_ref, to_digits_ref, freq_ref, residual_ref, weight_ref, chosen_ref, *refs):
    outs, (chosen_freq_ref, gathered_ref, total) = refs[:-3], refs[-3:]
    people, words = half_ref.shape
    markers, n_chosen = PER_WORD * words, gathered_ref.shape[1]
    chosen = chosen_ref[...].reshape(1, n_chosen) - lax.axis_index("markers") * markers
    digit = jnp.bitwise_and(chosen, PER_WORD - 1)
    row = lax.broadcasted_iota(jnp.int32, (words, 1), 0)
    pick = jnp.where(row == jnp.right_shift(chosen, 2), 1.0, 0.0).astype(jnp.bfloat16)
    word = dot32(half_ref[...], pick).astype(jnp.int32)
    word = jnp.bitwise_and(jnp.right_shift(word, 2 * digit), 3)
    gathered = word.astype(jnp.float32).astype(jnp.bfloat16)
    gathered_ref[...] = gathered
    order = to_digits_ref[...]
    moved = [moved_freq(freq_ref, group, order) for group in range(markers // GROUP)]
    moved = jnp.concatenate([
        jnp.concatenate([one[:, j * LANES:(j + 1) * LANES] for one in moved], axis=1)
        for j in range(PER_WORD)
    ], axis=0)
    moved = dot32(moved.astype(jnp.bfloat16), pick)
    chosen_freq = jnp.zeros((8, n_chosen), jnp.float32)
    for j in range(PER_WORD):
        one = moved[24 * j:24 * (j + 1)]
        chosen_freq = jnp.where(digit == j, one[:8] + one[8:16] + one[16:], chosen_freq)
    chosen_freq_ref[...] = chosen_freq
    rows = residual_ref[...].astype(jnp.float32) * weight_ref[...].reshape(1, -1)
    total[...] = standard(rows, gathered, chosen_freq[0:1])
    k = outs[0].shape[0]
    r, width = rows.shape[0], n_chosen // len(outs)
    for slot, out in enumerate(outs):
        at = pl.multiple_of(group_of(slot, direct) * width, width)
        for i in range(r // k):
            out[:, i * width:(i + 1) * width] = total[i * k:(i + 1) * k, pl.ds(at, width)]


def trait_scores(half, to_digits, freq, residuals, weight, chosen, k, direct):
    people, words = half.shape
    groups = words // LANES
    r, n_chosen = residuals.shape[0], chosen.shape[0]
    out = pl.pallas_call(
        functools.partial(trait_kernel, direct),
        out_shape=(jax.ShapeDtypeStruct((k, r // k * n_chosen // groups), jnp.float32),) * groups + (
            jax.ShapeDtypeStruct((8, n_chosen), jnp.float32),
            jax.ShapeDtypeStruct((people, n_chosen), jnp.bfloat16),
        ),
        in_specs=[IN_VMEM] * 6,
        out_specs=(IN_VMEM,) * (groups + 2),
        scratch_shapes=[pltpu.VMEM((r, n_chosen), jnp.float32)],
        compiler_params=pltpu.CompilerParams(vmem_limit_bytes=VMEM_LIMIT),
        cost_estimate=pl.CostEstimate(flops=2 * n_chosen * people * (words + 2 * r), bytes_accessed=2 * people * (words + n_chosen), transcendentals=0),
        name="traits",
    )(half, to_digits, freq, residuals, weight, chosen)
    return out[:-2], out[-2:]


def decode_kernel(half_ref, to_digits_ref, freq_ref, planes_ref, order_ref):
    order = to_digits_ref[...]
    for group in range(order_ref.shape[1] // GROUP):
        span = slice(group * GROUP, (group + 1) * GROUP)
        word = half_ref[:, group * LANES:(group + 1) * LANES].astype(jnp.float32).astype(jnp.int32)
        planes_ref[:, span] = jnp.concatenate(digits(word), axis=1)
        moved = moved_freq(freq_ref, group, order)
        order_ref[:, span] = moved[:8] + moved[8:16] + moved[16:]


def decode(half, to_digits, freq):
    people, words = half.shape
    markers = words * PER_WORD
    return pl.pallas_call(
        decode_kernel,
        out_shape=(
            jax.ShapeDtypeStruct((people, markers), jnp.bfloat16),
            jax.ShapeDtypeStruct((8, markers), jnp.float32),
        ),
        in_specs=[IN_VMEM] * 3,
        out_specs=(IN_VMEM,) * 2,
        compiler_params=pltpu.CompilerParams(vmem_limit_bytes=VMEM_LIMIT),
        cost_estimate=pl.CostEstimate(flops=people * markers * 16, bytes_accessed=4 * people * markers, transcendentals=0),
        name="decode",
    )(half, to_digits, freq)


def gram_of(sketch, residual):
    k = sketch.shape[0]
    parts = jnp.concatenate(split3(sketch), axis=0)
    raw = lax.dot_general(
        parts, jnp.concatenate([parts, residual], axis=0), (((1,), (1,)), ((), ())),
        preferred_element_type=jnp.float32,
    )
    block = [[raw[i * k:(i + 1) * k, j * k:(j + 1) * k] for j in range(3)] for i in range(3)]
    small = (block[0][2] + block[2][0]) + block[1][1]
    own = block[0][0] + ((block[0][1] + block[1][0]) + small)
    cross = raw[:k, 3 * k:] + (raw[k:2 * k, 3 * k:] + raw[2 * k:, 3 * k:])
    return jnp.concatenate([own, cross], axis=1)


def padded(width):
    return -(-width // LANES) * LANES


def chunk_of(slot, direct, rows, planes_ref, order_ref, chosen_freq_ref, gathered_ref):
    width = gathered_ref.shape[1] // (order_ref.shape[1] // GROUP)
    group = group_of(slot, direct)
    markers_at = pl.ds(pl.multiple_of(group * GROUP, GROUP), GROUP)
    scores_at = pl.ds(pl.multiple_of(group * width, width), width)
    planes = jnp.concatenate([planes_ref[:, markers_at], gathered_ref[:, scores_at]], axis=1)
    freq = jnp.concatenate([order_ref[0:1, markers_at], chosen_freq_ref[0:1, scores_at]], axis=1)
    return standard(rows, planes, freq)


def far_kernel(direct, first_ref, second_ref, residual_ref, weight_ref, *refs):
    common, trait_refs, refs = refs[:4], refs[4:6], refs[6:]
    relay_ref, straight_ref, kept_ref, across_ref, sketch_ref, gram_ref = refs
    weight = weight_ref[...].reshape(1, -1)
    sketch = (first_ref[...] + second_ref[...]) * weight
    sketch_ref[...] = sketch
    gram = gram_of(sketch, residual_ref[...])
    k, room = gram.shape[0], gram_ref.shape[1] - gram.shape[1]
    if room:
        gram = jnp.concatenate([gram, jnp.zeros((k, room), jnp.float32)], axis=1)
    gram_ref[...] = gram
    rows = sketch * weight
    for slot, low_ref, high_ref, trait_ref in (
        (FAR, relay_ref, straight_ref, trait_refs[0]), (ACROSS, kept_ref, across_ref, trait_refs[1])
    ):
        chunk = chunk_of(slot, direct, rows, *common)
        low_ref[:, :CUT] = chunk[:, :CUT]
        low_ref[:, CUT:CUT + gram.shape[1]] = gram
        low_ref[:, CUT + gram.shape[1]:] = trait_ref[...]
        high_ref[...] = chunk[:, CUT:]


def chunk_kernel(direct, slots, sketch_ref, weight_ref, gram_ref, *refs):
    n = len(slots)
    common, trait_refs, outs = refs[:4], refs[4:4 + n], refs[4 + n:]
    rows = sketch_ref[...] * weight_ref[...].reshape(1, -1)
    for slot, trait_ref, out in zip(slots, trait_refs, outs):
        chunk = chunk_of(slot, direct, rows, *common)
        at = chunk.shape[1] + gram_ref.shape[1]
        out[:, :chunk.shape[1]] = chunk
        out[:, chunk.shape[1]:at] = gram_ref[...]
        out[:, at:] = trait_ref[...]


def product_call(kernel, name, inputs, common, widths, people):
    k = inputs[0].shape[0]
    operands = (*inputs, *common)
    return pl.pallas_call(
        kernel,
        out_shape=tuple(jax.ShapeDtypeStruct((k, width), jnp.float32) for width in widths),
        in_specs=[IN_VMEM] * len(operands),
        out_specs=(IN_VMEM,) * len(widths),
        compiler_params=pltpu.CompilerParams(vmem_limit_bytes=VMEM_LIMIT),
        cost_estimate=pl.CostEstimate(flops=4 * k * people * sum(widths), bytes_accessed=2 * people * sum(widths), transcendentals=0),
        name=name,
    )(*operands)


def eliminate(system, k):
    row_at = lax.broadcasted_iota(jnp.int32, (k, 1), 0)
    shape = system.shape
    block = 8
    for start in range(0, k, block):
        columns = [
            jnp.broadcast_to(system[:, j:j + 1], shape) for j in range(start, start + block)
        ]
        for t in range(block):
            j = start + t
            inverse = lax.rsqrt(columns[t][j:j + 1, :])
            factor = columns[t] * inverse
            for s in range(t + 1, block):
                columns[s] = columns[s] - factor * factor[start + s:start + s + 1, :]
            scaled = system[j:j + 1, :] * inverse
            updated = system - factor * scaled
            system = jnp.where(row_at == j, scaled, jnp.where(row_at > j, updated, system))
    return system


def finish_kernel(root_people, r, width, digit_order, sketch_ref, to_natural_ref, own_ref, *refs):
    more, (components_ref, coefficients_ref, next_ref, out_ref) = refs[:-4], refs[-4:]
    k = sketch_ref.shape[0]
    score_width = out_ref.shape[1]
    gram_at = width + score_width
    trait_at = own_ref.shape[1] - r // k * score_width
    total = own_ref[...]
    if more:
        near_ref, relay_ref, relayed_ref, straight_ref, across_ref = more
        end = relayed_ref.shape[1]
        beside = [near_ref[...], relay_ref[:, CUT:CUT + trait_at - gram_at], relay_ref[:, end:]]
        total = total + jnp.concatenate(beside, axis=1)
        total = jnp.concatenate([
            total[:, :CUT] + relayed_ref[:, :CUT],
            total[:, CUT:gram_at] + (straight_ref[...] + across_ref[...]),
            total[:, gram_at:] + relayed_ref[:, CUT:],
        ], axis=1)
    row_at = lax.broadcasted_iota(jnp.int32, (k, k), 0)
    column_at = lax.broadcasted_iota(jnp.int32, (k, k), 1)
    identity = jnp.where(row_at == column_at, 1.0, 0.0)
    system = eliminate(jnp.concatenate([total[:, gram_at:gram_at + k + r], identity], axis=1), k)
    coefficients = system[:, k:k + r]
    inverse = system[:, k + r:]
    coefficients_ref[...] = coefficients
    components_ref[...] = root_people * jnp.dot(
        inverse, sketch_ref[...], precision=HIGHEST, preferred_element_type=jnp.float32
    )
    solved = jnp.dot(inverse, total[:, :gram_at], precision=HIGHEST, preferred_element_type=jnp.float32)
    basis = solved[:, :width]
    if digit_order:
        both = dot32(jnp.concatenate(split2(basis), axis=0), to_natural_ref[...])
        basis = both[:k] + both[k:]
    next_ref[...] = basis
    removed = lax.dot_general(
        coefficients, solved[:, width:], (((0,), (0,)), ((), ())),
        precision=HIGHEST, preferred_element_type=jnp.float32,
    )
    for i in range(r // k):
        at = trait_at + i * score_width
        out_ref[i * k:(i + 1) * k, :] = (
            total[:, at:at + score_width] - removed[i * k:(i + 1) * k]
        ) * (1.0 / root_people)


def finish(root_people, r, width, score_width, digit_order, sketch, to_natural, own, more):
    k = sketch.shape[0]
    return pl.pallas_call(
        functools.partial(finish_kernel, root_people, r, width, digit_order),
        out_shape=(
            jax.ShapeDtypeStruct(sketch.shape, jnp.float32),
            jax.ShapeDtypeStruct((k, r), jnp.float32),
            jax.ShapeDtypeStruct((k, width), jnp.float32),
            jax.ShapeDtypeStruct((r, score_width), jnp.float32),
        ),
        in_specs=[IN_VMEM] * (3 + len(more)),
        out_specs=(IN_VMEM,) * 4,
        compiler_params=pltpu.CompilerParams(vmem_limit_bytes=VMEM_LIMIT),
        name="finish",
    )(sketch, to_natural, own, *more)


def shards(genotype, allele_freq, person_weight, basis, residuals, block_markers):
    people, words = genotype.shape
    markers = words * PER_WORD
    k, r = basis.shape[0], residuals.shape[0]
    marker_count = lax.axis_size("markers")
    people_count = lax.axis_size("people")
    groups = markers // GROUP
    direct = people_count == groups and groups == 4
    half, to_digits, to_natural = load_words(genotype)
    sketch = sketch_partial(half, to_digits, basis, allele_freq)
    apart = 1
    while apart * 2 < marker_count:
        sketch = sketch + from_partner(sketch, "markers", apart)
        apart *= 2
    other = from_partner(sketch, "markers", apart)
    traits, (chosen_freq, gathered) = trait_scores(
        half, to_digits, allele_freq, residuals, person_weight, block_markers, k, direct
    )
    planes, order = decode(half, to_digits, allele_freq)
    common = planes, order, chosen_freq, gathered
    part_width = gathered.shape[1] // groups
    width = GROUP + part_width
    room = padded(k + r)
    low, high = CUT + room + traits[0].shape[1], width - CUT
    relay, straight, kept, across, sketch, gram = product_call(
        functools.partial(far_kernel, direct), "far", (sketch, other, residuals, person_weight),
        common + (traits[FAR], traits[ACROSS]), (low, high, low, high, people, room), people,
    )

    def chunks(name, *slots):
        return product_call(
            functools.partial(chunk_kernel, direct, slots), name, (sketch, person_weight, gram),
            common + tuple(traits[slot] for slot in slots),
            (width + room + traits[0].shape[1],) * len(slots), people,
        )
    if direct:
        relay = from_partner(jnp.concatenate([relay, traits[1]], axis=1), "people", 1)
        straight = from_partner(straight, "people", FAR)
        across = from_partner(across, "people", ACROSS)
        near, = chunks("near", 1)
        near = from_partner(near[:, :width], "people", 1)
        relayed = from_partner(kept + relay[:, :low], "people", ACROSS)
        own, = chunks("own", 0)
        more = near, relay, relayed, straight, across
    else:
        first, second = chunks("near", 0, 1)
        pieces = {
            0: first, 1: second,
            FAR: jnp.concatenate([relay[:, :CUT], straight, relay[:, CUT:]], axis=1),
            ACROSS: jnp.concatenate([kept[:, :CUT], across, kept[:, CUT:]], axis=1),
        }
        whole = jnp.stack([pieces[slot] for slot in range(groups)], axis=1)
        value = whole[:, :, :GROUP].reshape(k, groups, PER_WORD, LANES)
        value = value.swapaxes(2, 3).reshape(k, markers)
        ends = [GROUP] + [width + room + i * part_width for i in range(r // k)]
        scores = [whole[:, :, at:at + part_width].reshape(k, -1) for at in ends]
        value, scores, gram = lax.psum((value, scores, gram), "people")
        index = lax.axis_index("people")

        def own_part(array):
            part = array.shape[1] // people_count
            return lax.dynamic_slice_in_dim(array, index * part, part, 1)
        scores = [own_part(one) for one in scores]
        own = jnp.concatenate([own_part(value), scores[0], gram] + scores[1:], axis=1)
        more = ()
    components, coefficients, basis_own, score_own = finish(
        math.sqrt(people * people_count), r, markers // people_count, block_markers.shape[0] // people_count,
        direct, sketch, to_natural, own, more
    )
    return components, coefficients, basis_own[None], score_own[None]


def solution(mesh):
    placed = (
        P(("cohort", "people"), "markers"),
        P(("cohort", "markers")),
        P(("cohort", "people")),
        P("cohort", "markers"),
        P("cohort", "people"),
        P("markers"),
    )
    return jax.shard_map(
        shards,
        mesh=mesh,
        in_specs=placed,
        out_specs=(
            P("cohort", "people"),
            P("cohort", None),
            P("markers", "cohort", "people"),
            P("markers", "cohort", "people"),
        ),
        check_vma=False,
    )
```

```python
import functools
import math

import jax
import jax.numpy as jnp
from jax import lax
from jax.experimental import pallas as pl
from jax.experimental.pallas import tpu as pltpu
from jax.sharding import PartitionSpec as P

LANES = 128
PER_WORD = 4
GROUP = LANES * PER_WORD
CUT = 128
FAR, ACROSS = 3, 2
VMEM_LIMIT = 40 * 1024 * 1024
VMEM_SKETCH = 51 * 1024 * 1024
HIGHEST = lax.Precision.HIGHEST
IN_VMEM = pl.BlockSpec(memory_space=pltpu.VMEM)
IN_HBM = pl.BlockSpec(memory_space=pltpu.HBM)


def from_partner(block, axis, apart):
    count = lax.axis_size(axis)
    route = [(low, low ^ apart) for low in range(count)]
    return lax.ppermute(block, axis, route)


def split2(value):
    high = value.astype(jnp.bfloat16)
    low = (value - high.astype(jnp.float32)).astype(jnp.bfloat16)
    return high, low


def split3(value):
    high, rest = value.astype(jnp.bfloat16), None
    rest = value - high.astype(jnp.float32)
    middle, low = split2(rest)
    return high, middle, low


def digits(words):
    out = []
    for j in range(PER_WORD):
        one = words if j == 0 else jnp.right_shift(words, 2 * j)
        one = one if j == PER_WORD - 1 else jnp.bitwise_and(one, 3)
        out.append(one.astype(jnp.float32).astype(jnp.bfloat16))
    return out


def natural_of_column(shape):
    column = lax.broadcasted_iota(jnp.int32, shape, len(shape) - 1)
    return PER_WORD * jnp.bitwise_and(column, LANES - 1) + jnp.right_shift(column, 7)


def to_digit_order():
    row = lax.broadcasted_iota(jnp.int32, (GROUP, GROUP), 0)
    column = natural_of_column((1, GROUP))
    return jnp.where(row == column, 1.0, 0.0).astype(jnp.bfloat16)


def to_natural_order():
    row = lax.broadcasted_iota(jnp.int32, (GROUP, GROUP), 0)
    natural = PER_WORD * jnp.bitwise_and(row, LANES - 1) + jnp.right_shift(row, 7)
    column = lax.broadcasted_iota(jnp.int32, (GROUP, GROUP), 1)
    return jnp.where(natural == column, 1.0, 0.0).astype(jnp.bfloat16)


def dot32(a, b):
    return jnp.dot(a, b, preferred_element_type=jnp.float32)


def group_of(slot, direct):
    return jnp.bitwise_xor(lax.axis_index("people"), slot) if direct else slot


def load_kernel(words_ref, half_ref, order_ref, back_ref, held, sems):
    parts = sems.shape[0]
    rows = held.shape[0] // parts
    copies = []
    for part in range(parts):
        at = pl.ds(part * rows, rows)
        copies.append(pltpu.make_async_copy(words_ref.at[at, :], held.at[at, :], sems.at[part]))
        copies[-1].start()
    order_ref[...] = to_digit_order()
    back_ref[...] = to_natural_order()
    for part, copy in enumerate(copies):
        copy.wait()
        at = slice(part * rows, (part + 1) * rows)
        half_ref[at, :] = held[at, :].astype(jnp.float32).astype(jnp.bfloat16)


def load_words(genotype):
    parts = 3
    return pl.pallas_call(
        load_kernel,
        out_shape=(
            jax.ShapeDtypeStruct(genotype.shape, jnp.bfloat16),
            jax.ShapeDtypeStruct((GROUP, GROUP), jnp.bfloat16),
            jax.ShapeDtypeStruct((GROUP, GROUP), jnp.bfloat16),
        ),
        in_specs=[IN_HBM],
        out_specs=(IN_VMEM,) * 3,
        scratch_shapes=[pltpu.VMEM(genotype.shape, genotype.dtype), pltpu.SemaphoreType.DMA((parts,))],
        compiler_params=pltpu.CompilerParams(vmem_limit_bytes=VMEM_SKETCH),
        cost_estimate=pl.CostEstimate(flops=0, bytes_accessed=6 * genotype.size, transcendentals=0),
        name="load",
    )(genotype)


def sketch_of(arranged, offset, half):
    words = half.astype(jnp.float32).astype(jnp.int32)
    total = lax.dot_general(
        arranged, jnp.concatenate(digits(words), axis=1), (((1,), (1,)), ((), ())),
        preferred_element_type=jnp.float32,
    )
    k = total.shape[0] // 2
    return total[:k] + total[k:] - offset


def first_sketch_kernel(half_ref, to_digits_ref, basis_ref, freq_ref, out_ref, arranged_ref, offset_ref):
    k, markers = basis_ref.shape
    freq = freq_ref[...].reshape(1, markers)
    scaled = basis_ref[...].astype(jnp.float32) * lax.rsqrt(2.0 * freq * (1.0 - freq))
    offset = jnp.sum(scaled * (2.0 * freq), axis=1, keepdims=True)
    offset_ref[...] = jnp.broadcast_to(offset, offset_ref.shape)
    order = to_digits_ref[...]
    stacked = jnp.concatenate(split2(scaled), axis=0)
    pieces = [[] for _ in range(PER_WORD)]
    for group in range(markers // GROUP):
        moved = dot32(stacked[:, group * GROUP:(group + 1) * GROUP], order).astype(jnp.bfloat16)
        for j in range(PER_WORD):
            pieces[j].append(moved[:, j * LANES:(j + 1) * LANES])
    arranged = jnp.concatenate([piece for one in pieces for piece in one], axis=1)
    arranged_ref[...] = arranged
    out_ref[...] = sketch_of(arranged, offset, half_ref[:out_ref.shape[1], :])


def first_sketch(half, to_digits, basis, freq, cut):
    k, markers = basis.shape
    return pl.pallas_call(
        first_sketch_kernel,
        out_shape=(
            jax.ShapeDtypeStruct((k, cut), jnp.float32),
            jax.ShapeDtypeStruct((2 * k, markers), jnp.bfloat16),
            jax.ShapeDtypeStruct((k, LANES), jnp.float32),
        ),
        in_specs=[IN_VMEM] * 4,
        out_specs=(IN_VMEM,) * 3,
        compiler_params=pltpu.CompilerParams(vmem_limit_bytes=VMEM_LIMIT),
        name="sketch",
    )(half, to_digits, basis, freq)


def second_sketch_kernel(half_ref, arranged_ref, offset_ref, out_ref):
    low = half_ref.shape[0] - out_ref.shape[1]
    out_ref[...] = sketch_of(arranged_ref[...], offset_ref[:, 0:1], half_ref[low:, :])


def second_sketch(half, arranged, offset, cut):
    return pl.pallas_call(
        second_sketch_kernel,
        out_shape=jax.ShapeDtypeStruct((offset.shape[0], half.shape[0] - cut), jnp.float32),
        in_specs=[IN_VMEM] * 3,
        out_specs=IN_VMEM,
        compiler_params=pltpu.CompilerParams(vmem_limit_bytes=VMEM_LIMIT),
        name="more",
    )(half, arranged, offset)


def standard(rows, planes, freq):
    n_rows = rows.shape[0]
    row_sum = jnp.sum(rows, axis=1, keepdims=True)
    raw = dot32(jnp.concatenate(split2(rows), axis=0), planes)
    return (raw[:n_rows] + raw[n_rows:] - row_sum * (2.0 * freq)) * lax.rsqrt(2.0 * freq * (1.0 - freq))


def moved_freq(freq_ref, group, order):
    markers = freq_ref.shape[0]
    freq = jnp.broadcast_to(freq_ref[...].reshape(1, markers), (8, markers))
    return dot32(jnp.concatenate(split3(freq[:, group * GROUP:(group + 1) * GROUP]), axis=0), order)


def trait_kernel(direct, half_ref, to_digits_ref, freq_ref, residual_ref, weight_ref, chosen_ref, *refs):
    outs, (order_ref, chosen_freq_ref, gathered_ref, total) = refs[:-4], refs[-4:]
    people, words = half_ref.shape
    markers, n_chosen = PER_WORD * words, gathered_ref.shape[1]
    chosen = chosen_ref[...].reshape(1, n_chosen) - lax.axis_index("markers") * markers
    digit = jnp.bitwise_and(chosen, PER_WORD - 1)
    row = lax.broadcasted_iota(jnp.int32, (words, 1), 0)
    pick = jnp.where(row == jnp.right_shift(chosen, 2), 1.0, 0.0).astype(jnp.bfloat16)
    word = dot32(half_ref[...], pick).astype(jnp.int32)
    word = jnp.bitwise_and(jnp.right_shift(word, 2 * digit), 3)
    gathered = word.astype(jnp.float32).astype(jnp.bfloat16)
    gathered_ref[...] = gathered
    order = to_digits_ref[...]
    moved = [moved_freq(freq_ref, group, order) for group in range(markers // GROUP)]
    for group, one in enumerate(moved):
        order_ref[:, group * GROUP:(group + 1) * GROUP] = one[:8] + one[8:16] + one[16:]
    moved = jnp.concatenate([
        jnp.concatenate([one[:, j * LANES:(j + 1) * LANES] for one in moved], axis=1)
        for j in range(PER_WORD)
    ], axis=0)
    moved = dot32(moved.astype(jnp.bfloat16), pick)
    chosen_freq = jnp.zeros((8, n_chosen), jnp.float32)
    for j in range(PER_WORD):
        one = moved[24 * j:24 * (j + 1)]
        chosen_freq = jnp.where(digit == j, one[:8] + one[8:16] + one[16:], chosen_freq)
    chosen_freq_ref[...] = chosen_freq
    rows = residual_ref[...].astype(jnp.float32) * weight_ref[...].reshape(1, -1)
    total[...] = standard(rows, gathered, chosen_freq[0:1])
    k = outs[0].shape[0]
    r, width = rows.shape[0], n_chosen // len(outs)
    for slot, out in enumerate(outs):
        at = pl.multiple_of(group_of(slot, direct) * width, width)
        for i in range(r // k):
            out[:, i * width:(i + 1) * width] = total[i * k:(i + 1) * k, pl.ds(at, width)]


def trait_scores(half, to_digits, freq, residuals, weight, chosen, k, direct):
    people, words = half.shape
    groups = words // LANES
    r, n_chosen = residuals.shape[0], chosen.shape[0]
    out = pl.pallas_call(
        functools.partial(trait_kernel, direct),
        out_shape=(jax.ShapeDtypeStruct((k, r // k * n_chosen // groups), jnp.float32),) * groups + (
            jax.ShapeDtypeStruct((8, words * PER_WORD), jnp.float32),
            jax.ShapeDtypeStruct((8, n_chosen), jnp.float32),
            jax.ShapeDtypeStruct((people, n_chosen), jnp.bfloat16),
        ),
        in_specs=[IN_VMEM] * 6,
        out_specs=(IN_VMEM,) * (groups + 3),
        scratch_shapes=[pltpu.VMEM((r, n_chosen), jnp.float32)],
        compiler_params=pltpu.CompilerParams(vmem_limit_bytes=VMEM_LIMIT),
        cost_estimate=pl.CostEstimate(flops=2 * n_chosen * people * (words + 2 * r), bytes_accessed=2 * people * (words + n_chosen), transcendentals=0),
        name="traits",
    )(half, to_digits, freq, residuals, weight, chosen)
    return out[:-3], out[-3:]


def decode_kernel(half_ref, planes_ref):
    for group in range(planes_ref.shape[1] // GROUP):
        word = half_ref[:, group * LANES:(group + 1) * LANES].astype(jnp.float32).astype(jnp.int32)
        planes_ref[:, group * GROUP:(group + 1) * GROUP] = jnp.concatenate(digits(word), axis=1)


def decode(half):
    people, words = half.shape
    markers = words * PER_WORD
    return pl.pallas_call(
        decode_kernel,
        out_shape=jax.ShapeDtypeStruct((people, markers), jnp.bfloat16),
        in_specs=[IN_VMEM],
        out_specs=IN_VMEM,
        compiler_params=pltpu.CompilerParams(vmem_limit_bytes=VMEM_LIMIT),
        cost_estimate=pl.CostEstimate(flops=people * markers * 16, bytes_accessed=4 * people * markers, transcendentals=0),
        name="decode",
    )(half)


def gram_of(sketch, residual):
    k = sketch.shape[0]
    parts = jnp.concatenate(split3(sketch), axis=0)
    raw = lax.dot_general(
        parts, jnp.concatenate([parts, residual], axis=0), (((1,), (1,)), ((), ())),
        preferred_element_type=jnp.float32,
    )
    block = [[raw[i * k:(i + 1) * k, j * k:(j + 1) * k] for j in range(3)] for i in range(3)]
    small = (block[0][2] + block[2][0]) + block[1][1]
    own = block[0][0] + ((block[0][1] + block[1][0]) + small)
    cross = raw[:k, 3 * k:] + (raw[k:2 * k, 3 * k:] + raw[2 * k:, 3 * k:])
    return jnp.concatenate([own, cross], axis=1)


def padded(width):
    return -(-width // LANES) * LANES


def chunk_of(slot, direct, rows, planes_ref, order_ref, chosen_freq_ref, gathered_ref):
    width = gathered_ref.shape[1] // (order_ref.shape[1] // GROUP)
    group = group_of(slot, direct)
    markers_at = pl.ds(pl.multiple_of(group * GROUP, GROUP), GROUP)
    scores_at = pl.ds(pl.multiple_of(group * width, width), width)
    planes = jnp.concatenate([planes_ref[:, markers_at], gathered_ref[:, scores_at]], axis=1)
    freq = jnp.concatenate([order_ref[0:1, markers_at], chosen_freq_ref[0:1, scores_at]], axis=1)
    return standard(rows, planes, freq)


def far_kernel(direct, first_ref, first_other_ref, second_ref, second_other_ref, residual_ref, weight_ref, *refs):
    common, trait_refs, refs = refs[:4], refs[4:6], refs[6:]
    relay_ref, straight_ref, kept_ref, across_ref, sketch_ref, gram_ref = refs
    weight = weight_ref[...].reshape(1, -1)
    sketch = jnp.concatenate(
        [first_ref[...] + first_other_ref[...], second_ref[...] + second_other_ref[...]], axis=1
    ) * weight
    sketch_ref[...] = sketch
    gram = gram_of(sketch, residual_ref[...])
    k, room = gram.shape[0], gram_ref.shape[1] - gram.shape[1]
    if room:
        gram = jnp.concatenate([gram, jnp.zeros((k, room), jnp.float32)], axis=1)
    gram_ref[...] = gram
    rows = sketch * weight
    for slot, low_ref, high_ref, trait_ref in (
        (FAR, relay_ref, straight_ref, trait_refs[0]), (ACROSS, kept_ref, across_ref, trait_refs[1])
    ):
        chunk = chunk_of(slot, direct, rows, *common)
        low_ref[:, :CUT] = chunk[:, :CUT]
        low_ref[:, CUT:CUT + gram.shape[1]] = gram
        low_ref[:, CUT + gram.shape[1]:] = trait_ref[...]
        high_ref[...] = chunk[:, CUT:]


def chunk_kernel(direct, slots, sketch_ref, weight_ref, gram_ref, *refs):
    n = len(slots)
    common, trait_refs, outs = refs[:4], refs[4:4 + n], refs[4 + n:]
    rows = sketch_ref[...] * weight_ref[...].reshape(1, -1)
    for slot, trait_ref, out in zip(slots, trait_refs, outs):
        chunk = chunk_of(slot, direct, rows, *common)
        at = chunk.shape[1] + gram_ref.shape[1]
        out[:, :chunk.shape[1]] = chunk
        out[:, chunk.shape[1]:at] = gram_ref[...]
        out[:, at:] = trait_ref[...]


def product_call(kernel, name, inputs, common, widths, people):
    k = inputs[0].shape[0]
    operands = (*inputs, *common)
    return pl.pallas_call(
        kernel,
        out_shape=tuple(jax.ShapeDtypeStruct((k, width), jnp.float32) for width in widths),
        in_specs=[IN_VMEM] * len(operands),
        out_specs=(IN_VMEM,) * len(widths),
        compiler_params=pltpu.CompilerParams(vmem_limit_bytes=VMEM_LIMIT),
        cost_estimate=pl.CostEstimate(flops=4 * k * people * sum(widths), bytes_accessed=2 * people * sum(widths), transcendentals=0),
        name=name,
    )(*operands)


def eliminate(system, k):
    row_at = lax.broadcasted_iota(jnp.int32, (k, 1), 0)
    shape = system.shape
    block = 8
    for start in range(0, k, block):
        columns = [
            jnp.broadcast_to(system[:, j:j + 1], shape) for j in range(start, start + block)
        ]
        for t in range(block):
            j = start + t
            inverse = lax.rsqrt(columns[t][j:j + 1, :])
            factor = columns[t] * inverse
            for s in range(t + 1, block):
                columns[s] = columns[s] - factor * factor[start + s:start + s + 1, :]
            scaled = system[j:j + 1, :] * inverse
            updated = system - factor * scaled
            system = jnp.where(row_at == j, scaled, jnp.where(row_at > j, updated, system))
    return system


def finish_kernel(root_people, r, width, digit_order, sketch_ref, to_natural_ref, own_ref, *refs):
    more, (components_ref, coefficients_ref, next_ref, out_ref) = refs[:-4], refs[-4:]
    k = sketch_ref.shape[0]
    score_width = out_ref.shape[1]
    gram_at = width + score_width
    trait_at = own_ref.shape[1] - r // k * score_width
    total = own_ref[...]
    if more:
        near_ref, relay_ref, relayed_ref, straight_ref, across_ref = more
        end = relayed_ref.shape[1]
        beside = [near_ref[...], relay_ref[:, CUT:CUT + trait_at - gram_at], relay_ref[:, end:]]
        total = total + jnp.concatenate(beside, axis=1)
        total = jnp.concatenate([
            total[:, :CUT] + relayed_ref[:, :CUT],
            total[:, CUT:gram_at] + (straight_ref[...] + across_ref[...]),
            total[:, gram_at:] + relayed_ref[:, CUT:],
        ], axis=1)
    row_at = lax.broadcasted_iota(jnp.int32, (k, k), 0)
    column_at = lax.broadcasted_iota(jnp.int32, (k, k), 1)
    identity = jnp.where(row_at == column_at, 1.0, 0.0)
    system = eliminate(jnp.concatenate([total[:, gram_at:gram_at + k + r], identity], axis=1), k)
    coefficients = system[:, k:k + r]
    inverse = system[:, k + r:]
    coefficients_ref[...] = coefficients
    components_ref[...] = root_people * jnp.dot(
        inverse, sketch_ref[...], precision=HIGHEST, preferred_element_type=jnp.float32
    )
    solved = jnp.dot(inverse, total[:, :gram_at], precision=HIGHEST, preferred_element_type=jnp.float32)
    basis = solved[:, :width]
    if digit_order:
        both = dot32(jnp.concatenate(split2(basis), axis=0), to_natural_ref[...])
        basis = both[:k] + both[k:]
    next_ref[...] = basis
    removed = lax.dot_general(
        coefficients, solved[:, width:], (((0,), (0,)), ((), ())),
        precision=HIGHEST, preferred_element_type=jnp.float32,
    )
    for i in range(r // k):
        at = trait_at + i * score_width
        out_ref[i * k:(i + 1) * k, :] = (
            total[:, at:at + score_width] - removed[i * k:(i + 1) * k]
        ) * (1.0 / root_people)


def finish(root_people, r, width, score_width, digit_order, sketch, to_natural, own, more):
    k = sketch.shape[0]
    return pl.pallas_call(
        functools.partial(finish_kernel, root_people, r, width, digit_order),
        out_shape=(
            jax.ShapeDtypeStruct(sketch.shape, jnp.float32),
            jax.ShapeDtypeStruct((k, r), jnp.float32),
            jax.ShapeDtypeStruct((k, width), jnp.float32),
            jax.ShapeDtypeStruct((r, score_width), jnp.float32),
        ),
        in_specs=[IN_VMEM] * (3 + len(more)),
        out_specs=(IN_VMEM,) * 4,
        compiler_params=pltpu.CompilerParams(vmem_limit_bytes=VMEM_LIMIT),
        name="finish",
    )(sketch, to_natural, own, *more)


def shards(genotype, allele_freq, person_weight, basis, residuals, block_markers):
    people, words = genotype.shape
    markers = words * PER_WORD
    k, r = basis.shape[0], residuals.shape[0]
    marker_count = lax.axis_size("markers")
    people_count = lax.axis_size("people")
    groups = markers // GROUP
    direct = people_count == groups and groups == 4
    half, to_digits, to_natural = load_words(genotype)
    cut = people // 2
    apart = marker_count // 2

    def chip_sum(part):
        step = 1
        while step < apart:
            part = part + from_partner(part, "markers", step)
            step *= 2
        return part
    first, arranged, offset = first_sketch(half, to_digits, basis, allele_freq, cut)
    second = second_sketch(half, arranged, offset, cut)
    first, second = lax.optimization_barrier((chip_sum(first), second))
    first_other = from_partner(first, "markers", apart)
    second = chip_sum(second)
    second_other = from_partner(second, "markers", apart)
    traits, (order, chosen_freq, gathered) = trait_scores(
        half, to_digits, allele_freq, residuals, person_weight, block_markers, k, direct
    )
    planes = decode(half)
    common = planes, order, chosen_freq, gathered
    part_width = gathered.shape[1] // groups
    width = GROUP + part_width
    room = padded(k + r)
    low, high = CUT + room + traits[0].shape[1], width - CUT
    relay, straight, kept, across, sketch, gram = product_call(
        functools.partial(far_kernel, direct), "far", (first, first_other, second, second_other, residuals, person_weight),
        common + (traits[FAR], traits[ACROSS]), (low, high, low, high, people, room), people,
    )

    def chunks(name, *slots):
        return product_call(
            functools.partial(chunk_kernel, direct, slots), name, (sketch, person_weight, gram),
            common + tuple(traits[slot] for slot in slots),
            (width + room + traits[0].shape[1],) * len(slots), people,
        )
    if direct:
        relay = from_partner(jnp.concatenate([relay, traits[1]], axis=1), "people", 1)
        straight = from_partner(straight, "people", FAR)
        across = from_partner(across, "people", ACROSS)
        near, = chunks("near", 1)
        near = from_partner(near[:, :width], "people", 1)
        relayed = from_partner(kept + relay[:, :low], "people", ACROSS)
        own, = chunks("own", 0)
        more = near, relay, relayed, straight, across
    else:
        first, second = chunks("near", 0, 1)
        pieces = {
            0: first, 1: second,
            FAR: jnp.concatenate([relay[:, :CUT], straight, relay[:, CUT:]], axis=1),
            ACROSS: jnp.concatenate([kept[:, :CUT], across, kept[:, CUT:]], axis=1),
        }
        whole = jnp.stack([pieces[slot] for slot in range(groups)], axis=1)
        value = whole[:, :, :GROUP].reshape(k, groups, PER_WORD, LANES)
        value = value.swapaxes(2, 3).reshape(k, markers)
        ends = [GROUP] + [width + room + i * part_width for i in range(r // k)]
        scores = [whole[:, :, at:at + part_width].reshape(k, -1) for at in ends]
        value, scores, gram = lax.psum((value, scores, gram), "people")
        index = lax.axis_index("people")

        def own_part(array):
            part = array.shape[1] // people_count
            return lax.dynamic_slice_in_dim(array, index * part, part, 1)
        scores = [own_part(one) for one in scores]
        own = jnp.concatenate([own_part(value), scores[0], gram] + scores[1:], axis=1)
        more = ()
    components, coefficients, basis_own, score_own = finish(
        math.sqrt(people * people_count), r, markers // people_count, block_markers.shape[0] // people_count,
        direct, sketch, to_natural, own, more
    )
    return components, coefficients, basis_own[None], score_own[None]


def solution(mesh):
    placed = (
        P(("cohort", "people"), "markers"),
        P(("cohort", "markers")),
        P(("cohort", "people")),
        P("cohort", "markers"),
        P("cohort", "people"),
        P("markers"),
    )
    return jax.shard_map(
        shards,
        mesh=mesh,
        in_specs=placed,
        out_specs=(
            P("cohort", "people"),
            P("cohort", None),
            P("markers", "cohort", "people"),
            P("markers", "cohort", "people"),
        ),
        check_vma=False,
    )
```

```python
import functools
import math

import jax
import jax.numpy as jnp
from jax import lax
from jax.experimental import pallas as pl
from jax.experimental.pallas import tpu as pltpu
from jax.sharding import PartitionSpec as P

LANES = 128
PER_WORD = 4
GROUP = LANES * PER_WORD
CUT = 128
FAR, ACROSS = 3, 2
VMEM_LIMIT = 40 * 1024 * 1024
VMEM_SKETCH = 51 * 1024 * 1024
HIGHEST = lax.Precision.HIGHEST
IN_VMEM = pl.BlockSpec(memory_space=pltpu.VMEM)
IN_HBM = pl.BlockSpec(memory_space=pltpu.HBM)


def from_partner(block, axis, apart):
    count = lax.axis_size(axis)
    route = [(low, low ^ apart) for low in range(count)]
    return lax.ppermute(block, axis, route)


def split2(value):
    high = value.astype(jnp.bfloat16)
    low = (value - high.astype(jnp.float32)).astype(jnp.bfloat16)
    return high, low


def split3(value):
    high, rest = value.astype(jnp.bfloat16), None
    rest = value - high.astype(jnp.float32)
    middle, low = split2(rest)
    return high, middle, low


def digits(words):
    out = []
    for j in range(PER_WORD):
        one = words if j == 0 else jnp.right_shift(words, 2 * j)
        one = one if j == PER_WORD - 1 else jnp.bitwise_and(one, 3)
        out.append(one.astype(jnp.float32).astype(jnp.bfloat16))
    return out


def natural_of_column(shape):
    column = lax.broadcasted_iota(jnp.int32, shape, len(shape) - 1)
    return PER_WORD * jnp.bitwise_and(column, LANES - 1) + jnp.right_shift(column, 7)


def to_digit_order():
    row = lax.broadcasted_iota(jnp.int32, (GROUP, GROUP), 0)
    column = natural_of_column((1, GROUP))
    return jnp.where(row == column, 1.0, 0.0).astype(jnp.bfloat16)


def to_natural_order():
    row = lax.broadcasted_iota(jnp.int32, (GROUP, GROUP), 0)
    natural = PER_WORD * jnp.bitwise_and(row, LANES - 1) + jnp.right_shift(row, 7)
    column = lax.broadcasted_iota(jnp.int32, (GROUP, GROUP), 1)
    return jnp.where(natural == column, 1.0, 0.0).astype(jnp.bfloat16)


def dot32(a, b):
    return jnp.dot(a, b, preferred_element_type=jnp.float32)


def group_of(slot, direct):
    return jnp.bitwise_xor(lax.axis_index("people"), slot) if direct else slot


def load_kernel(words_ref, half_ref, order_ref, back_ref, held, sems):
    parts = sems.shape[0]
    rows = held.shape[0] // parts
    copies = []
    for part in range(parts):
        at = pl.ds(part * rows, rows)
        copies.append(pltpu.make_async_copy(words_ref.at[at, :], held.at[at, :], sems.at[part]))
        copies[-1].start()
    order_ref[...] = to_digit_order()
    back_ref[...] = to_natural_order()
    for part, copy in enumerate(copies):
        copy.wait()
        at = slice(part * rows, (part + 1) * rows)
        half_ref[at, :] = held[at, :].astype(jnp.float32).astype(jnp.bfloat16)


def load_words(genotype):
    parts = 3
    return pl.pallas_call(
        load_kernel,
        out_shape=(
            jax.ShapeDtypeStruct(genotype.shape, jnp.bfloat16),
            jax.ShapeDtypeStruct((GROUP, GROUP), jnp.bfloat16),
            jax.ShapeDtypeStruct((GROUP, GROUP), jnp.bfloat16),
        ),
        in_specs=[IN_HBM],
        out_specs=(IN_VMEM,) * 3,
        scratch_shapes=[pltpu.VMEM(genotype.shape, genotype.dtype), pltpu.SemaphoreType.DMA((parts,))],
        compiler_params=pltpu.CompilerParams(vmem_limit_bytes=VMEM_SKETCH),
        cost_estimate=pl.CostEstimate(flops=0, bytes_accessed=6 * genotype.size, transcendentals=0),
        name="load",
    )(genotype)


def sketch_of(arranged, offset, half):
    words = half.astype(jnp.float32).astype(jnp.int32)
    total = lax.dot_general(
        arranged, jnp.concatenate(digits(words), axis=1), (((1,), (1,)), ((), ())),
        preferred_element_type=jnp.float32,
    )
    k = total.shape[0] // 2
    return total[:k] + total[k:] - offset


def first_sketch_kernel(half_ref, to_digits_ref, basis_ref, freq_ref, out_ref, arranged_ref, offset_ref):
    k, markers = basis_ref.shape
    freq = freq_ref[...].reshape(1, markers)
    scaled = basis_ref[...].astype(jnp.float32) * lax.rsqrt(2.0 * freq * (1.0 - freq))
    offset = jnp.sum(scaled * (2.0 * freq), axis=1, keepdims=True)
    offset_ref[...] = jnp.broadcast_to(offset, offset_ref.shape)
    order = to_digits_ref[...]
    stacked = jnp.concatenate(split2(scaled), axis=0)
    pieces = [[] for _ in range(PER_WORD)]
    for group in range(markers // GROUP):
        moved = dot32(stacked[:, group * GROUP:(group + 1) * GROUP], order).astype(jnp.bfloat16)
        for j in range(PER_WORD):
            pieces[j].append(moved[:, j * LANES:(j + 1) * LANES])
    arranged = jnp.concatenate([piece for one in pieces for piece in one], axis=1)
    arranged_ref[...] = arranged
    out_ref[...] = sketch_of(arranged, offset, half_ref[:out_ref.shape[1], :])


def first_sketch(half, to_digits, basis, freq, cut):
    k, markers = basis.shape
    return pl.pallas_call(
        first_sketch_kernel,
        out_shape=(
            jax.ShapeDtypeStruct((k, cut), jnp.float32),
            jax.ShapeDtypeStruct((2 * k, markers), jnp.bfloat16),
            jax.ShapeDtypeStruct((k, LANES), jnp.float32),
        ),
        in_specs=[IN_VMEM] * 4,
        out_specs=(IN_VMEM,) * 3,
        compiler_params=pltpu.CompilerParams(vmem_limit_bytes=VMEM_LIMIT),
        name="sketch",
    )(half, to_digits, basis, freq)


def second_sketch_kernel(half_ref, arranged_ref, offset_ref, out_ref):
    low = half_ref.shape[0] - out_ref.shape[1]
    out_ref[...] = sketch_of(arranged_ref[...], offset_ref[:, 0:1], half_ref[low:, :])


def second_sketch(half, arranged, offset, cut):
    return pl.pallas_call(
        second_sketch_kernel,
        out_shape=jax.ShapeDtypeStruct((offset.shape[0], half.shape[0] - cut), jnp.float32),
        in_specs=[IN_VMEM] * 3,
        out_specs=IN_VMEM,
        compiler_params=pltpu.CompilerParams(vmem_limit_bytes=VMEM_LIMIT),
        name="more",
    )(half, arranged, offset)


def standard(rows, planes, freq):
    n_rows = rows.shape[0]
    row_sum = jnp.sum(rows, axis=1, keepdims=True)
    raw = dot32(jnp.concatenate(split2(rows), axis=0), planes)
    return (raw[:n_rows] + raw[n_rows:] - row_sum * (2.0 * freq)) * lax.rsqrt(2.0 * freq * (1.0 - freq))


def moved_freq(freq_ref, group, order):
    markers = freq_ref.shape[0]
    freq = jnp.broadcast_to(freq_ref[...].reshape(1, markers), (8, markers))
    return dot32(jnp.concatenate(split3(freq[:, group * GROUP:(group + 1) * GROUP]), axis=0), order)


def trait_kernel(direct, half_ref, to_digits_ref, freq_ref, residual_ref, weight_ref, chosen_ref, *refs):
    outs, (order_ref, chosen_freq_ref, gathered_ref, total) = refs[:-4], refs[-4:]
    people, words = half_ref.shape
    markers, n_chosen = PER_WORD * words, gathered_ref.shape[1]
    chosen = chosen_ref[...].reshape(1, n_chosen) - lax.axis_index("markers") * markers
    digit = jnp.bitwise_and(chosen, PER_WORD - 1)
    row = lax.broadcasted_iota(jnp.int32, (words, 1), 0)
    pick = jnp.where(row == jnp.right_shift(chosen, 2), 1.0, 0.0).astype(jnp.bfloat16)
    word = dot32(half_ref[...], pick).astype(jnp.int32)
    word = jnp.bitwise_and(jnp.right_shift(word, 2 * digit), 3)
    gathered = word.astype(jnp.float32).astype(jnp.bfloat16)
    gathered_ref[...] = gathered
    order = to_digits_ref[...]
    moved = [moved_freq(freq_ref, group, order) for group in range(markers // GROUP)]
    for group, one in enumerate(moved):
        order_ref[:, group * GROUP:(group + 1) * GROUP] = one[:8] + one[8:16] + one[16:]
    moved = jnp.concatenate([
        jnp.concatenate([one[:, j * LANES:(j + 1) * LANES] for one in moved], axis=1)
        for j in range(PER_WORD)
    ], axis=0)
    moved = dot32(moved.astype(jnp.bfloat16), pick)
    chosen_freq = jnp.zeros((8, n_chosen), jnp.float32)
    for j in range(PER_WORD):
        one = moved[24 * j:24 * (j + 1)]
        chosen_freq = jnp.where(digit == j, one[:8] + one[8:16] + one[16:], chosen_freq)
    chosen_freq_ref[...] = chosen_freq
    rows = residual_ref[...].astype(jnp.float32) * weight_ref[...].reshape(1, -1)
    total[...] = standard(rows, gathered, chosen_freq[0:1])
    k = outs[0].shape[0]
    r, width = rows.shape[0], n_chosen // len(outs)
    for slot, out in enumerate(outs):
        at = pl.multiple_of(group_of(slot, direct) * width, width)
        for i in range(r // k):
            out[:, i * width:(i + 1) * width] = total[i * k:(i + 1) * k, pl.ds(at, width)]


def trait_scores(half, to_digits, freq, residuals, weight, chosen, k, direct):
    people, words = half.shape
    groups = words // LANES
    r, n_chosen = residuals.shape[0], chosen.shape[0]
    out = pl.pallas_call(
        functools.partial(trait_kernel, direct),
        out_shape=(jax.ShapeDtypeStruct((k, r // k * n_chosen // groups), jnp.float32),) * groups + (
            jax.ShapeDtypeStruct((8, words * PER_WORD), jnp.float32),
            jax.ShapeDtypeStruct((8, n_chosen), jnp.float32),
            jax.ShapeDtypeStruct((people, n_chosen), jnp.bfloat16),
        ),
        in_specs=[IN_VMEM] * 6,
        out_specs=(IN_VMEM,) * (groups + 3),
        scratch_shapes=[pltpu.VMEM((r, n_chosen), jnp.float32)],
        compiler_params=pltpu.CompilerParams(vmem_limit_bytes=VMEM_LIMIT),
        cost_estimate=pl.CostEstimate(flops=2 * n_chosen * people * (words + 2 * r), bytes_accessed=2 * people * (words + n_chosen), transcendentals=0),
        name="traits",
    )(half, to_digits, freq, residuals, weight, chosen)
    return out[:-3], out[-3:]


def decode_kernel(half_ref, planes_ref):
    for group in range(planes_ref.shape[1] // GROUP):
        word = half_ref[:, group * LANES:(group + 1) * LANES].astype(jnp.float32).astype(jnp.int32)
        planes_ref[:, group * GROUP:(group + 1) * GROUP] = jnp.concatenate(digits(word), axis=1)


def decode(half):
    people, words = half.shape
    markers = words * PER_WORD
    return pl.pallas_call(
        decode_kernel,
        out_shape=jax.ShapeDtypeStruct((people, markers), jnp.bfloat16),
        in_specs=[IN_VMEM],
        out_specs=IN_VMEM,
        compiler_params=pltpu.CompilerParams(vmem_limit_bytes=VMEM_LIMIT),
        cost_estimate=pl.CostEstimate(flops=people * markers * 16, bytes_accessed=4 * people * markers, transcendentals=0),
        name="decode",
    )(half)


def gram_of(sketch, residual):
    k = sketch.shape[0]
    parts = jnp.concatenate(split3(sketch), axis=0)
    raw = lax.dot_general(
        parts, jnp.concatenate([parts, residual], axis=0), (((1,), (1,)), ((), ())),
        preferred_element_type=jnp.float32,
    )
    block = [[raw[i * k:(i + 1) * k, j * k:(j + 1) * k] for j in range(3)] for i in range(3)]
    small = (block[0][2] + block[2][0]) + block[1][1]
    own = block[0][0] + ((block[0][1] + block[1][0]) + small)
    cross = raw[:k, 3 * k:] + (raw[k:2 * k, 3 * k:] + raw[2 * k:, 3 * k:])
    return jnp.concatenate([own, cross], axis=1)


def padded(width):
    return -(-width // LANES) * LANES


def chunk_of(slot, direct, rows, planes_ref, order_ref, chosen_freq_ref, gathered_ref):
    width = gathered_ref.shape[1] // (order_ref.shape[1] // GROUP)
    group = group_of(slot, direct)
    markers_at = pl.ds(pl.multiple_of(group * GROUP, GROUP), GROUP)
    scores_at = pl.ds(pl.multiple_of(group * width, width), width)
    planes = jnp.concatenate([planes_ref[:, markers_at], gathered_ref[:, scores_at]], axis=1)
    freq = jnp.concatenate([order_ref[0:1, markers_at], chosen_freq_ref[0:1, scores_at]], axis=1)
    return standard(rows, planes, freq)


def far_kernel(direct, first_ref, first_other_ref, second_ref, second_other_ref, residual_ref, weight_ref, *refs):
    common, trait_refs, refs = refs[:4], refs[4:6], refs[6:]
    relay_ref, straight_ref, kept_ref, across_ref, sketch_ref, gram_ref = refs
    weight = weight_ref[...].reshape(1, -1)
    sketch = jnp.concatenate(
        [first_ref[...] + first_other_ref[...], second_ref[...] + second_other_ref[...]], axis=1
    ) * weight
    sketch_ref[...] = sketch
    gram = gram_of(sketch, residual_ref[...])
    k, room = gram.shape[0], gram_ref.shape[1] - gram.shape[1]
    if room:
        gram = jnp.concatenate([gram, jnp.zeros((k, room), jnp.float32)], axis=1)
    gram_ref[...] = gram
    rows = sketch * weight
    for slot, low_ref, high_ref, trait_ref in (
        (FAR, relay_ref, straight_ref, trait_refs[0]), (ACROSS, kept_ref, across_ref, trait_refs[1])
    ):
        chunk = chunk_of(slot, direct, rows, *common)
        low_ref[:, :CUT] = chunk[:, :CUT]
        low_ref[:, CUT:CUT + gram.shape[1]] = gram
        low_ref[:, CUT + gram.shape[1]:] = trait_ref[...]
        high_ref[...] = chunk[:, CUT:]


def chunk_kernel(direct, slots, sketch_ref, weight_ref, gram_ref, *refs):
    n = len(slots)
    common, trait_refs, outs = refs[:4], refs[4:4 + n], refs[4 + n:]
    rows = sketch_ref[...] * weight_ref[...].reshape(1, -1)
    for slot, trait_ref, out in zip(slots, trait_refs, outs):
        chunk = chunk_of(slot, direct, rows, *common)
        at = chunk.shape[1] + gram_ref.shape[1]
        out[:, :chunk.shape[1]] = chunk
        out[:, chunk.shape[1]:at] = gram_ref[...]
        out[:, at:] = trait_ref[...]


def product_call(kernel, name, inputs, common, widths, people):
    k = inputs[0].shape[0]
    operands = (*inputs, *common)
    return pl.pallas_call(
        kernel,
        out_shape=tuple(jax.ShapeDtypeStruct((k, width), jnp.float32) for width in widths),
        in_specs=[IN_VMEM] * len(operands),
        out_specs=(IN_VMEM,) * len(widths),
        compiler_params=pltpu.CompilerParams(vmem_limit_bytes=VMEM_LIMIT),
        cost_estimate=pl.CostEstimate(flops=4 * k * people * sum(widths), bytes_accessed=2 * people * sum(widths), transcendentals=0),
        name=name,
    )(*operands)


def eliminate(system, k):
    row_at = lax.broadcasted_iota(jnp.int32, (k, 1), 0)
    shape = system.shape
    block = 16
    for start in range(0, k, block):
        columns = [
            jnp.broadcast_to(system[:, j:j + 1], shape) for j in range(start, start + block)
        ]
        for t in range(block):
            j = start + t
            inverse = lax.rsqrt(columns[t][j:j + 1, :])
            factor = columns[t] * inverse
            for s in range(t + 1, block):
                columns[s] = columns[s] - factor * factor[start + s:start + s + 1, :]
            scaled = system[j:j + 1, :] * inverse
            updated = system - factor * scaled
            system = jnp.where(row_at == j, scaled, jnp.where(row_at > j, updated, system))
    return system


def finish_kernel(root_people, r, width, digit_order, sketch_ref, to_natural_ref, own_ref, *refs):
    more, (components_ref, coefficients_ref, next_ref, out_ref) = refs[:-4], refs[-4:]
    k = sketch_ref.shape[0]
    score_width = out_ref.shape[1]
    gram_at = width + score_width
    trait_at = own_ref.shape[1] - r // k * score_width
    total = own_ref[...]
    if more:
        near_ref, relay_ref, relayed_ref, straight_ref, across_ref = more
        end = relayed_ref.shape[1]
        beside = [near_ref[...], relay_ref[:, CUT:CUT + trait_at - gram_at], relay_ref[:, end:]]
        total = total + jnp.concatenate(beside, axis=1)
        total = jnp.concatenate([
            total[:, :CUT] + relayed_ref[:, :CUT],
            total[:, CUT:gram_at] + (straight_ref[...] + across_ref[...]),
            total[:, gram_at:] + relayed_ref[:, CUT:],
        ], axis=1)
    row_at = lax.broadcasted_iota(jnp.int32, (k, k), 0)
    column_at = lax.broadcasted_iota(jnp.int32, (k, k), 1)
    identity = jnp.where(row_at == column_at, 1.0, 0.0)
    system = eliminate(jnp.concatenate([total[:, gram_at:gram_at + k + r], identity], axis=1), k)
    coefficients = system[:, k:k + r]
    inverse = system[:, k + r:]
    coefficients_ref[...] = coefficients
    components_ref[...] = root_people * jnp.dot(
        inverse, sketch_ref[...], precision=HIGHEST, preferred_element_type=jnp.float32
    )
    solved = jnp.dot(inverse, total[:, :gram_at], precision=HIGHEST, preferred_element_type=jnp.float32)
    basis = solved[:, :width]
    if digit_order:
        both = dot32(jnp.concatenate(split2(basis), axis=0), to_natural_ref[...])
        basis = both[:k] + both[k:]
    next_ref[...] = basis
    removed = lax.dot_general(
        coefficients, solved[:, width:], (((0,), (0,)), ((), ())),
        precision=HIGHEST, preferred_element_type=jnp.float32,
    )
    for i in range(r // k):
        at = trait_at + i * score_width
        out_ref[i * k:(i + 1) * k, :] = (
            total[:, at:at + score_width] - removed[i * k:(i + 1) * k]
        ) * (1.0 / root_people)


def finish(root_people, r, width, score_width, digit_order, sketch, to_natural, own, more):
    k = sketch.shape[0]
    return pl.pallas_call(
        functools.partial(finish_kernel, root_people, r, width, digit_order),
        out_shape=(
            jax.ShapeDtypeStruct(sketch.shape, jnp.float32),
            jax.ShapeDtypeStruct((k, r), jnp.float32),
            jax.ShapeDtypeStruct((k, width), jnp.float32),
            jax.ShapeDtypeStruct((r, score_width), jnp.float32),
        ),
        in_specs=[IN_VMEM] * (3 + len(more)),
        out_specs=(IN_VMEM,) * 4,
        compiler_params=pltpu.CompilerParams(vmem_limit_bytes=VMEM_LIMIT),
        name="finish",
    )(sketch, to_natural, own, *more)


def shards(genotype, allele_freq, person_weight, basis, residuals, block_markers):
    people, words = genotype.shape
    markers = words * PER_WORD
    k, r = basis.shape[0], residuals.shape[0]
    marker_count = lax.axis_size("markers")
    people_count = lax.axis_size("people")
    groups = markers // GROUP
    direct = people_count == groups and groups == 4
    half, to_digits, to_natural = load_words(genotype)
    cut = people // 2
    apart = marker_count // 2

    def chip_sum(part):
        step = 1
        while step < apart:
            part = part + from_partner(part, "markers", step)
            step *= 2
        return part
    first, arranged, offset = first_sketch(half, to_digits, basis, allele_freq, cut)
    second = second_sketch(half, arranged, offset, cut)
    first, second = lax.optimization_barrier((chip_sum(first), second))
    first_other = from_partner(first, "markers", apart)
    second = chip_sum(second)
    second_other = from_partner(second, "markers", apart)
    traits, (order, chosen_freq, gathered) = trait_scores(
        half, to_digits, allele_freq, residuals, person_weight, block_markers, k, direct
    )
    planes = decode(half)
    common = planes, order, chosen_freq, gathered
    part_width = gathered.shape[1] // groups
    width = GROUP + part_width
    room = padded(k + r)
    low, high = CUT + room + traits[0].shape[1], width - CUT
    relay, straight, kept, across, sketch, gram = product_call(
        functools.partial(far_kernel, direct), "far", (first, first_other, second, second_other, residuals, person_weight),
        common + (traits[FAR], traits[ACROSS]), (low, high, low, high, people, room), people,
    )

    def chunks(name, *slots):
        return product_call(
            functools.partial(chunk_kernel, direct, slots), name, (sketch, person_weight, gram),
            common + tuple(traits[slot] for slot in slots),
            (width + room + traits[0].shape[1],) * len(slots), people,
        )
    if direct:
        relay = from_partner(jnp.concatenate([relay, traits[1]], axis=1), "people", 1)
        straight = from_partner(straight, "people", FAR)
        across = from_partner(across, "people", ACROSS)
        near, = chunks("near", 1)
        near = from_partner(near[:, :width], "people", 1)
        relayed = from_partner(kept + relay[:, :low], "people", ACROSS)
        own, = chunks("own", 0)
        more = near, relay, relayed, straight, across
    else:
        first, second = chunks("near", 0, 1)
        pieces = {
            0: first, 1: second,
            FAR: jnp.concatenate([relay[:, :CUT], straight, relay[:, CUT:]], axis=1),
            ACROSS: jnp.concatenate([kept[:, :CUT], across, kept[:, CUT:]], axis=1),
        }
        whole = jnp.stack([pieces[slot] for slot in range(groups)], axis=1)
        value = whole[:, :, :GROUP].reshape(k, groups, PER_WORD, LANES)
        value = value.swapaxes(2, 3).reshape(k, markers)
        ends = [GROUP] + [width + room + i * part_width for i in range(r // k)]
        scores = [whole[:, :, at:at + part_width].reshape(k, -1) for at in ends]
        value, scores, gram = lax.psum((value, scores, gram), "people")
        index = lax.axis_index("people")

        def own_part(array):
            part = array.shape[1] // people_count
            return lax.dynamic_slice_in_dim(array, index * part, part, 1)
        scores = [own_part(one) for one in scores]
        own = jnp.concatenate([own_part(value), scores[0], gram] + scores[1:], axis=1)
        more = ()
    components, coefficients, basis_own, score_own = finish(
        math.sqrt(people * people_count), r, markers // people_count, block_markers.shape[0] // people_count,
        direct, sketch, to_natural, own, more
    )
    return components, coefficients, basis_own[None], score_own[None]


def solution(mesh):
    placed = (
        P(("cohort", "people"), "markers"),
        P(("cohort", "markers")),
        P(("cohort", "people")),
        P("cohort", "markers"),
        P("cohort", "people"),
        P("markers"),
    )
    return jax.shard_map(
        shards,
        mesh=mesh,
        in_specs=placed,
        out_specs=(
            P("cohort", "people"),
            P("cohort", None),
            P("markers", "cohort", "people"),
            P("markers", "cohort", "people"),
        ),
        check_vma=False,
    )
```

```python
import functools
import math

import jax
import jax.numpy as jnp
from jax import lax
from jax.experimental import pallas as pl
from jax.experimental.pallas import tpu as pltpu
from jax.sharding import PartitionSpec as P

LANES = 128
PER_WORD = 4
GROUP = LANES * PER_WORD
CUT = 128
FAR, ACROSS = 3, 2
VMEM_LIMIT = 40 * 1024 * 1024
VMEM_SKETCH = 51 * 1024 * 1024
HIGHEST = lax.Precision.HIGHEST
IN_VMEM = pl.BlockSpec(memory_space=pltpu.VMEM)
IN_HBM = pl.BlockSpec(memory_space=pltpu.HBM)


def from_partner(block, axis, apart):
    count = lax.axis_size(axis)
    route = [(low, low ^ apart) for low in range(count)]
    return lax.ppermute(block, axis, route)


def split2(value):
    high = value.astype(jnp.bfloat16)
    low = (value - high.astype(jnp.float32)).astype(jnp.bfloat16)
    return high, low


def split3(value):
    high, rest = value.astype(jnp.bfloat16), None
    rest = value - high.astype(jnp.float32)
    middle, low = split2(rest)
    return high, middle, low


def digits(words):
    out = []
    for j in range(PER_WORD):
        one = words if j == 0 else jnp.right_shift(words, 2 * j)
        one = one if j == PER_WORD - 1 else jnp.bitwise_and(one, 3)
        out.append(one.astype(jnp.float32).astype(jnp.bfloat16))
    return out


def natural_of_column(shape):
    column = lax.broadcasted_iota(jnp.int32, shape, len(shape) - 1)
    return PER_WORD * jnp.bitwise_and(column, LANES - 1) + jnp.right_shift(column, 7)


def to_digit_order():
    row = lax.broadcasted_iota(jnp.int32, (GROUP, GROUP), 0)
    column = natural_of_column((1, GROUP))
    return jnp.where(row == column, 1.0, 0.0).astype(jnp.bfloat16)


def to_natural_order():
    row = lax.broadcasted_iota(jnp.int32, (GROUP, GROUP), 0)
    natural = PER_WORD * jnp.bitwise_and(row, LANES - 1) + jnp.right_shift(row, 7)
    column = lax.broadcasted_iota(jnp.int32, (GROUP, GROUP), 1)
    return jnp.where(natural == column, 1.0, 0.0).astype(jnp.bfloat16)


def dot32(a, b):
    return jnp.dot(a, b, preferred_element_type=jnp.float32)


def group_of(slot, direct):
    return jnp.bitwise_xor(lax.axis_index("people"), slot) if direct else slot


def load_kernel(words_ref, half_ref, order_ref, back_ref, held, sems):
    parts = sems.shape[0]
    rows = held.shape[0] // parts
    copies = []
    for part in range(parts):
        at = pl.ds(part * rows, rows)
        copies.append(pltpu.make_async_copy(words_ref.at[at, :], held.at[at, :], sems.at[part]))
        copies[-1].start()
    order_ref[...] = to_digit_order()
    back_ref[...] = to_natural_order()
    for part, copy in enumerate(copies):
        copy.wait()
        at = slice(part * rows, (part + 1) * rows)
        half_ref[at, :] = held[at, :].astype(jnp.float32).astype(jnp.bfloat16)


def load_words(genotype):
    parts = 3
    return pl.pallas_call(
        load_kernel,
        out_shape=(
            jax.ShapeDtypeStruct(genotype.shape, jnp.bfloat16),
            jax.ShapeDtypeStruct((GROUP, GROUP), jnp.bfloat16),
            jax.ShapeDtypeStruct((GROUP, GROUP), jnp.bfloat16),
        ),
        in_specs=[IN_HBM],
        out_specs=(IN_VMEM,) * 3,
        scratch_shapes=[pltpu.VMEM(genotype.shape, genotype.dtype), pltpu.SemaphoreType.DMA((parts,))],
        compiler_params=pltpu.CompilerParams(vmem_limit_bytes=VMEM_SKETCH),
        cost_estimate=pl.CostEstimate(flops=0, bytes_accessed=6 * genotype.size, transcendentals=0),
        name="load",
    )(genotype)


def sketch_of(arranged, offset, half):
    words = half.astype(jnp.float32).astype(jnp.int32)
    total = lax.dot_general(
        arranged, jnp.concatenate(digits(words), axis=1), (((1,), (1,)), ((), ())),
        preferred_element_type=jnp.float32,
    )
    k = total.shape[0] // 2
    return total[:k] + total[k:] - offset


def first_sketch_kernel(half_ref, to_digits_ref, basis_ref, freq_ref, out_ref, arranged_ref, offset_ref):
    k, markers = basis_ref.shape
    freq = freq_ref[...].reshape(1, markers)
    scaled = basis_ref[...].astype(jnp.float32) * lax.rsqrt(2.0 * freq * (1.0 - freq))
    offset = jnp.sum(scaled * (2.0 * freq), axis=1, keepdims=True)
    offset_ref[...] = jnp.broadcast_to(offset, offset_ref.shape)
    order = to_digits_ref[...]
    stacked = jnp.concatenate(split2(scaled), axis=0)
    pieces = [[] for _ in range(PER_WORD)]
    groups = markers // GROUP
    tall = jnp.concatenate([stacked[:, group * GROUP:(group + 1) * GROUP] for group in range(groups)], axis=0)
    tall = dot32(tall, order).astype(jnp.bfloat16)
    for group in range(groups):
        moved = tall[2 * k * group:2 * k * (group + 1)]
        for j in range(PER_WORD):
            pieces[j].append(moved[:, j * LANES:(j + 1) * LANES])
    arranged = jnp.concatenate([piece for one in pieces for piece in one], axis=1)
    arranged_ref[...] = arranged
    out_ref[...] = sketch_of(arranged, offset, half_ref[:out_ref.shape[1], :])


def first_sketch(half, to_digits, basis, freq, cut):
    k, markers = basis.shape
    return pl.pallas_call(
        first_sketch_kernel,
        out_shape=(
            jax.ShapeDtypeStruct((k, cut), jnp.float32),
            jax.ShapeDtypeStruct((2 * k, markers), jnp.bfloat16),
            jax.ShapeDtypeStruct((k, LANES), jnp.float32),
        ),
        in_specs=[IN_VMEM] * 4,
        out_specs=(IN_VMEM,) * 3,
        compiler_params=pltpu.CompilerParams(vmem_limit_bytes=VMEM_LIMIT),
        name="sketch",
    )(half, to_digits, basis, freq)


def second_sketch_kernel(half_ref, arranged_ref, offset_ref, out_ref):
    low = half_ref.shape[0] - out_ref.shape[1]
    out_ref[...] = sketch_of(arranged_ref[...], offset_ref[:, 0:1], half_ref[low:, :])


def second_sketch(half, arranged, offset, cut):
    return pl.pallas_call(
        second_sketch_kernel,
        out_shape=jax.ShapeDtypeStruct((offset.shape[0], half.shape[0] - cut), jnp.float32),
        in_specs=[IN_VMEM] * 3,
        out_specs=IN_VMEM,
        compiler_params=pltpu.CompilerParams(vmem_limit_bytes=VMEM_LIMIT),
        name="more",
    )(half, arranged, offset)


def standard(rows, planes, freq):
    n_rows = rows.shape[0]
    row_sum = jnp.sum(rows, axis=1, keepdims=True)
    raw = dot32(jnp.concatenate(split2(rows), axis=0), planes)
    return (raw[:n_rows] + raw[n_rows:] - row_sum * (2.0 * freq)) * lax.rsqrt(2.0 * freq * (1.0 - freq))


def moved_freq(freq_ref, group, order):
    markers = freq_ref.shape[0]
    freq = jnp.broadcast_to(freq_ref[...].reshape(1, markers), (8, markers))
    return dot32(jnp.concatenate(split3(freq[:, group * GROUP:(group + 1) * GROUP]), axis=0), order)


def trait_kernel(direct, half_ref, to_digits_ref, freq_ref, residual_ref, weight_ref, chosen_ref, *refs):
    outs, (order_ref, chosen_freq_ref, gathered_ref, total) = refs[:-4], refs[-4:]
    people, words = half_ref.shape
    markers, n_chosen = PER_WORD * words, gathered_ref.shape[1]
    chosen = chosen_ref[...].reshape(1, n_chosen) - lax.axis_index("markers") * markers
    digit = jnp.bitwise_and(chosen, PER_WORD - 1)
    row = lax.broadcasted_iota(jnp.int32, (words, 1), 0)
    pick = jnp.where(row == jnp.right_shift(chosen, 2), 1.0, 0.0).astype(jnp.bfloat16)
    word = dot32(half_ref[...], pick).astype(jnp.int32)
    word = jnp.bitwise_and(jnp.right_shift(word, 2 * digit), 3)
    gathered = word.astype(jnp.float32).astype(jnp.bfloat16)
    gathered_ref[...] = gathered
    order = to_digits_ref[...]
    moved = [moved_freq(freq_ref, group, order) for group in range(markers // GROUP)]
    for group, one in enumerate(moved):
        order_ref[:, group * GROUP:(group + 1) * GROUP] = one[:8] + one[8:16] + one[16:]
    moved = jnp.concatenate([
        jnp.concatenate([one[:, j * LANES:(j + 1) * LANES] for one in moved], axis=1)
        for j in range(PER_WORD)
    ], axis=0)
    moved = dot32(moved.astype(jnp.bfloat16), pick)
    chosen_freq = jnp.zeros((8, n_chosen), jnp.float32)
    for j in range(PER_WORD):
        one = moved[24 * j:24 * (j + 1)]
        chosen_freq = jnp.where(digit == j, one[:8] + one[8:16] + one[16:], chosen_freq)
    chosen_freq_ref[...] = chosen_freq
    rows = residual_ref[...].astype(jnp.float32) * weight_ref[...].reshape(1, -1)
    total[...] = standard(rows, gathered, chosen_freq[0:1])
    k = outs[0].shape[0]
    r, width = rows.shape[0], n_chosen // len(outs)
    for slot, out in enumerate(outs):
        at = pl.multiple_of(group_of(slot, direct) * width, width)
        for i in range(r // k):
            out[:, i * width:(i + 1) * width] = total[i * k:(i + 1) * k, pl.ds(at, width)]


def trait_scores(half, to_digits, freq, residuals, weight, chosen, k, direct):
    people, words = half.shape
    groups = words // LANES
    r, n_chosen = residuals.shape[0], chosen.shape[0]
    out = pl.pallas_call(
        functools.partial(trait_kernel, direct),
        out_shape=(jax.ShapeDtypeStruct((k, r // k * n_chosen // groups), jnp.float32),) * groups + (
            jax.ShapeDtypeStruct((8, words * PER_WORD), jnp.float32),
            jax.ShapeDtypeStruct((8, n_chosen), jnp.float32),
            jax.ShapeDtypeStruct((people, n_chosen), jnp.bfloat16),
        ),
        in_specs=[IN_VMEM] * 6,
        out_specs=(IN_VMEM,) * (groups + 3),
        scratch_shapes=[pltpu.VMEM((r, n_chosen), jnp.float32)],
        compiler_params=pltpu.CompilerParams(vmem_limit_bytes=VMEM_LIMIT),
        cost_estimate=pl.CostEstimate(flops=2 * n_chosen * people * (words + 2 * r), bytes_accessed=2 * people * (words + n_chosen), transcendentals=0),
        name="traits",
    )(half, to_digits, freq, residuals, weight, chosen)
    return out[:-3], out[-3:]


def decode_kernel(half_ref, planes_ref):
    for group in range(planes_ref.shape[1] // GROUP):
        word = half_ref[:, group * LANES:(group + 1) * LANES].astype(jnp.float32).astype(jnp.int32)
        planes_ref[:, group * GROUP:(group + 1) * GROUP] = jnp.concatenate(digits(word), axis=1)


def decode(half):
    people, words = half.shape
    markers = words * PER_WORD
    return pl.pallas_call(
        decode_kernel,
        out_shape=jax.ShapeDtypeStruct((people, markers), jnp.bfloat16),
        in_specs=[IN_VMEM],
        out_specs=IN_VMEM,
        compiler_params=pltpu.CompilerParams(vmem_limit_bytes=VMEM_LIMIT),
        cost_estimate=pl.CostEstimate(flops=people * markers * 16, bytes_accessed=4 * people * markers, transcendentals=0),
        name="decode",
    )(half)


def gram_of(sketch, residual):
    k = sketch.shape[0]
    parts = jnp.concatenate(split3(sketch), axis=0)
    raw = lax.dot_general(
        parts, jnp.concatenate([parts, residual], axis=0), (((1,), (1,)), ((), ())),
        preferred_element_type=jnp.float32,
    )
    block = [[raw[i * k:(i + 1) * k, j * k:(j + 1) * k] for j in range(3)] for i in range(3)]
    small = (block[0][2] + block[2][0]) + block[1][1]
    own = block[0][0] + ((block[0][1] + block[1][0]) + small)
    cross = raw[:k, 3 * k:] + (raw[k:2 * k, 3 * k:] + raw[2 * k:, 3 * k:])
    return jnp.concatenate([own, cross], axis=1)


def padded(width):
    return -(-width // LANES) * LANES


def chunk_of(slot, direct, rows, planes_ref, order_ref, chosen_freq_ref, gathered_ref):
    width = gathered_ref.shape[1] // (order_ref.shape[1] // GROUP)
    group = group_of(slot, direct)
    markers_at = pl.ds(pl.multiple_of(group * GROUP, GROUP), GROUP)
    scores_at = pl.ds(pl.multiple_of(group * width, width), width)
    planes = jnp.concatenate([planes_ref[:, markers_at], gathered_ref[:, scores_at]], axis=1)
    freq = jnp.concatenate([order_ref[0:1, markers_at], chosen_freq_ref[0:1, scores_at]], axis=1)
    return standard(rows, planes, freq)


def far_kernel(direct, first_ref, first_other_ref, second_ref, second_other_ref, residual_ref, weight_ref, *refs):
    common, trait_refs, refs = refs[:4], refs[4:6], refs[6:]
    relay_ref, straight_ref, kept_ref, across_ref, sketch_ref, gram_ref = refs
    weight = weight_ref[...].reshape(1, -1)
    sketch = jnp.concatenate(
        [first_ref[...] + first_other_ref[...], second_ref[...] + second_other_ref[...]], axis=1
    ) * weight
    sketch_ref[...] = sketch
    gram = gram_of(sketch, residual_ref[...])
    k, room = gram.shape[0], gram_ref.shape[1] - gram.shape[1]
    if room:
        gram = jnp.concatenate([gram, jnp.zeros((k, room), jnp.float32)], axis=1)
    gram_ref[...] = gram
    rows = sketch * weight
    for slot, low_ref, high_ref, trait_ref in (
        (FAR, relay_ref, straight_ref, trait_refs[0]), (ACROSS, kept_ref, across_ref, trait_refs[1])
    ):
        chunk = chunk_of(slot, direct, rows, *common)
        low_ref[:, :CUT] = chunk[:, :CUT]
        low_ref[:, CUT:CUT + gram.shape[1]] = gram
        low_ref[:, CUT + gram.shape[1]:] = trait_ref[...]
        high_ref[...] = chunk[:, CUT:]


def chunk_kernel(direct, slots, sketch_ref, weight_ref, gram_ref, *refs):
    n = len(slots)
    common, trait_refs, outs = refs[:4], refs[4:4 + n], refs[4 + n:]
    rows = sketch_ref[...] * weight_ref[...].reshape(1, -1)
    for slot, trait_ref, out in zip(slots, trait_refs, outs):
        chunk = chunk_of(slot, direct, rows, *common)
        at = chunk.shape[1] + gram_ref.shape[1]
        out[:, :chunk.shape[1]] = chunk
        out[:, chunk.shape[1]:at] = gram_ref[...]
        out[:, at:] = trait_ref[...]


def product_call(kernel, name, inputs, common, widths, people):
    k = inputs[0].shape[0]
    operands = (*inputs, *common)
    return pl.pallas_call(
        kernel,
        out_shape=tuple(jax.ShapeDtypeStruct((k, width), jnp.float32) for width in widths),
        in_specs=[IN_VMEM] * len(operands),
        out_specs=(IN_VMEM,) * len(widths),
        compiler_params=pltpu.CompilerParams(vmem_limit_bytes=VMEM_LIMIT),
        cost_estimate=pl.CostEstimate(flops=4 * k * people * sum(widths), bytes_accessed=2 * people * sum(widths), transcendentals=0),
        name=name,
    )(*operands)


def eliminate(system, k):
    row_at = lax.broadcasted_iota(jnp.int32, (k, 1), 0)
    shape = system.shape
    block = 16
    for start in range(0, k, block):
        columns = [
            jnp.broadcast_to(system[:, j:j + 1], shape) for j in range(start, start + block)
        ]
        for t in range(block):
            j = start + t
            inverse = lax.rsqrt(columns[t][j:j + 1, :])
            factor = columns[t] * inverse
            for s in range(t + 1, block):
                columns[s] = columns[s] - factor * factor[start + s:start + s + 1, :]
            scaled = system[j:j + 1, :] * inverse
            updated = system - factor * scaled
            system = jnp.where(row_at == j, scaled, jnp.where(row_at > j, updated, system))
    return system


def finish_kernel(root_people, r, width, digit_order, sketch_ref, to_natural_ref, own_ref, *refs):
    more, (components_ref, coefficients_ref, next_ref, out_ref) = refs[:-4], refs[-4:]
    k = sketch_ref.shape[0]
    score_width = out_ref.shape[1]
    gram_at = width + score_width
    trait_at = own_ref.shape[1] - r // k * score_width
    total = own_ref[...]
    if more:
        near_ref, relay_ref, relayed_ref, straight_ref, across_ref = more
        end = relayed_ref.shape[1]
        beside = [near_ref[...], relay_ref[:, CUT:CUT + trait_at - gram_at], relay_ref[:, end:]]
        total = total + jnp.concatenate(beside, axis=1)
        total = jnp.concatenate([
            total[:, :CUT] + relayed_ref[:, :CUT],
            total[:, CUT:gram_at] + (straight_ref[...] + across_ref[...]),
            total[:, gram_at:] + relayed_ref[:, CUT:],
        ], axis=1)
    row_at = lax.broadcasted_iota(jnp.int32, (k, k), 0)
    column_at = lax.broadcasted_iota(jnp.int32, (k, k), 1)
    identity = jnp.where(row_at == column_at, 1.0, 0.0)
    system = eliminate(jnp.concatenate([total[:, gram_at:gram_at + k + r], identity], axis=1), k)
    coefficients = system[:, k:k + r]
    inverse = system[:, k + r:]
    coefficients_ref[...] = coefficients
    components_ref[...] = root_people * jnp.dot(
        inverse, sketch_ref[...], precision=HIGHEST, preferred_element_type=jnp.float32
    )
    solved = jnp.dot(inverse, total[:, :gram_at], precision=HIGHEST, preferred_element_type=jnp.float32)
    basis = solved[:, :width]
    if digit_order:
        both = dot32(jnp.concatenate(split2(basis), axis=0), to_natural_ref[...])
        basis = both[:k] + both[k:]
    next_ref[...] = basis
    removed = lax.dot_general(
        coefficients, solved[:, width:], (((0,), (0,)), ((), ())),
        precision=HIGHEST, preferred_element_type=jnp.float32,
    )
    for i in range(r // k):
        at = trait_at + i * score_width
        out_ref[i * k:(i + 1) * k, :] = (
            total[:, at:at + score_width] - removed[i * k:(i + 1) * k]
        ) * (1.0 / root_people)


def finish(root_people, r, width, score_width, digit_order, sketch, to_natural, own, more):
    k = sketch.shape[0]
    return pl.pallas_call(
        functools.partial(finish_kernel, root_people, r, width, digit_order),
        out_shape=(
            jax.ShapeDtypeStruct(sketch.shape, jnp.float32),
            jax.ShapeDtypeStruct((k, r), jnp.float32),
            jax.ShapeDtypeStruct((k, width), jnp.float32),
            jax.ShapeDtypeStruct((r, score_width), jnp.float32),
        ),
        in_specs=[IN_VMEM] * (3 + len(more)),
        out_specs=(IN_VMEM,) * 4,
        compiler_params=pltpu.CompilerParams(vmem_limit_bytes=VMEM_LIMIT),
        name="finish",
    )(sketch, to_natural, own, *more)


def shards(genotype, allele_freq, person_weight, basis, residuals, block_markers):
    people, words = genotype.shape
    markers = words * PER_WORD
    k, r = basis.shape[0], residuals.shape[0]
    marker_count = lax.axis_size("markers")
    people_count = lax.axis_size("people")
    groups = markers // GROUP
    direct = people_count == groups and groups == 4
    half, to_digits, to_natural = load_words(genotype)
    cut = people // 2
    apart = marker_count // 2

    def chip_sum(part):
        step = 1
        while step < apart:
            part = part + from_partner(part, "markers", step)
            step *= 2
        return part
    first, arranged, offset = first_sketch(half, to_digits, basis, allele_freq, cut)
    second = second_sketch(half, arranged, offset, cut)
    first, second = lax.optimization_barrier((chip_sum(first), second))
    first_other = from_partner(first, "markers", apart)
    second = chip_sum(second)
    second_other = from_partner(second, "markers", apart)
    traits, (order, chosen_freq, gathered) = trait_scores(
        half, to_digits, allele_freq, residuals, person_weight, block_markers, k, direct
    )
    planes = decode(half)
    common = planes, order, chosen_freq, gathered
    part_width = gathered.shape[1] // groups
    width = GROUP + part_width
    room = padded(k + r)
    low, high = CUT + room + traits[0].shape[1], width - CUT
    relay, straight, kept, across, sketch, gram = product_call(
        functools.partial(far_kernel, direct), "far", (first, first_other, second, second_other, residuals, person_weight),
        common + (traits[FAR], traits[ACROSS]), (low, high, low, high, people, room), people,
    )

    def chunks(name, *slots):
        return product_call(
            functools.partial(chunk_kernel, direct, slots), name, (sketch, person_weight, gram),
            common + tuple(traits[slot] for slot in slots),
            (width + room + traits[0].shape[1],) * len(slots), people,
        )
    if direct:
        relay = from_partner(jnp.concatenate([relay, traits[1]], axis=1), "people", 1)
        straight = from_partner(straight, "people", FAR)
        across = from_partner(across, "people", ACROSS)
        near, = chunks("near", 1)
        near = from_partner(near[:, :width], "people", 1)
        relayed = from_partner(kept + relay[:, :low], "people", ACROSS)
        own, = chunks("own", 0)
        more = near, relay, relayed, straight, across
    else:
        first, second = chunks("near", 0, 1)
        pieces = {
            0: first, 1: second,
            FAR: jnp.concatenate([relay[:, :CUT], straight, relay[:, CUT:]], axis=1),
            ACROSS: jnp.concatenate([kept[:, :CUT], across, kept[:, CUT:]], axis=1),
        }
        whole = jnp.stack([pieces[slot] for slot in range(groups)], axis=1)
        value = whole[:, :, :GROUP].reshape(k, groups, PER_WORD, LANES)
        value = value.swapaxes(2, 3).reshape(k, markers)
        ends = [GROUP] + [width + room + i * part_width for i in range(r // k)]
        scores = [whole[:, :, at:at + part_width].reshape(k, -1) for at in ends]
        value, scores, gram = lax.psum((value, scores, gram), "people")
        index = lax.axis_index("people")

        def own_part(array):
            part = array.shape[1] // people_count
            return lax.dynamic_slice_in_dim(array, index * part, part, 1)
        scores = [own_part(one) for one in scores]
        own = jnp.concatenate([own_part(value), scores[0], gram] + scores[1:], axis=1)
        more = ()
    components, coefficients, basis_own, score_own = finish(
        math.sqrt(people * people_count), r, markers // people_count, block_markers.shape[0] // people_count,
        direct, sketch, to_natural, own, more
    )
    return components, coefficients, basis_own[None], score_own[None]


def solution(mesh):
    placed = (
        P(("cohort", "people"), "markers"),
        P(("cohort", "markers")),
        P(("cohort", "people")),
        P("cohort", "markers"),
        P("cohort", "people"),
        P("markers"),
    )
    return jax.shard_map(
        shards,
        mesh=mesh,
        in_specs=placed,
        out_specs=(
            P("cohort", "people"),
            P("cohort", None),
            P("markers", "cohort", "people"),
            P("markers", "cohort", "people"),
        ),
        check_vma=False,
    )
```
